32 devices in a mesh: gx: 8 (over z, core), gy: 4 (over y, x).
Axes of the slice: x: 2, y: 2, z: 4, core: 2. Of those that a mesh axis runs over, the one named last changes fastest.
Arguments:
- forcing: float32 [9, 1024, 1024], P(None, 'gx', 'gy')
- start_potential: float32 [9, 1024, 1024], P(None, 'gx', 'gy'), may hold values from -3 to 3
- horiz_coef: float32 [1024, 1024], P('gx', 'gy'), may hold values from 0.5 to 2
- vert_coef: float32 [1024, 1024], P('gx', 'gy'), may hold values from 0.5 to 8
- vert_mix: float32 [9, 9], replicated, may hold values from -1.5 to 1.5
- mode_shapes: float32 [6, 1024, 1024], P(None, 'gx', 'gy'), may hold values from -6 to 6
- block_body: int32 [1024, 8], P('gx', 'gy'), may hold values from 0 to 127
- response: float32 [6, 6, 64], P(None, None, ('gx', 'gy')), may hold values from -2.5 to 2.5
- velocity_old: float32 [6, 64], P(None, ('gx', 'gy')), may hold values from -6 to 6
Outputs:
- potential: float32 [9, 1024, 1024], P(None, 'gx', 'gy')
- velocity: float32 [6, 64], P(None, ('gx', 'gy'))
- normal_flux: float32 [1024, 1024], P('gx', 'gy')
The draws below stay inside these ranges and needn't reach their ends.
Inputs may be any that keep to these rules, and one draw needn't show every extreme that they name: `block_body`: values of 64 or more mark blocks outside every footprint.
All inputs are finite; a program needn't handle non-finite values.
Results may differ from the reference program's by a relative error of at most 0.00023.
Values sent between devices are 32-bit elements; how exact they have to be, the bound alone decides.
No kernel may reach another device: no remote copies, remote signals or barrier semaphores. Data moves between devices by JAX's collectives and lax.ppermute only.
A program may use at most 64 MiB of HBM per device.

```python
import math
import jax
import jax.numpy as jnp
from jax import lax

LEVELS = 9
MODES = 6
BLOCK = 128
NX = 1024
NY = 1024
BODIES = 64
FOOT = 8192


def draw_forcing(key, part):
    key_base = jax.random.fold_in(key, 0)
    row_pos = jnp.arange(NX, dtype=jnp.float32) / NX
    col_pos = jnp.arange(NY, dtype=jnp.float32) / NY
    ramp = jnp.exp(math.log(3.0) * row_pos)[:, None] * jnp.exp(math.log(3.0) * col_pos)[None, :] / 3.0
    base = jax.random.normal(key_base, (LEVELS, NX, NY), jnp.float32)
    return base * ramp


def plant(entries, own_key, low, largest):
    dims = entries.shape
    spot = [jax.random.randint(jax.random.fold_in(own_key, axis), (), 0, dims[axis]) for axis in range(len(dims))]
    entries = entries.at[tuple(spot)].set(low)
    longest = dims.index(max(dims))
    spot[longest] = (spot[longest] + 1) % dims[longest]
    return entries.at[tuple(spot)].set(largest)


def level_of(rng, dims, cuts, low, high):
    level, own = 1.0, jax.random.fold_in(rng, 6)
    for position, shards_of in cuts:
        steps = jnp.exp(jax.random.uniform(jax.random.fold_in(own, position), (shards_of,), jnp.float32, low / len(cuts), high / len(cuts)))
        level = level * jnp.repeat(steps, dims[position] // shards_of).reshape([-1 if axis == position else 1 for axis in range(len(dims))])
    return level


def scatter_about(own_key, dims, deviation, limit, cuts=(), kind=jnp.bfloat16):
    values = deviation * jax.random.normal(own_key, dims, jnp.float32)
    if cuts:
        values = values * level_of(own_key, dims, cuts, -0.22, 0.18)
    return jnp.clip(values, -limit, limit).astype(kind)


def setup_inputs(seed: int = 0) -> dict:
    keys = jax.random.split(jax.random.key(seed), 10)
    return {
        "forcing": draw_forcing(jax.random.fold_in(keys[9], 71), 0),
        "start_potential": scatter_about(keys[1], (LEVELS, NX, NY), 0.5, 3.0, ((1, 8), (2, 4)), jnp.float32),
        "horiz_coef": jnp.clip(jnp.exp(math.log(2.0) - 1.3862944 * jax.random.uniform(keys[2], (NX, NY), jnp.float32) ** level_of(keys[2], (NX, NY), ((0, 8), (1, 4)), -0.2, 0.2)), 0.5, 2.0),
        "vert_coef": jnp.clip(jnp.exp(math.log(8.0) - 2.7725887 * jax.random.uniform(keys[3], (NX, NY), jnp.float32) ** level_of(keys[3], (NX, NY), ((0, 8), (1, 4)), -0.2, 0.2)), 0.5, 8.0),
        "vert_mix": scatter_about(keys[4], (LEVELS, LEVELS), 0.25, 1.5, (), jnp.float32),
        "mode_shapes": scatter_about(keys[5], (MODES, NX, NY), 1.0, 6.0, ((1, 8), (2, 4)), jnp.float32),
        "block_body": plant(jax.random.randint(keys[6], (NX, NY // BLOCK), 0, 2 * BODIES), jax.random.fold_in(keys[6], 1), 0, (2 * BODIES) - 1).astype(jnp.int32),
        "response": scatter_about(keys[7], (MODES, MODES, BODIES), MODES ** -0.5, 2.5, ((2, 32),), jnp.float32),
        "velocity_old": scatter_about(keys[8], (MODES, BODIES), 1.0, 6.0, ((1, 32),), jnp.float32),
    }


def horizontal(padded):
    central = padded[:, 2:-2, 2:-2]
    nearest = padded[:, 1:-3, 2:-2] + padded[:, 3:-1, 2:-2] + padded[:, 2:-2, 1:-3] + padded[:, 2:-2, 3:-1]
    farther = padded[:, :-4, 2:-2] + padded[:, 4:, 2:-2] + padded[:, 2:-2, :-4] + padded[:, 2:-2, 4:]
    return (60.0 * central - 16.0 * nearest + farther) / 12.0

def vertical(values_in):
    upper_level = jnp.concatenate([jnp.zeros_like(values_in[:1]), values_in[:-1]], axis=0)
    lower_level = jnp.concatenate([values_in[1:], values_in[-1:]], axis=0)
    return 2.0 * values_in - upper_level - lower_level

def apply_operator(padded, horiz_coef, vert_coef):
    interior = padded[:, 2:-2, 2:-2]
    return horiz_coef * horizontal(padded) + vert_coef * vertical(interior)

def precondition(residual, line_scale, vert_mix):
    weighted = residual * line_scale
    return weighted + jnp.einsum('lm,mxy->lxy', vert_mix, weighted, precision=lax.Precision.HIGHEST)

def reference(forcing, start_potential, horiz_coef, vert_coef, vert_mix, mode_shapes, block_body, response, velocity_old):
    line_scale = 1.0 / (5.0 * horiz_coef + 2.0 * vert_coef)

    def operate(values_in):
        padded = jnp.pad(values_in, ((0, 0), (2, 2), (2, 2)))
        return apply_operator(padded, horiz_coef, vert_coef)
    potential = start_potential
    residual = forcing - operate(start_potential)
    for repeat in range(2):
        direction = precondition(residual, line_scale, vert_mix)
        operated = operate(direction)
        step_size = jnp.sum(residual * operated) / jnp.sum(operated * operated)
        potential = potential + step_size * direction
        residual = residual - step_size * operated
    pressure = start_potential[0] - potential[0]
    mode_count = mode_shapes.shape[0]
    row_count, col_count = pressure.shape
    block_count = col_count // BLOCK
    block_sums = lax.optimization_barrier(jnp.sum((mode_shapes * pressure).reshape(mode_count, row_count, block_count, BLOCK), axis=3))
    flat_sums = block_sums.reshape(mode_count, row_count * block_count).T
    block_ids = block_body.reshape(-1).astype(jnp.int32)
    forces = jax.ops.segment_sum(flat_sums, block_ids, num_segments=2 * BODIES)[:BODIES].T * (1.0 / math.sqrt(FOOT))
    velocity = velocity_old + jnp.einsum('kmb,mb->kb', response, forces, precision=lax.Precision.HIGHEST)
    padded_vel = jnp.concatenate([velocity, jnp.zeros((mode_count, BODIES), jnp.float32)], axis=1)
    block_vel = jnp.take(padded_vel, block_ids, axis=1).reshape(mode_count, row_count, block_count)
    normal_flux = lax.optimization_barrier(jnp.sum(mode_shapes.reshape(mode_count, row_count, block_count, BLOCK) * block_vel[..., None], axis=0)).reshape(row_count, col_count)
    return (potential, velocity, normal_flux)
```

```python
import functools
import math

import jax
import jax.numpy as jnp
from jax import lax
from jax.experimental import pallas as pl
from jax.experimental.pallas import tpu as pltpu
from jax.sharding import PartitionSpec as P

FOOT = 8192
LANES = 128
SUB = 8
HALO = 6
F32 = jnp.float32
HBM = pl.BlockSpec(memory_space=pl.ANY)
VMEM = pl.BlockSpec(memory_space=pltpu.VMEM)
SMEM = pl.BlockSpec(memory_space=pltpu.SMEM)


def run_copies(copies):
    for copy in copies:
        copy.start()
    for copy in copies:
        copy.wait()


def pack_rows(phi, forcing, horiz, vert, near_out, far_out, sems):
    levels, rows, _ = phi.shape
    parity = lax.rem(lax.axis_index("gx"), 2)
    near_row = pl.multiple_of((1 - parity) * (rows - SUB), SUB)
    far_row = pl.multiple_of(parity * (rows - SUB), SUB)
    copies = []
    for out, row in ((near_out, near_row), (far_out, far_row)):
        pairs = (
            (phi.at[:, pl.ds(row, SUB), :], out.at[0:levels]),
            (forcing.at[:, pl.ds(row, SUB), :], out.at[levels : 2 * levels]),
            (horiz.at[pl.ds(row, SUB), :], out.at[2 * levels]),
            (vert.at[pl.ds(row, SUB), :], out.at[2 * levels + 1]),
        )
        for src, dst in pairs:
            copies.append(pltpu.make_async_copy(src, dst, sems.at[len(copies)]))
    run_copies(copies)


def pack_cols(phi, forcing, horiz, vert, near_in, far_in, near_out, far_out, strip, sems):
    levels, rows, cols = phi.shape
    planes = 2 * levels + 2
    row_par = lax.rem(lax.axis_index("gx"), 2)
    col_par = lax.rem(lax.axis_index("gy"), 2)
    near_row = pl.multiple_of((1 - row_par) * (rows + SUB), SUB)
    far_row = pl.multiple_of(row_par * (rows + SUB), SUB)
    copies = []
    for side, col in ((0, 0), (1, cols - LANES)):
        lanes = pl.ds(col, LANES)
        main = pl.ds(SUB, rows)
        pairs = (
            (phi.at[:, :, lanes], strip.at[side, 0:levels, main]),
            (forcing.at[:, :, lanes], strip.at[side, levels : 2 * levels, main]),
            (horiz.at[:, lanes], strip.at[side, 2 * levels, main]),
            (vert.at[:, lanes], strip.at[side, 2 * levels + 1, main]),
            (near_in.at[:, :, lanes], strip.at[side, :, pl.ds(near_row, SUB)]),
            (far_in.at[:, :, lanes], strip.at[side, :, pl.ds(far_row, SUB)]),
        )
        for src, dst in pairs:
            copies.append(pltpu.make_async_copy(src, dst, sems.at[len(copies)]))
    run_copies(copies)
    lane = lax.broadcasted_iota(jnp.int32, (SUB, LANES), 1)
    even = col_par == 0

    def body(i, carry):
        tile = pl.ds(pl.multiple_of(i * SUB, SUB), SUB)
        left = jnp.zeros((SUB, LANES), F32)
        right = jnp.zeros((SUB, LANES), F32)
        for p in range(planes):
            low = HALO * p
            here = (lane >= low) & (lane < low + HALO)
            left = jnp.where(here, pltpu.roll(strip[0, p, tile], low, 1), left)
            right = jnp.where(here, pltpu.roll(strip[1, p, tile], low + HALO, 1), right)
        near_out[tile] = jnp.where(even, right, left)
        far_out[tile] = jnp.where(even, left, right)
        return carry

    lax.fori_loop(0, (rows + 2 * SUB) // SUB, body, 0)


def stencil(ref, tile_row, wanted, tiles, levels, coefs, lane):
    center = [
        [ref[t, l, pl.ds(tile_row, SUB), :] for l in range(levels)] for t in range(tiles)
    ]
    result = []
    for t in wanted:
        after, before = center[(t + 1) % tiles], center[(t - 1) % tiles]
        mid_coef, last_coef, horiz12, vert = coefs[t]
        per_level = []
        for l in range(levels):
            x = center[t][l]

            def rows_at(offset):
                return ref[t, l, pl.ds(tile_row + offset, SUB), :]

            right1 = pltpu.roll(jnp.where(lane < 1, after[l], x), LANES - 1, 1)
            right2 = pltpu.roll(jnp.where(lane < 2, after[l], x), LANES - 2, 1)
            left1 = pltpu.roll(jnp.where(lane >= LANES - 1, before[l], x), 1, 1)
            left2 = pltpu.roll(jnp.where(lane >= LANES - 2, before[l], x), 2, 1)
            nearest = (rows_at(-1) + rows_at(1)) + (right1 + left1)
            farther = (rows_at(-2) + rows_at(2)) + (right2 + left2)
            if l == 0:
                beside = center[t][1]
            elif l == levels - 1:
                beside = center[t][l - 1]
            else:
                beside = center[t][l - 1] + center[t][l + 1]
            coef = last_coef if l == levels - 1 else mid_coef
            per_level.append(coef * x + horiz12 * (farther - 16.0 * nearest) - vert * beside)
        result.append(per_level)
    return result


def mix_levels(mix, weighted, levels):
    out = []
    for l in range(levels):
        total = (mix[l, l] + 1.0) * weighted[l]
        for m in range(levels):
            if m != l:
                total = total + mix[l, m] * weighted[m]
        out.append(total)
    return out


def body_hits(bodies_t, block, count, width):
    ids = bodies_t[block : block + 1, :]
    ids = jnp.where(ids < count, ids, -1)
    wanted = lax.broadcasted_iota(jnp.int32, (width, ids.shape[1]), 0)
    return (jnp.broadcast_to(ids, wanted.shape) == wanted).astype(F32)


def dot_nt(a, b):
    return lax.dot_general(
        a, b, (((1,), (1,)), ((), ())), precision=lax.Precision.HIGHEST, preferred_element_type=F32
    )


def main_kernel(
    body_total,
    phi,
    forcing,
    horiz,
    vert,
    row_near,
    row_far,
    col_near,
    col_far,
    mix,
    modes,
    bodies_t,
    response_t,
    old_t,
    dir_out,
    part_out,
    message,
    phi_s,
    res_s,
    horiz_s,
    vert_s,
    mid_s,
    last_s,
    scale_s,
    dir_s,
    img_s,
    part_s,
    mode_s,
    sums_s,
    small_s,
    sems,
    out_sems,
):
    levels, rows, cols = phi.shape
    mode_count = modes.shape[0]
    blocks = cols // LANES
    tiles = blocks + 1
    row_tiles = rows // SUB
    base = 2 * SUB
    gx, gy = lax.axis_index("gx"), lax.axis_index("gy")
    row_par, col_par = lax.rem(gx, 2), lax.rem(gy, 2)
    near_row = pl.multiple_of((1 - row_par) * (rows + SUB) + SUB, SUB)
    far_row = pl.multiple_of(row_par * (rows + SUB) + SUB, SUB)
    copies = []

    def start(src, dst):
        copy = pltpu.make_async_copy(src, dst, sems.at[len(copies)])
        copy.start()
        copies.append(copy)

    main = pl.ds(base, rows)
    for t in range(blocks):
        lanes = pl.ds(t * LANES, LANES)
        start(phi.at[:, :, lanes], phi_s.at[t, :, main])
        start(forcing.at[:, :, lanes], res_s.at[t, :, main])
        start(horiz.at[:, lanes], horiz_s.at[t, main])
        start(vert.at[:, lanes], vert_s.at[t, main])
        for got, row in ((row_near, near_row), (row_far, far_row)):
            here = pl.ds(row, SUB)
            start(got.at[0:levels, :, lanes], phi_s.at[t, :, here])
            start(got.at[levels : 2 * levels, :, lanes], res_s.at[t, :, here])
            start(got.at[2 * levels, :, lanes], horiz_s.at[t, here])
            start(got.at[2 * levels + 1, :, lanes], vert_s.at[t, here])
    needed = list(copies)
    for t in range(blocks):
        start(modes.at[:, :, pl.ds(t * LANES, LANES)], mode_s.at[t])
    mode_copies = copies[len(needed) :]

    lane = lax.broadcasted_iota(jnp.int32, (SUB, LANES), 1)
    sub = lax.broadcasted_iota(jnp.int32, (SUB, LANES), 0)
    side = tiles - 1
    even = col_par == 0
    planes = [phi_s.at[side, l] for l in range(levels)]
    planes += [res_s.at[side, l] for l in range(levels)]
    planes += [horiz_s.at[side], vert_s.at[side]]

    def unpack(i, carry):
        src = pl.ds(pl.multiple_of(i * SUB, SUB), SUB)
        dst = pl.ds(pl.multiple_of(i * SUB + SUB, SUB), SUB)
        near, far = col_near[src, :], col_far[src, :]
        right = jnp.where(even, near, far)
        left = jnp.where(even, far, near)
        for p, plane in enumerate(planes):
            low = HALO * p
            from_right = pltpu.roll(right, (LANES - low) % LANES, 1)
            from_left = pltpu.roll(left, (LANES - HALO - low) % LANES, 1)
            value = jnp.where(lane < HALO, from_right, 0.0)
            plane[dst, :] = jnp.where(lane >= LANES - HALO, from_left, value)
        return carry

    lax.fori_loop(0, row_tiles + 2, unpack, 0)
    for copy in needed:
        copy.wait()

    def coefficients(i, carry):
        here = pl.ds(pl.multiple_of(i * SUB + SUB, SUB), SUB)
        for t in range(tiles):
            h, v = horiz_s[t, here, :], vert_s[t, here, :]
            bottom = 5.0 * h + 2.0 * v
            inside = bottom > 0.0
            scale_s[t, here, :] = jnp.where(inside, 1.0 / jnp.where(inside, bottom, 1.0), 0.0)
            last = 5.0 * h + v
            mid_s[t, here, :] = last + v
            last_s[t, here, :] = last
            horiz_s[t, here, :] = h * (1.0 / 12.0)
        return carry

    lax.fori_loop(0, row_tiles + 2, coefficients, 0)

    def coefs_at(row, t):
        here = pl.ds(row, SUB)
        return (mid_s[t, here, :], last_s[t, here, :], horiz_s[t, here, :], vert_s[t, here, :])

    everything = range(tiles)

    def first(i, carry):
        row = pl.multiple_of(i * SUB + SUB, SUB)
        here = pl.ds(row, SUB)
        coefs = [coefs_at(row, t) for t in everything]
        image = stencil(phi_s, row, everything, tiles, levels, coefs, lane)
        for t in everything:
            scale = scale_s[t, here, :]
            weighted = []
            for l in range(levels):
                residual = res_s[t, l, here, :] - image[t][l]
                res_s[t, l, here, :] = residual
                weighted.append(residual * scale)
            for l, value in enumerate(mix_levels(mix, weighted, levels)):
                dir_s[t, l, here, :] = value
        return carry

    lax.fori_loop(0, row_tiles + 2, first, 0)
    outgoing = []

    def send(scratch, out, where):
        for t in range(blocks):
            copy = pltpu.make_async_copy(
                scratch.at[t, :, main], out.at[:, :, pl.ds(t * LANES, LANES)], where.at[t]
            )
            copy.start()
            outgoing.append(copy)

    send(dir_s, dir_out, out_sems.at[0])

    def second(i, carry):
        row = pl.multiple_of(i * SUB + SUB, SUB)
        here = pl.ds(row, SUB)
        coefs = [coefs_at(row, t) for t in everything]
        image = stencil(dir_s, row, everything, tiles, levels, coefs, lane)
        for t in everything:
            scale = scale_s[t, here, :]
            weighted = []
            for l in range(levels):
                img_s[t, l, here, :] = image[t][l]
                weighted.append(image[t][l] * scale)
            for l, value in enumerate(mix_levels(mix, weighted, levels)):
                part_s[t, l, here, :] = value
        return carry

    lax.fori_loop(0, row_tiles + 2, second, 0)
    send(part_s, part_out, out_sems.at[1])
    for copy in mode_copies:
        copy.wait()

    def third(i, totals):
        row = pl.multiple_of(i * SUB + base, SUB)
        here = pl.ds(row, SUB)
        own = pl.ds(pl.multiple_of(i * SUB, SUB), SUB)
        coefs = [coefs_at(row, t) for t in range(blocks)]
        image = stencil(part_s, row, range(blocks), tiles, levels, coefs, lane)
        totals = list(totals)
        for t in range(blocks):
            for l in range(levels):
                residual = res_s[t, l, here, :]
                img1 = img_s[t, l, here, :]
                img2 = image[t][l]
                products = (residual * img1, img1 * img1, residual * img2, img1 * img2, img2 * img2)
                totals = [total + product for total, product in zip(totals, products)]
        sums = jnp.zeros((SUB, LANES), F32)
        for t in range(blocks):
            for q, field in enumerate((dir_s, part_s)):
                surface = field[t, 0, here, :]
                for k in range(mode_count):
                    term = jnp.sum(mode_s[t, k, own, :] * surface, axis=1, keepdims=True)
                    sums = jnp.where(lane == (2 * t + q) * SUB + k, term, sums)
        sums_s[own, :] = sums
        return tuple(totals)

    zero = jnp.zeros((SUB, LANES), F32)
    totals = lax.fori_loop(0, row_tiles, third, (zero,) * 5)

    width = message.shape[1]
    sums_t = sums_s[...].T
    forces = jnp.zeros((SUB, width), F32)
    for t in range(blocks):
        hits = body_hits(bodies_t, t, body_total, width)
        first_sums = sums_t[2 * t * SUB : (2 * t + 1) * SUB, :]
        second_sums = sums_t[(2 * t + 1) * SUB : (2 * t + 2) * SUB, :]
        forces = forces + lax.dot_general(
            first_sums,
            hits,
            (((1,), (1,)), ((), ())),
            precision=lax.Precision.HIGHEST,
            preferred_element_type=F32,
        )
        forces = forces + pltpu.roll(dot_nt(second_sums, hits), body_total, 1)
    wide_sub = lax.broadcasted_iota(jnp.int32, (SUB, width), 0)
    wide_lane = lax.broadcasted_iota(jnp.int32, (SUB, width), 1)
    for q, total in enumerate(totals):
        forces = jnp.where((wide_sub == SUB - 2) & (wide_lane == q), jnp.sum(total), forces)
    message[0:SUB, :] = forces

    owned = old_t.shape[0]
    small_s[...] = jnp.zeros((LANES, LANES), F32)
    for k in range(mode_count):
        small_s[k * SUB : k * SUB + owned, 0:mode_count] = response_t[k]
        small_s[k * SUB : k * SUB + owned, mode_count : mode_count + 1] = old_t[:, k : k + 1]
    table = small_s[...].T[0:SUB, :]
    if width > LANES:
        table = jnp.concatenate([table, jnp.zeros((SUB, width - LANES), F32)], axis=1)
    me = (gx * lax.axis_size("gy") + gy) * owned
    for pair in range(mode_count // 2):
        tile = jnp.zeros((SUB, width), F32)
        for half in range(2):
            place = half * body_total + me
            shift = lax.rem(place - (2 * pair + half) * SUB + width, width)
            here = (wide_lane >= place) & (wide_lane < place + owned)
            tile = jnp.where(here, pltpu.roll(table, shift, 1), tile)
        message[(pair + 1) * SUB : (pair + 2) * SUB, :] = tile
    for copy in outgoing:
        copy.wait()


def last_kernel(
    body_total,
    message,
    phi,
    direction,
    part,
    modes,
    bodies_t,
    potential,
    velocity_t,
    flux,
    phi_s,
    dir_s,
    part_s,
    mode_s,
    flux_s,
    in_sems,
    mode_sem,
    out_sems,
):
    levels, rows, cols = phi.shape
    mode_count = modes.shape[0]
    blocks = cols // LANES
    width = message.shape[1]
    owned = velocity_t.shape[0]
    copies = []
    for l in range(levels):
        group = []
        for q, (src, dst) in enumerate(((phi, phi_s), (direction, dir_s), (part, part_s))):
            copy = pltpu.make_async_copy(src.at[l], dst.at[l], in_sems.at[l, q])
            copy.start()
            group.append(copy)
        copies.append(group)
    mode_copy = pltpu.make_async_copy(modes, mode_s, mode_sem.at[0])
    mode_copy.start()

    top = message[0:SUB, :]

    def scalar(q):
        return top[SUB - 2 : SUB - 1, q : q + 1]

    cross_first, square_first, cross_mixed, square_mixed, square_second = [
        scalar(q) for q in range(5)
    ]
    first_step = cross_first / square_first
    next_top = (
        cross_first
        - first_step * cross_mixed
        - first_step * square_first
        + first_step * first_step * square_mixed
    )
    next_bottom = (
        square_first - 2.0 * first_step * square_mixed + first_step * first_step * square_second
    )
    second_step = next_top / next_bottom
    on_dir = first_step + second_step
    on_part = first_step * second_step

    wide_sub = lax.broadcasted_iota(jnp.int32, (SUB, width), 0)
    wide_lane = lax.broadcasted_iota(jnp.int32, (SUB, width), 1)
    foot_scale = 1.0 / math.sqrt(FOOT)
    forces = foot_scale * (on_part * pltpu.roll(top, body_total, 1) - on_dir * top)
    forces = jnp.where(wide_sub == mode_count, 1.0, forces)
    forces = jnp.where(wide_lane < body_total, forces, 0.0)
    velocity = jnp.zeros((SUB, width), F32)
    for k in range(mode_count):
        table = message[(k // 2 + 1) * SUB : (k // 2 + 2) * SUB, :]
        if k % 2:
            table = pltpu.roll(table, body_total, 1)
        value = jnp.sum(table * forces, axis=0, keepdims=True)
        velocity = jnp.where(wide_sub == k, value, velocity)

    me = (lax.axis_index("gx") * lax.axis_size("gy") + lax.axis_index("gy")) * owned
    mine = ((wide_lane == me + wide_sub) & (wide_sub < owned)).astype(F32)
    velocity_t[...] = dot_nt(mine, velocity)[0:owned, 0:mode_count]

    per_row = []
    for t in range(blocks):
        hits = body_hits(bodies_t, t, body_total, width)
        per_row.append(
            lax.dot_general(
                velocity,
                hits,
                (((1,), (0,)), ((), ())),
                precision=lax.Precision.HIGHEST,
                preferred_element_type=F32,
            )
        )
    per_row.append(jnp.zeros((LANES - blocks * SUB, rows), F32))
    spread = jnp.concatenate(per_row, axis=0).T

    mode_copy.wait()
    for t in range(blocks):
        lanes = pl.ds(t * LANES, LANES)
        total = jnp.zeros((rows, LANES), F32)
        for k in range(mode_count):
            total = total + mode_s[k, :, lanes] * spread[:, t * SUB + k : t * SUB + k + 1]
        flux_s[:, lanes] = total
    flux_copy = pltpu.make_async_copy(flux_s, flux, out_sems.at[levels])
    flux_copy.start()
    outgoing = [flux_copy]
    for l in range(levels):
        for copy in copies[l]:
            copy.wait()
        phi_s[l] = phi_s[l] + (on_dir * dir_s[l] - on_part * part_s[l])
        copy = pltpu.make_async_copy(phi_s.at[l], potential.at[l], out_sems.at[l])
        copy.start()
        outgoing.append(copy)
    for copy in outgoing:
        copy.wait()


def swap_near(value, axis):
    size = lax.axis_size(axis)
    return lax.ppermute(value, axis, [(i, i ^ 1) for i in range(size)])


def swap_far(value, axis):
    size = lax.axis_size(axis)
    pairs = [(i, i + 1) for i in range(1, size - 1, 2)]
    return lax.ppermute(value, axis, pairs + [(j, i) for i, j in pairs])


def sum_over(value, axes):
    for axis in axes:
        size = lax.axis_size(axis)
        step = 1
        while step < size:
            value = value + lax.ppermute(value, axis, [(i, i ^ step) for i in range(size)])
            step *= 2
    return value


def per_device(
    forcing,
    start_potential,
    horiz_coef,
    vert_coef,
    vert_mix,
    mode_shapes,
    block_body,
    response,
    velocity_old,
):
    levels, rows, cols = forcing.shape
    mode_count = mode_shapes.shape[0]
    planes = 2 * levels + 2
    blocks = cols // LANES
    tiles = blocks + 1
    owned = velocity_old.shape[1]
    body_total = owned * lax.axis_size(("gx", "gy"))
    width = 2 * body_total
    bodies_t = block_body.T
    response_t = jnp.swapaxes(response, 1, 2)
    old_t = velocity_old.T
    limit = pltpu.CompilerParams(vmem_limit_bytes=40 * 2**20)

    row_message = jax.ShapeDtypeStruct((planes, SUB, cols), F32)
    near, far = pl.pallas_call(
        pack_rows,
        out_shape=(row_message, row_message),
        in_specs=[HBM] * 4,
        out_specs=(VMEM, VMEM),
        scratch_shapes=[pltpu.SemaphoreType.DMA((8,))],
        name="pack_rows",
    )(start_potential, forcing, horiz_coef, vert_coef)
    row_near, row_far = swap_near(near, "gx"), swap_far(far, "gx")

    col_message = jax.ShapeDtypeStruct((rows + 2 * SUB, LANES), F32)
    near, far = pl.pallas_call(
        pack_cols,
        out_shape=(col_message, col_message),
        in_specs=[HBM] * 6,
        out_specs=(VMEM, VMEM),
        scratch_shapes=[
            pltpu.VMEM((2, planes, rows + 2 * SUB, LANES), F32),
            pltpu.SemaphoreType.DMA((12,)),
        ],
        compiler_params=limit,
        name="pack_cols",
    )(start_potential, forcing, horiz_coef, vert_coef, row_near, row_far)
    col_near, col_far = swap_near(near, "gy"), swap_far(far, "gy")

    field = pltpu.VMEM((tiles, levels, rows + 4 * SUB, LANES), F32)
    plane = pltpu.VMEM((tiles, rows + 4 * SUB, LANES), F32)
    whole = jax.ShapeDtypeStruct((levels, rows, cols), F32)
    direction, part, message = pl.pallas_call(
        functools.partial(main_kernel, body_total),
        out_shape=(whole, whole, jax.ShapeDtypeStruct((4 * SUB, width), F32)),
        in_specs=[HBM] * 6 + [VMEM] * 2 + [SMEM, HBM] + [VMEM] * 3,
        out_specs=(HBM, HBM, VMEM),
        scratch_shapes=[
            field,
            field,
            plane,
            plane,
            plane,
            plane,
            plane,
            field,
            field,
            field,
            pltpu.VMEM((blocks, mode_count, rows, LANES), F32),
            pltpu.VMEM((rows, LANES), F32),
            pltpu.VMEM((LANES, LANES), F32),
            pltpu.SemaphoreType.DMA((13 * blocks,)),
            pltpu.SemaphoreType.DMA((2, blocks)),
        ],
        compiler_params=limit,
        name="main_kernel",
    )(
        start_potential,
        forcing,
        horiz_coef,
        vert_coef,
        row_near,
        row_far,
        col_near,
        col_far,
        vert_mix,
        mode_shapes,
        bodies_t,
        response_t,
        old_t,
    )
    message = sum_over(message, ("gx", "gy"))

    local = pltpu.VMEM((levels, rows, cols), F32)
    potential, velocity_t, flux = pl.pallas_call(
        functools.partial(last_kernel, body_total),
        out_shape=(
            whole,
            jax.ShapeDtypeStruct((owned, mode_count), F32),
            jax.ShapeDtypeStruct((rows, cols), F32),
        ),
        in_specs=[VMEM] + [HBM] * 4 + [VMEM],
        out_specs=(HBM, VMEM, HBM),
        scratch_shapes=[
            local,
            local,
            local,
            pltpu.VMEM((mode_count, rows, cols), F32),
            pltpu.VMEM((rows, cols), F32),
            pltpu.SemaphoreType.DMA((levels, 3)),
            pltpu.SemaphoreType.DMA((1,)),
            pltpu.SemaphoreType.DMA((levels + 1,)),
        ],
        compiler_params=limit,
        name="last_kernel",
    )(message, start_potential, direction, part, mode_shapes, bodies_t)
    return (potential, velocity_t.T, flux)


def solution(mesh):
    return jax.shard_map(
        per_device,
        mesh=mesh,
        in_specs=(
            P(None, "gx", "gy"),
            P(None, "gx", "gy"),
            P("gx", "gy"),
            P("gx", "gy"),
            P(),
            P(None, "gx", "gy"),
            P("gx", "gy"),
            P(None, None, ("gx", "gy")),
            P(None, ("gx", "gy")),
        ),
        out_specs=(P(None, "gx", "gy"), P(None, ("gx", "gy")), P("gx", "gy")),
        check_vma=False,
    )
```

```python
import functools
import math

import jax
import jax.numpy as jnp
from jax import lax
from jax.experimental import pallas as pl
from jax.experimental.pallas import tpu as pltpu
from jax.sharding import PartitionSpec as P

FOOT = 8192
LANES = 128
SUB = 8
FAR = 16.0
F32 = jnp.float32
HBM = pl.BlockSpec(memory_space=pltpu.HBM)
VMEM = pl.BlockSpec(memory_space=pltpu.VMEM)
SMEM = pl.BlockSpec(memory_space=pltpu.SMEM)


def iota(shape, dim):
    return lax.broadcasted_iota(jnp.int32, shape, dim)


def tile_at(index):
    return pl.ds(pl.multiple_of(index * SUB, SUB), SUB)


def stencil(ref, row, wanted, tiles, levels, coefs, lane, wrap):
    center = [[ref[t, l, pl.ds(row, SUB), :] for l in range(levels)] for t in range(tiles)]
    result = []
    for t in wanted:
        horiz, vert = coefs[t]
        last_coef = 5.0 * horiz + vert
        mid_coef = last_coef + vert
        horiz12 = horiz * (1.0 / 12.0)
        per_level = []
        for l in range(levels):
            x = center[t][l]
            after = center[(t + 1) % tiles][l] if wrap or t + 1 < tiles else 0.0
            before = center[(t - 1) % tiles][l] if wrap or t > 0 else 0.0

            def rows_at(offset):
                return ref[t, l, pl.ds(row + offset, SUB), :]

            right1 = pltpu.roll(jnp.where(lane < 1, after, x), LANES - 1, 1)
            right2 = pltpu.roll(jnp.where(lane < 2, after, x), LANES - 2, 1)
            left1 = pltpu.roll(jnp.where(lane >= LANES - 1, before, x), 1, 1)
            left2 = pltpu.roll(jnp.where(lane >= LANES - 2, before, x), 2, 1)
            nearest = (rows_at(-1) + rows_at(1)) + (right1 + left1)
            farther = (rows_at(-2) + rows_at(2)) + (right2 + left2)
            if l == 0:
                beside = center[t][1]
            elif l == levels - 1:
                beside = center[t][l - 1]
            else:
                beside = center[t][l - 1] + center[t][l + 1]
            coef = last_coef if l == levels - 1 else mid_coef
            per_level.append(coef * x + horiz12 * (farther - FAR * nearest) - vert * beside)
        result.append(per_level)
    return result


def residual_kernel(
    phi, forcing, horiz_in, vert_in, res, near_out, far_out, phi_s, horiz, vert, sems
):
    levels, rows, cols = phi.shape
    blocks = cols // LANES
    row_tiles = rows // SUB
    lane, sub = iota((SUB, LANES), 1), iota((SUB, LANES), 0)
    zero = jnp.zeros((SUB, LANES), F32)
    pairs = [(horiz_in, horiz), (vert_in, vert)]
    for t in range(blocks):
        lanes = pl.ds(t * LANES, LANES)
        pairs.append((phi.at[:, :, lanes], phi_s.at[t, :, pl.ds(SUB, rows)]))
        pairs.append((forcing.at[:, :, lanes], res.at[t]))
    copies = [pltpu.make_async_copy(a, b, sems.at[n]) for n, (a, b) in enumerate(pairs)]
    for copy in copies:
        copy.start()
    for t in range(blocks):
        for l in range(levels):
            phi_s[t, l, 0:SUB, :] = zero
            phi_s[t, l, rows + SUB : rows + 2 * SUB, :] = zero
    for copy in copies:
        copy.wait()

    def body(i, carry):
        here = tile_at(i)
        row = pl.multiple_of(i * SUB + SUB, SUB)
        coefs = []
        for t in range(blocks):
            lanes = pl.ds(t * LANES, LANES)
            coefs.append((horiz[here, lanes], vert[here, lanes]))
        image = stencil(phi_s, row, range(blocks), blocks, levels, coefs, lane, False)
        for t in range(blocks):
            for l in range(levels):
                res[t, l, here, :] = res[t, l, here, :] - image[t][l]
        return carry

    lax.fori_loop(0, row_tiles, body, 0, unroll=2)

    even = lax.rem(lax.axis_index("gx"), 2) == 0
    upper = sub < SUB // 2
    first, last = pl.ds(0, SUB), pl.ds(rows - SUB, SUB)
    for t in range(blocks):
        lanes = pl.ds(t * LANES, LANES)
        for l in range(levels + 1):
            if l < levels:
                pairs = [
                    (res[t, l, at, :], phi_s[t, l, pl.ds(row, SUB), :])
                    for at, row in ((first, SUB), (last, rows))
                ]
            else:
                pairs = [(horiz[at, lanes], vert[at, lanes]) for at in (first, last)]
            (a_top, b_top), (a_low, b_low) = pairs
            top = jnp.where(upper, a_top, pltpu.roll(b_top, SUB // 2, 0))
            low = jnp.where(upper, pltpu.roll(b_low, SUB // 2, 0), a_low)
            near_out[l, :, lanes] = jnp.where(even, low, top)
            far_out[l, :, lanes] = jnp.where(even, top, low)


def lane_kinds(lane, levels):
    pair = (lane >= 8 * levels) & (lane < 12 * levels)
    from_left = jnp.where(pair, lane & 2, 4 - (lane & 4)) != 0
    return pair, from_left


def coef_slot(levels):
    return (12 * levels + 7) // 8 * 8


def pack_tile(res, phi, coefs, lane):
    levels = len(res)
    packed = jnp.zeros((SUB, LANES), F32)
    slots = [(8 * l, 8, value) for l, value in enumerate(res)]
    slots += [(coef_slot(levels) + 8 * n, 8, value) for n, value in enumerate(coefs)]
    slots += [(8 * levels + 4 * l, 4, value) for l, value in enumerate(phi)]
    for low, size, value in slots:
        here = (lane >= low) & (lane < low + size)
        packed = jnp.where(here, pltpu.roll(value, low + size // 2, 1), packed)
    pair = (lane >= 8 * levels) & (lane < 12 * levels)
    after = jnp.where(pair & ((lane & 3) == 0), pltpu.roll(packed, LANES - 1, 1), 0.0)
    before = jnp.where(pair & ((lane & 3) == 3), pltpu.roll(packed, 1, 1), 0.0)
    return packed - FAR * (after + before)


def inner_kernel(
    body_total, res, phi, horiz, vert, response_t, old_t, packed, table, small_s
):
    blocks, levels, rows, _ = res.shape
    cols = phi.shape[2]
    right = pl.ds(cols - LANES, LANES)
    left = pl.ds(0, LANES)
    lane = iota((SUB, LANES), 1)
    first = lane < LANES // 2

    def body(i, carry):
        here = tile_at(i)
        packed[tile_at(i + 1), :] = pack_tile(
            [jnp.where(first, res[0, l, here, :], res[blocks - 1, l, here, :]) for l in range(levels)],
            [jnp.where(first, phi[l, here, left], phi[l, here, right]) for l in range(levels)],
            [jnp.where(first, ref[here, left], ref[here, right]) for ref in (horiz, vert)],
            lane,
        )
        return carry

    lax.fori_loop(1, rows // SUB - 1, body, 0, unroll=2)

    owned, mode_count = old_t.shape
    width = table.shape[1]
    small_s[...] = jnp.zeros((LANES, LANES), F32)
    for k in range(mode_count):
        small_s[k * SUB : k * SUB + owned, 0:mode_count] = response_t[k]
        small_s[k * SUB : k * SUB + owned, mode_count : mode_count + 1] = old_t[:, k : k + 1]
    values = small_s[...].T[0:SUB, :]
    if width > LANES:
        values = jnp.concatenate([values, jnp.zeros((SUB, width - LANES), F32)], axis=1)
    wide_lane = iota((SUB, width), 1)
    me = (lax.axis_index("gx") * lax.axis_size("gy") + lax.axis_index("gy")) * owned
    for pair in range(mode_count // 2):
        tile = jnp.zeros((SUB, width), F32)
        for half in range(2):
            place = half * body_total + me
            shift = lax.rem(place - (2 * pair + half) * SUB + width, width)
            here = (wide_lane >= place) & (wide_lane < place + owned)
            tile = jnp.where(here, pltpu.roll(values, shift, 1), tile)
        table[pair * SUB : (pair + 1) * SUB, :] = tile


def edge_kernel(
    res, phi, horiz, vert, row_near, row_far, packed, edge, edge_coef, own, near_out, far_out
):
    blocks, levels, rows, _ = res.shape
    row_tiles = rows // SUB
    lane, sub = iota((SUB, LANES), 1), iota((SUB, LANES), 0)
    even = lax.rem(lax.axis_index("gx"), 2) == 0
    upper = sub < SUB // 2
    half = SUB // 2
    values = {}
    for t in range(blocks):
        lanes = pl.ds(t * LANES, LANES)
        near, far = row_near[levels, :, lanes], row_far[levels, :, lanes]
        above, below = jnp.where(even, far, near), jnp.where(even, near, far)
        h_up, v_up = jnp.where(upper, 0.0, above), jnp.where(upper, 0.0, pltpu.roll(above, half, 0))
        h_down = jnp.where(upper, below, 0.0)
        v_down = jnp.where(upper, pltpu.roll(below, half, 0), 0.0)
        edge_coef[0, 0, t], edge_coef[0, 1, t] = h_up, v_up
        edge_coef[1, 0, t], edge_coef[1, 1, t] = h_down, v_down
        first, last = pl.ds(0, SUB), pl.ds(rows - SUB, SUB)
        h_first, h_last = horiz[first, lanes], horiz[last, lanes]
        coefs = [(h_up, v_up), (h_first, vert[first, lanes]), (h_last, vert[last, lanes])]
        coefs.append((h_down, v_down))
        for n, pair in enumerate(coefs):
            values[n, t, "coef"] = pair
        scaled = [h * (1.0 / 12.0) for h, _ in coefs]

        def from_above(value):
            near_row = jnp.where(sub < 1, pltpu.roll(value, 1, 0), 0.0)
            far_row = jnp.where(sub < 2, pltpu.roll(value, 2, 0), 0.0)
            return far_row - FAR * near_row

        def from_below(value):
            near_row = jnp.where(sub >= SUB - 1, pltpu.roll(value, SUB - 1, 0), 0.0)
            far_row = jnp.where(sub >= SUB - 2, pltpu.roll(value, SUB - 2, 0), 0.0)
            return far_row - FAR * near_row

        for l in range(levels):
            near, far = row_near[l, :, lanes], row_far[l, :, lanes]
            above, below = jnp.where(even, far, near), jnp.where(even, near, far)
            res_up = jnp.where(upper, 0.0, above)
            phi_up = jnp.where(upper, 0.0, pltpu.roll(above, half, 0))
            res_down = jnp.where(upper, below, 0.0)
            phi_down = jnp.where(upper, pltpu.roll(below, half, 0), 0.0)
            phi_first, phi_last = phi[l, first, lanes], phi[l, last, lanes]
            fixed = (
                res_up - scaled[0] * from_below(phi_first),
                res[t, l, first, :] - scaled[1] * from_above(phi_up),
                res[t, l, last, :] - scaled[2] * from_below(phi_down),
                res_down - scaled[3] * from_above(phi_last),
            )
            for n, value in enumerate(fixed):
                edge[n, t, l] = value
                values[n, t, l] = value
            for n, value in enumerate((phi_up, phi_first, phi_last, phi_down)):
                values[n, t, l, "phi"] = value

    start = lane < LANES // 2
    end = blocks - 1
    tiles = [packed[i * SUB : (i + 1) * SUB, :] for i in range(row_tiles + 2)]
    for n, place in enumerate((0, 1, row_tiles, row_tiles + 1)):
        tiles[place] = pack_tile(
            [jnp.where(start, values[n, 0, l], values[n, end, l]) for l in range(levels)],
            [
                jnp.where(start, values[n, 0, l, "phi"], values[n, end, l, "phi"])
                for l in range(levels)
            ],
            [jnp.where(start, values[n, 0, "coef"][c], values[n, end, "coef"][c]) for c in range(2)],
            lane,
        )
    pair, from_left = lane_kinds(lane, levels)
    col_even = lax.rem(lax.axis_index("gy"), 2) == 0
    turned = []
    for i, tile in enumerate(tiles):
        moved = jnp.where((lane & 2) == 0, pltpu.roll(tile, LANES - 2, 1), pltpu.roll(tile, 2, 1))
        turned.append(jnp.where(pair, moved, tile))
        own[i * SUB : (i + 1) * SUB, :] = turned[i]
    fold = (row_tiles + 2) // 2
    for i in range(fold):
        other = tiles[i + fold]
        to_right = jnp.where(pair, other, pltpu.roll(other, 4, 1))
        to_right = jnp.where(from_left, turned[i], to_right)
        to_left = jnp.where(pair, other, pltpu.roll(other, LANES - 4, 1))
        to_left = jnp.where(from_left, to_left, turned[i])
        near_out[i * SUB : (i + 1) * SUB, :] = jnp.where(col_even, to_right, to_left)
        far_out[i * SUB : (i + 1) * SUB, :] = jnp.where(col_even, to_left, to_right)


def lane_sums(entries, lane):
    step = 1
    while len(entries) > 1:
        low = (lane & step) == 0
        merged = []
        for a, b in zip(entries[::2], entries[1::2]):
            if a is None:
                merged.append(None)
                continue
            b = jnp.zeros_like(a) if b is None else b
            merged.append(jnp.where(low, a, b) + pltpu.roll(jnp.where(low, b, a), step, 1))
        entries = merged
        step *= 2
    total = entries[0]
    while step < LANES:
        total = total + pltpu.roll(total, step, 1)
        step *= 2
    return total


def main_kernel(
    body_total,
    res,
    edge,
    horiz,
    vert,
    edge_coef,
    own,
    col_near,
    col_far,
    table,
    mix,
    modes,
    bodies_t,
    dir_s,
    part_s,
    message,
    res_s,
    img_s,
    horiz_s,
    vert_s,
    scale_s,
    got_s,
    sums_s,
):
    blocks, levels, rows, _ = res.shape
    mode_count = modes.shape[0]
    tiles = blocks + 1
    side = blocks
    row_tiles = rows // SUB
    base = 2 * SUB
    lane = iota((SUB, LANES), 1)
    everything = range(tiles)

    pair, from_left = lane_kinds(lane, levels)
    even = lax.rem(lax.axis_index("gy"), 2) == 0
    fold = (row_tiles + 2) // 2
    for i in range(fold):
        here = pl.ds(i * SUB, SUB)
        near, far = col_near[here, :], col_far[here, :]
        left, right = jnp.where(even, far, near), jnp.where(even, near, far)
        got_s[here, :] = jnp.where(from_left, left, right)
        left = jnp.where(pair, pltpu.roll(left, 2, 1), pltpu.roll(left, LANES - 4, 1))
        right = jnp.where(pair, pltpu.roll(right, LANES - 2, 1), pltpu.roll(right, 4, 1))
        there = pl.ds((i + fold) * SUB, SUB)
        got_s[there, :] = jnp.where(from_left, left, right)

    def first(i, inner, residuals, coefs):
        here = tile_at(i)
        there = tile_at(i + 1)
        got, mine = got_s[here, :], own[here, :]
        halo = (lane < 4) | (lane >= LANES - 4)
        slot = coef_slot(levels)
        side_coef = [
            jnp.where(halo, pltpu.roll(got, (LANES - 4 - slot - 8 * n) % LANES, 1), 0.0) for n in range(2)
        ]
        coefs = list(coefs) + [tuple(side_coef)]
        outer = (lane < 2, lane >= LANES - 2, (lane < 2) | (lane >= LANES - 2))
        scales, edges = [], []
        for t in everything:
            h, v = coefs[t]
            bottom = 5.0 * h + 2.0 * v
            inside = bottom > 0.0
            scale = jnp.where(inside, 1.0 / jnp.where(inside, bottom, 1.0), 0.0)
            scales.append(scale)
            scale_s[t, there, :] = scale
            horiz_s[t, there, :] = h
            vert_s[t, there, :] = v
            if t == side:
                mask = outer[2]
            elif blocks == 1:
                mask = outer[2]
            elif t == 0:
                mask = outer[0]
            elif t == blocks - 1:
                mask = outer[1]
            else:
                mask = None
            edges.append(None if mask is None else jnp.where(mask, h * (1.0 / 12.0), 0.0))
        weighted = [[] for _ in everything]
        for l in range(levels):
            place = (LANES - 2 - 8 * levels - 4 * l) % LANES
            theirs = pltpu.roll(got, place, 1)
            ours = pltpu.roll(mine, place, 1)
            for t in everything:
                if t == side:
                    value = pltpu.roll(got, (LANES - 4 - 8 * l) % LANES, 1) - edges[t] * ours
                else:
                    value = residuals[t][l]
                    if edges[t] is not None:
                        value = value - edges[t] * theirs
                    if inner:
                        res_s[t, l, there, :] = value
                weighted[t].append(value * scales[t])
        for t in everything:
            for l, value in enumerate(mix_levels(mix, weighted[t], levels)):
                dir_s[t, l, there, :] = value

    def own_coefs(i):
        here = tile_at(i)
        result = []
        for t in range(blocks):
            lanes = pl.ds(t * LANES, LANES)
            result.append((horiz[here, lanes], vert[here, lanes]))
        return result

    for n, i in enumerate((0, 1, row_tiles, row_tiles + 1)):
        residuals = [[edge[n, t, l] for l in range(levels)] for t in range(blocks)]
        if 1 <= i <= row_tiles:
            coefs = own_coefs(i - 1)
        else:
            coefs = [(edge_coef[n // 2, 0, t], edge_coef[n // 2, 1, t]) for t in range(blocks)]
        first(i, 1 <= i <= row_tiles, residuals, coefs)

    def first_body(i, carry):
        here = tile_at(i - 1)
        residuals = [[res[t, l, here, :] for l in range(levels)] for t in range(blocks)]
        first(i, True, residuals, own_coefs(i - 1))
        return carry

    lax.fori_loop(2, row_tiles, first_body, 0, unroll=2)

    def coefs_at(row, count):
        here = pl.ds(row, SUB)
        return [(horiz_s[t, here, :], vert_s[t, here, :]) for t in range(count)]

    def second(i, carry):
        row = pl.multiple_of(i * SUB + SUB, SUB)
        here = pl.ds(row, SUB)
        image = stencil(
            dir_s, row, everything, tiles, levels, coefs_at(row, tiles), lane, True
        )
        for t in everything:
            scale = scale_s[t, here, :]
            weighted = []
            for l in range(levels):
                img_s[t, l, here, :] = image[t][l]
                weighted.append(image[t][l] * scale)
            for l, value in enumerate(mix_levels(mix, weighted, levels)):
                part_s[t, l, here, :] = value
        return carry

    lax.fori_loop(0, row_tiles + 2, second, 0, unroll=3)

    for i in range(row_tiles):
        row = pl.ds(base + i * SUB, SUB)
        here = pl.ds(i * SUB, SUB)
        entries = [None] * 32
        for t in range(blocks):
            lanes = pl.ds(t * LANES, LANES)
            for q, field in enumerate((dir_s, part_s)):
                surface = field[t, 0, row, :]
                for k in range(mode_count):
                    entries[(2 * t + q) * SUB + k] = modes[k, here, lanes] * surface
        sums_s[here, :] = lane_sums(entries, lane)

    def third(i, totals):
        row = pl.multiple_of(i * SUB + base, SUB)
        here = pl.ds(row, SUB)
        image = stencil(
            part_s, row, range(blocks), tiles, levels, coefs_at(row, blocks), lane, True
        )
        totals = list(totals)
        for t in range(blocks):
            for l in range(levels):
                residual = res_s[t, l, here, :]
                img1 = img_s[t, l, here, :]
                img2 = image[t][l]
                products = (residual * img1, img1 * img1, residual * img2, img1 * img2, img2 * img2)
                totals = [total + product for total, product in zip(totals, products)]
        return tuple(totals)

    zero = jnp.zeros((SUB, LANES), F32)
    totals = lax.fori_loop(0, row_tiles, third, (zero,) * 5, unroll=2)

    width = message.shape[1]
    sums_t = sums_s[...].T
    forces = jnp.zeros((SUB, width), F32)
    for t in range(blocks):
        hits = body_hits(bodies_t, t, body_total, width)
        first_sums = sums_t[2 * t * SUB : (2 * t + 1) * SUB, :]
        second_sums = sums_t[(2 * t + 1) * SUB : (2 * t + 2) * SUB, :]
        forces = forces + dot_nt(first_sums, hits)
        forces = forces + pltpu.roll(dot_nt(second_sums, hits), body_total, 1)
    wide_sub, wide_lane = iota((SUB, width), 0), iota((SUB, width), 1)
    for q, total in enumerate(totals):
        forces = jnp.where((wide_sub == SUB - 2) & (wide_lane == q), jnp.sum(total), forces)
    message[0:SUB, :] = forces
    message[SUB:, :] = table[...]


def mix_levels(mix, weighted, levels):
    out = []
    for l in range(levels):
        total = (mix[l, l] + 1.0) * weighted[l]
        for m in range(levels):
            if m != l:
                total = total + mix[l, m] * weighted[m]
        out.append(total)
    return out


def body_hits(bodies_t, block, count, width):
    ids = bodies_t[block : block + 1, :]
    ids = jnp.where(ids < count, ids, -1)
    wanted = lax.broadcasted_iota(jnp.int32, (width, ids.shape[1]), 0)
    return (jnp.broadcast_to(ids, wanted.shape) == wanted).astype(F32)


def dot_nt(a, b):
    return lax.dot_general(
        a, b, (((1,), (1,)), ((), ())), precision=lax.Precision.HIGHEST, preferred_element_type=F32
    )


def last_kernel(
    body_total,
    message,
    phi,
    direction,
    part,
    modes,
    bodies_t,
    potential,
    velocity_t,
    flux,
    phi_s,
    flux_s,
    out_sems,
):
    levels, rows, cols = phi.shape
    mode_count = modes.shape[0]
    blocks = cols // LANES
    width = message.shape[1]
    owned = velocity_t.shape[0]
    main = pl.ds(2 * SUB, rows)
    top = message[0:SUB, :]

    def scalar(q):
        return top[SUB - 2 : SUB - 1, q : q + 1]

    cross_first, square_first, cross_mixed, square_mixed, square_second = [
        scalar(q) for q in range(5)
    ]
    first_step = cross_first / square_first
    next_top = (
        cross_first
        - first_step * cross_mixed
        - first_step * square_first
        + first_step * first_step * square_mixed
    )
    next_bottom = (
        square_first - 2.0 * first_step * square_mixed + first_step * first_step * square_second
    )
    second_step = next_top / next_bottom
    on_dir = first_step + second_step
    on_part = first_step * second_step

    wide_sub = lax.broadcasted_iota(jnp.int32, (SUB, width), 0)
    wide_lane = lax.broadcasted_iota(jnp.int32, (SUB, width), 1)
    foot_scale = 1.0 / math.sqrt(FOOT)
    forces = foot_scale * (on_part * pltpu.roll(top, body_total, 1) - on_dir * top)
    forces = jnp.where(wide_sub == mode_count, 1.0, forces)
    forces = jnp.where(wide_lane < body_total, forces, 0.0)
    velocity = jnp.zeros((SUB, width), F32)
    for k in range(mode_count):
        table = message[(k // 2 + 1) * SUB : (k // 2 + 2) * SUB, :]
        if k % 2:
            table = pltpu.roll(table, body_total, 1)
        value = jnp.sum(table * forces, axis=0, keepdims=True)
        velocity = jnp.where(wide_sub == k, value, velocity)

    me = (lax.axis_index("gx") * lax.axis_size("gy") + lax.axis_index("gy")) * owned
    mine = ((wide_lane == me + wide_sub) & (wide_sub < owned)).astype(F32)
    velocity_t[...] = dot_nt(mine, velocity)[0:owned, 0:mode_count]

    per_row = []
    for t in range(blocks):
        hits = body_hits(bodies_t, t, body_total, width)
        per_row.append(
            lax.dot_general(
                velocity,
                hits,
                (((1,), (0,)), ((), ())),
                precision=lax.Precision.HIGHEST,
                preferred_element_type=F32,
            )
        )
    per_row.append(jnp.zeros((LANES - blocks * SUB, rows), F32))
    spread = jnp.concatenate(per_row, axis=0).T

    for t in range(blocks):
        lanes = pl.ds(t * LANES, LANES)
        total = jnp.zeros((rows, LANES), F32)
        for k in range(mode_count):
            total = total + modes[k, :, lanes] * spread[:, t * SUB + k : t * SUB + k + 1]
        flux_s[:, lanes] = total
    flux_copy = pltpu.make_async_copy(flux_s, flux, out_sems.at[levels])
    flux_copy.start()
    outgoing = [flux_copy]
    for l in range(levels):
        for t in range(blocks):
            lanes = pl.ds(t * LANES, LANES)
            change = on_dir * direction[t, l, main, :] - on_part * part[t, l, main, :]
            phi_s[l, :, lanes] = phi[l, :, lanes] + change
        copy = pltpu.make_async_copy(phi_s.at[l], potential.at[l], out_sems.at[l])
        copy.start()
        outgoing.append(copy)
    for copy in outgoing:
        copy.wait()


def swap_near(value, axis):
    size = lax.axis_size(axis)
    return lax.ppermute(value, axis, [(i, i ^ 1) for i in range(size)])


def swap_far(value, axis):
    size = lax.axis_size(axis)
    pairs = [(i, i + 1) for i in range(1, size - 1, 2)]
    return lax.ppermute(value, axis, pairs + [(j, i) for i, j in pairs])


def sum_over(value, axes):
    for axis in axes:
        size = lax.axis_size(axis)
        step = 1
        while step < size:
            value = value + lax.ppermute(value, axis, [(i, i ^ step) for i in range(size)])
            step *= 2
    return value


def per_device(
    forcing,
    start_potential,
    horiz_coef,
    vert_coef,
    vert_mix,
    mode_shapes,
    block_body,
    response,
    velocity_old,
):
    levels, rows, cols = forcing.shape
    mode_count = mode_shapes.shape[0]
    blocks = cols // LANES
    tiles = blocks + 1
    padded = rows + 4 * SUB
    owned = velocity_old.shape[1]
    body_total = owned * lax.axis_size(("gx", "gy"))
    width = 2 * body_total
    bodies_t = block_body.T
    response_t = jnp.swapaxes(response, 1, 2)
    old_t = velocity_old.T
    limit = pltpu.CompilerParams(vmem_limit_bytes=24 * 2**20)

    def call(kernel, name, outs, ins, args, scratch=()):
        return pl.pallas_call(
            kernel,
            out_shape=tuple(jax.ShapeDtypeStruct(shape, F32) for shape, _ in outs),
            in_specs=ins,
            out_specs=tuple(spec for _, spec in outs),
            scratch_shapes=list(scratch),
            compiler_params=limit,
            name=name,
        )(*args)

    strip = (levels + 1, SUB, cols)
    inner = (blocks, levels, rows, LANES)
    res, near, far = call(
        residual_kernel,
        "residual_kernel",
        [(inner, VMEM), (strip, VMEM), (strip, VMEM)],
        [HBM] * 4,
        [
            pltpu.with_memory_space_constraint(value, pltpu.HBM)
            for value in (start_potential, forcing, horiz_coef, vert_coef)
        ],
        [
            pltpu.VMEM((blocks, levels, rows + 2 * SUB, LANES), F32),
            pltpu.VMEM((rows, cols), F32),
            pltpu.VMEM((rows, cols), F32),
            pltpu.SemaphoreType.DMA((2 + 2 * blocks,)),
        ],
    )
    row_near, row_far = swap_near(near, "gx"), swap_far(far, "gx")
    packed_shape = (rows + 2 * SUB, LANES)
    packed, table = call(
        functools.partial(inner_kernel, body_total),
        "inner_kernel",
        [(packed_shape, VMEM), ((3 * SUB, width), VMEM)],
        [VMEM] * 6,
        (res, start_potential, horiz_coef, vert_coef, response_t, old_t),
        [pltpu.VMEM((LANES, LANES), F32)],
    )
    strip = (rows // 2 + SUB, LANES)
    edge, edge_coef, own, near, far = call(
        edge_kernel,
        "edge_kernel",
        [
            ((4, blocks, levels, SUB, LANES), VMEM),
            ((2, 2, blocks, SUB, LANES), VMEM),
            (packed_shape, VMEM),
            (strip, VMEM),
            (strip, VMEM),
        ],
        [VMEM] * 7,
        (res, start_potential, horiz_coef, vert_coef, row_near, row_far, packed),
    )
    col_near, col_far = swap_near(near, "gy"), swap_far(far, "gy")

    field = (tiles, levels, padded, LANES)
    plane = pltpu.VMEM((tiles, padded, LANES), F32)
    direction, part, message = call(
        functools.partial(main_kernel, body_total),
        "main_kernel",
        [(field, VMEM), (field, VMEM), ((4 * SUB, width), VMEM)],
        [VMEM] * 9 + [SMEM] + [VMEM] * 2,
        (
            res,
            edge,
            horiz_coef,
            vert_coef,
            edge_coef,
            own,
            col_near,
            col_far,
            table,
            vert_mix,
            mode_shapes,
            bodies_t,
        ),
        [
            pltpu.VMEM((blocks, levels, padded, LANES), F32),
            pltpu.VMEM(field, F32),
            plane,
            plane,
            plane,
            pltpu.VMEM(packed_shape, F32),
            pltpu.VMEM((rows, LANES), F32),
        ],
    )
    message = sum_over(message, ("gx", "gy"))

    potential, velocity_t, flux = call(
        functools.partial(last_kernel, body_total),
        "last_kernel",
        [((levels, rows, cols), HBM), ((owned, mode_count), VMEM), ((rows, cols), HBM)],
        [VMEM] * 6,
        (message, start_potential, direction, part, mode_shapes, bodies_t),
        [
            pltpu.VMEM((levels, rows, cols), F32),
            pltpu.VMEM((rows, cols), F32),
            pltpu.SemaphoreType.DMA((levels + 1,)),
        ],
    )
    return (potential, velocity_t.T, flux)


def solution(mesh):
    return jax.shard_map(
        per_device,
        mesh=mesh,
        in_specs=(
            P(None, "gx", "gy"),
            P(None, "gx", "gy"),
            P("gx", "gy"),
            P("gx", "gy"),
            P(),
            P(None, "gx", "gy"),
            P("gx", "gy"),
            P(None, None, ("gx", "gy")),
            P(None, ("gx", "gy")),
        ),
        out_specs=(P(None, "gx", "gy"), P(None, ("gx", "gy")), P("gx", "gy")),
        check_vma=False,
    )
```

```python
import functools
import math

import jax
import jax.numpy as jnp
from jax import lax
from jax.experimental import pallas as pl
from jax.experimental.pallas import tpu as pltpu
from jax.sharding import PartitionSpec as P

FOOT = 8192
LANES = 128
SUB = 8
FAR = 16.0
F32 = jnp.float32
HBM = pl.BlockSpec(memory_space=pltpu.HBM)
VMEM = pl.BlockSpec(memory_space=pltpu.VMEM)
SMEM = pl.BlockSpec(memory_space=pltpu.SMEM)


def iota(shape, dim):
    return lax.broadcasted_iota(jnp.int32, shape, dim)


def tile_at(index):
    return pl.ds(pl.multiple_of(index * SUB, SUB), SUB)


def stencil(ref, row, wanted, tiles, levels, coefs, lane, wrap):
    for t in wanted:
        center = {
            u: [ref[u % tiles, l, pl.ds(row, SUB), :] for l in range(levels)]
            for u in (t - 1, t, t + 1)
        }
        horiz, vert = coefs[t]
        last_coef = 5.0 * horiz + vert
        mid_coef = last_coef + vert
        horiz12 = horiz * (1.0 / 12.0)
        per_level = []
        for l in range(levels):
            x = center[t][l]
            after = center[t + 1][l] if wrap or t + 1 < tiles else 0.0
            before = center[t - 1][l] if wrap or t > 0 else 0.0

            def rows_at(offset):
                return ref[t, l, pl.ds(row + offset, SUB), :]

            right1 = pltpu.roll(jnp.where(lane < 1, after, x), LANES - 1, 1)
            right2 = pltpu.roll(jnp.where(lane < 2, after, x), LANES - 2, 1)
            left1 = pltpu.roll(jnp.where(lane >= LANES - 1, before, x), 1, 1)
            left2 = pltpu.roll(jnp.where(lane >= LANES - 2, before, x), 2, 1)
            nearest = (rows_at(-1) + rows_at(1)) + (right1 + left1)
            farther = (rows_at(-2) + rows_at(2)) + (right2 + left2)
            if l == 0:
                beside = center[t][1]
            elif l == levels - 1:
                beside = center[t][l - 1]
            else:
                beside = center[t][l - 1] + center[t][l + 1]
            coef = last_coef if l == levels - 1 else mid_coef
            per_level.append(coef * x + horiz12 * (farther - FAR * nearest) - vert * beside)
        yield t, per_level


def strip_kernel(phi, forcing, horiz_in, vert_in, near_out, far_out, phi_s, res_s, horiz, vert, sems):
    levels, rows, cols = phi.shape
    blocks = cols // LANES
    lane, sub = iota((SUB, LANES), 1), iota((SUB, LANES), 0)
    pairs = []
    for end, row in enumerate((0, rows - SUB)):
        here = pl.ds(row, SUB)
        pairs.append((horiz_in.at[here], horiz.at[end]))
        pairs.append((vert_in.at[here], vert.at[end]))
        for t in range(blocks):
            lanes = pl.ds(t * LANES, LANES)
            pairs.append((phi.at[:, here, lanes], phi_s.at[end, t, :, pl.ds(SUB, SUB)]))
            pairs.append((forcing.at[:, here, lanes], res_s.at[end, t]))
    copies = [pltpu.make_async_copy(a, b, sems.at[n]) for n, (a, b) in enumerate(pairs)]
    for copy in copies:
        copy.start()
    zero = jnp.zeros((SUB, LANES), F32)
    for end in range(2):
        for t in range(blocks):
            for l in range(levels):
                phi_s[end, t, l, 0:SUB, :] = zero
                phi_s[end, t, l, 2 * SUB : 3 * SUB, :] = zero
    for copy in copies:
        copy.wait()
    even = lax.rem(lax.axis_index("gx"), 2) == 0
    upper = sub < SUB // 2
    kept = []
    for end in range(2):
        coefs = [
            (horiz[end, :, t * LANES : (t + 1) * LANES], vert[end, :, t * LANES : (t + 1) * LANES])
            for t in range(blocks)
        ]
        image = stencil(phi_s.at[end], SUB, range(blocks), blocks, levels, coefs, lane, False)
        strips = {}
        for t, image_t in image:
            for l in range(levels):
                potential = phi_s[end, t, l, SUB : 2 * SUB, :]
                strips[t, l] = (res_s[end, t, l] - image_t[l], potential)
            strips[t, levels] = coefs[t]
        kept.append(strips)
    for place, (a_top, b_top) in kept[0].items():
        a_low, b_low = kept[1][place]
        t, l = place
        lanes = pl.ds(t * LANES, LANES)
        top = jnp.where(upper, a_top, pltpu.roll(b_top, SUB // 2, 0))
        low = jnp.where(upper, pltpu.roll(b_low, SUB // 2, 0), a_low)
        near_out[l, :, lanes] = jnp.where(even, low, top)
        far_out[l, :, lanes] = jnp.where(even, top, low)


def lane_kinds(lane, levels):
    pair = (lane >= 8 * levels) & (lane < 12 * levels)
    from_left = jnp.where(pair, lane & 2, 4 - (lane & 4)) != 0
    return pair, from_left


def coef_slot(levels):
    return (12 * levels + 7) // 8 * 8


def pack_tile(res, phi, coefs, lane):
    levels = len(res)
    packed = jnp.zeros((SUB, LANES), F32)
    slots = [(8 * l, 8, value) for l, value in enumerate(res)]
    slots += [(coef_slot(levels) + 8 * n, 8, value) for n, value in enumerate(coefs)]
    slots += [(8 * levels + 4 * l, 4, value) for l, value in enumerate(phi)]
    for low, size, value in slots:
        here = (lane >= low) & (lane < low + size)
        packed = jnp.where(here, pltpu.roll(value, low + size // 2, 1), packed)
    pair = (lane >= 8 * levels) & (lane < 12 * levels)
    after = jnp.where(pair & ((lane & 3) == 0), pltpu.roll(packed, LANES - 1, 1), 0.0)
    before = jnp.where(pair & ((lane & 3) == 3), pltpu.roll(packed, 1, 1), 0.0)
    return packed - FAR * (after + before)


def inner_kernel(
    body_total, phi, forcing, horiz, vert, response_t, old_t, res, packed, table, phi_s, small_s
):
    blocks, levels, rows, _ = res.shape
    cols = phi.shape[2]
    zero = jnp.zeros((SUB, LANES), F32)
    for t in range(blocks):
        for l in range(levels):
            phi_s[t, l, 0:SUB, :] = zero
            phi_s[t, l, rows + SUB : rows + 2 * SUB, :] = zero
            phi_s[t, l, SUB : rows + SUB, :] = phi[l, :, t * LANES : (t + 1) * LANES]
    right = pl.ds(cols - LANES, LANES)
    left = pl.ds(0, LANES)
    lane = iota((SUB, LANES), 1)
    first = lane < LANES // 2

    def residual(i, carry):
        here = tile_at(i)
        row = pl.multiple_of(i * SUB + SUB, SUB)
        coefs = []
        for t in range(blocks):
            lanes = pl.ds(t * LANES, LANES)
            coefs.append((horiz[here, lanes], vert[here, lanes]))
        image = stencil(phi_s, row, range(blocks), blocks, levels, coefs, lane, False)
        for t, image_t in image:
            for l in range(levels):
                own = forcing[l, here, pl.ds(t * LANES, LANES)]
                res[t, l, here, :] = own - image_t[l]
        return carry

    lax.fori_loop(0, rows // SUB, residual, 0, unroll=2)

    def body(i, carry):
        here = tile_at(i)
        packed[tile_at(i + 1), :] = pack_tile(
            [jnp.where(first, res[0, l, here, :], res[blocks - 1, l, here, :]) for l in range(levels)],
            [jnp.where(first, phi[l, here, left], phi[l, here, right]) for l in range(levels)],
            [jnp.where(first, ref[here, left], ref[here, right]) for ref in (horiz, vert)],
            lane,
        )
        return carry

    lax.fori_loop(1, rows // SUB - 1, body, 0, unroll=7)

    owned, mode_count = old_t.shape
    width = table.shape[1]
    small_s[...] = jnp.zeros((LANES, LANES), F32)
    for k in range(mode_count):
        small_s[k * SUB : k * SUB + owned, 0:mode_count] = response_t[k]
        small_s[k * SUB : k * SUB + owned, mode_count : mode_count + 1] = old_t[:, k : k + 1]
    values = small_s[...].T[0:SUB, :]
    if width > LANES:
        values = jnp.concatenate([values, jnp.zeros((SUB, width - LANES), F32)], axis=1)
    wide_lane = iota((SUB, width), 1)
    me = (lax.axis_index("gx") * lax.axis_size("gy") + lax.axis_index("gy")) * owned
    for pair in range(mode_count // 2):
        tile = jnp.zeros((SUB, width), F32)
        for half in range(2):
            place = half * body_total + me
            shift = lax.rem(place - (2 * pair + half) * SUB + width, width)
            here = (wide_lane >= place) & (wide_lane < place + owned)
            tile = jnp.where(here, pltpu.roll(values, shift, 1), tile)
        table[pair * SUB : (pair + 1) * SUB, :] = tile


def edge_kernel(
    res, phi, horiz, vert, row_near, row_far, packed, edge, edge_coef, own, near_out, far_out
):
    blocks, levels, rows, _ = res.shape
    row_tiles = rows // SUB
    lane, sub = iota((SUB, LANES), 1), iota((SUB, LANES), 0)
    even = lax.rem(lax.axis_index("gx"), 2) == 0
    upper = sub < SUB // 2
    half = SUB // 2
    values = {}
    for t in range(blocks):
        lanes = pl.ds(t * LANES, LANES)
        near, far = row_near[levels, :, lanes], row_far[levels, :, lanes]
        above, below = jnp.where(even, far, near), jnp.where(even, near, far)
        h_up, v_up = jnp.where(upper, 0.0, above), jnp.where(upper, 0.0, pltpu.roll(above, half, 0))
        h_down = jnp.where(upper, below, 0.0)
        v_down = jnp.where(upper, pltpu.roll(below, half, 0), 0.0)
        edge_coef[0, 0, t], edge_coef[0, 1, t] = h_up, v_up
        edge_coef[1, 0, t], edge_coef[1, 1, t] = h_down, v_down
        first, last = pl.ds(0, SUB), pl.ds(rows - SUB, SUB)
        h_first, h_last = horiz[first, lanes], horiz[last, lanes]
        coefs = [(h_up, v_up), (h_first, vert[first, lanes]), (h_last, vert[last, lanes])]
        coefs.append((h_down, v_down))
        for n, pair in enumerate(coefs):
            values[n, t, "coef"] = pair
        scaled = [h * (1.0 / 12.0) for h, _ in coefs]

        def from_above(value):
            near_row = jnp.where(sub < 1, pltpu.roll(value, 1, 0), 0.0)
            far_row = jnp.where(sub < 2, pltpu.roll(value, 2, 0), 0.0)
            return far_row - FAR * near_row

        def from_below(value):
            near_row = jnp.where(sub >= SUB - 1, pltpu.roll(value, SUB - 1, 0), 0.0)
            far_row = jnp.where(sub >= SUB - 2, pltpu.roll(value, SUB - 2, 0), 0.0)
            return far_row - FAR * near_row

        for l in range(levels):
            near, far = row_near[l, :, lanes], row_far[l, :, lanes]
            above, below = jnp.where(even, far, near), jnp.where(even, near, far)
            res_up = jnp.where(upper, 0.0, above)
            phi_up = jnp.where(upper, 0.0, pltpu.roll(above, half, 0))
            res_down = jnp.where(upper, below, 0.0)
            phi_down = jnp.where(upper, pltpu.roll(below, half, 0), 0.0)
            phi_first, phi_last = phi[l, first, lanes], phi[l, last, lanes]
            fixed = (
                res_up - scaled[0] * from_below(phi_first),
                res[t, l, first, :] - scaled[1] * from_above(phi_up),
                res[t, l, last, :] - scaled[2] * from_below(phi_down),
                res_down - scaled[3] * from_above(phi_last),
            )
            for n, value in enumerate(fixed):
                edge[n, t, l] = value
                values[n, t, l] = value
            for n, value in enumerate((phi_up, phi_first, phi_last, phi_down)):
                values[n, t, l, "phi"] = value

    start = lane < LANES // 2
    end = blocks - 1
    tiles = [packed[i * SUB : (i + 1) * SUB, :] for i in range(row_tiles + 2)]
    for n, place in enumerate((0, 1, row_tiles, row_tiles + 1)):
        tiles[place] = pack_tile(
            [jnp.where(start, values[n, 0, l], values[n, end, l]) for l in range(levels)],
            [
                jnp.where(start, values[n, 0, l, "phi"], values[n, end, l, "phi"])
                for l in range(levels)
            ],
            [jnp.where(start, values[n, 0, "coef"][c], values[n, end, "coef"][c]) for c in range(2)],
            lane,
        )
    pair, from_left = lane_kinds(lane, levels)
    col_even = lax.rem(lax.axis_index("gy"), 2) == 0
    turned = []
    for i, tile in enumerate(tiles):
        moved = jnp.where((lane & 2) == 0, pltpu.roll(tile, LANES - 2, 1), pltpu.roll(tile, 2, 1))
        turned.append(jnp.where(pair, moved, tile))
        own[i * SUB : (i + 1) * SUB, :] = turned[i]
    fold = (row_tiles + 2) // 2
    for i in range(fold):
        other = tiles[i + fold]
        to_right = jnp.where(pair, other, pltpu.roll(other, 4, 1))
        to_right = jnp.where(from_left, turned[i], to_right)
        to_left = jnp.where(pair, other, pltpu.roll(other, LANES - 4, 1))
        to_left = jnp.where(from_left, to_left, turned[i])
        near_out[i * SUB : (i + 1) * SUB, :] = jnp.where(col_even, to_right, to_left)
        far_out[i * SUB : (i + 1) * SUB, :] = jnp.where(col_even, to_left, to_right)


def lane_sums(entries, lane):
    step = 1
    while len(entries) > 1:
        low = (lane & step) == 0
        merged = []
        for a, b in zip(entries[::2], entries[1::2]):
            if a is None:
                merged.append(None)
                continue
            b = jnp.zeros_like(a) if b is None else b
            merged.append(jnp.where(low, a, b) + pltpu.roll(jnp.where(low, b, a), step, 1))
        entries = merged
        step *= 2
    return entries[0]


def main_kernel(
    body_total,
    res,
    edge,
    horiz,
    vert,
    edge_coef,
    own,
    col_near,
    col_far,
    table,
    mix,
    modes,
    bodies_t,
    dir_s,
    part_s,
    message,
    res_s,
    img_s,
    horiz_s,
    vert_s,
    scale_s,
    got_s,
    sums_s,
):
    blocks, levels, rows, _ = res.shape
    mode_count = modes.shape[0]
    tiles = blocks + 1
    side = blocks
    row_tiles = rows // SUB
    base = 2 * SUB
    lane = iota((SUB, LANES), 1)
    everything = range(tiles)

    pair, from_left = lane_kinds(lane, levels)
    even = lax.rem(lax.axis_index("gy"), 2) == 0
    fold = (row_tiles + 2) // 2
    for i in range(fold):
        here = pl.ds(i * SUB, SUB)
        near, far = col_near[here, :], col_far[here, :]
        left, right = jnp.where(even, far, near), jnp.where(even, near, far)
        got_s[here, :] = jnp.where(from_left, left, right)
        left = jnp.where(pair, pltpu.roll(left, 2, 1), pltpu.roll(left, LANES - 4, 1))
        right = jnp.where(pair, pltpu.roll(right, LANES - 2, 1), pltpu.roll(right, 4, 1))
        there = pl.ds((i + fold) * SUB, SUB)
        got_s[there, :] = jnp.where(from_left, left, right)

    def first(i, inner, residuals, coefs):
        here = tile_at(i)
        there = tile_at(i + 1)
        got, mine = got_s[here, :], own[here, :]
        halo = (lane < 4) | (lane >= LANES - 4)
        slot = coef_slot(levels)
        side_coef = [
            jnp.where(halo, pltpu.roll(got, (LANES - 4 - slot - 8 * n) % LANES, 1), 0.0) for n in range(2)
        ]
        coefs = list(coefs) + [tuple(side_coef)]
        outer = (lane < 2, lane >= LANES - 2, (lane < 2) | (lane >= LANES - 2))
        scales, edges = [], []
        for t in everything:
            h, v = coefs[t]
            bottom = 5.0 * h + 2.0 * v
            inside = bottom > 0.0
            scale = jnp.where(inside, 1.0 / jnp.where(inside, bottom, 1.0), 0.0)
            scales.append(scale)
            scale_s[t, there, :] = scale
            horiz_s[t, there, :] = h
            vert_s[t, there, :] = v
            if t == side:
                mask = outer[2]
            elif blocks == 1:
                mask = outer[2]
            elif t == 0:
                mask = outer[0]
            elif t == blocks - 1:
                mask = outer[1]
            else:
                mask = None
            edges.append(None if mask is None else jnp.where(mask, h * (1.0 / 12.0), 0.0))
        weighted = [[] for _ in everything]
        for l in range(levels):
            place = (LANES - 2 - 8 * levels - 4 * l) % LANES
            theirs = pltpu.roll(got, place, 1)
            ours = pltpu.roll(mine, place, 1)
            for t in everything:
                if t == side:
                    value = pltpu.roll(got, (LANES - 4 - 8 * l) % LANES, 1) - edges[t] * ours
                else:
                    value = residuals[t][l]
                    if edges[t] is not None:
                        value = value - edges[t] * theirs
                    if inner:
                        res_s[t, l, there, :] = value
                weighted[t].append(value * scales[t])
        for t in everything:
            for l, value in enumerate(mix_levels(mix, weighted[t], levels)):
                dir_s[t, l, there, :] = value

    def own_coefs(i):
        here = tile_at(i)
        result = []
        for t in range(blocks):
            lanes = pl.ds(t * LANES, LANES)
            result.append((horiz[here, lanes], vert[here, lanes]))
        return result

    for n, i in enumerate((0, 1, row_tiles, row_tiles + 1)):
        residuals = [[edge[n, t, l] for l in range(levels)] for t in range(blocks)]
        if 1 <= i <= row_tiles:
            coefs = own_coefs(i - 1)
        else:
            coefs = [(edge_coef[n // 2, 0, t], edge_coef[n // 2, 1, t]) for t in range(blocks)]
        first(i, 1 <= i <= row_tiles, residuals, coefs)

    def first_body(i, carry):
        here = tile_at(i - 1)
        residuals = [[res[t, l, here, :] for l in range(levels)] for t in range(blocks)]
        first(i, True, residuals, own_coefs(i - 1))
        return carry

    lax.fori_loop(2, row_tiles, first_body, 0, unroll=7)

    def coefs_at(row, count):
        here = pl.ds(row, SUB)
        return [(horiz_s[t, here, :], vert_s[t, here, :]) for t in range(count)]

    def second(i, carry):
        row = pl.multiple_of(i * SUB + SUB, SUB)
        here = pl.ds(row, SUB)
        image = stencil(
            dir_s, row, everything, tiles, levels, coefs_at(row, tiles), lane, True
        )
        for t, image_t in image:
            scale = scale_s[t, here, :]
            weighted = []
            for l in range(levels):
                img_s[t, l, here, :] = image_t[l]
                weighted.append(image_t[l] * scale)
            for l, value in enumerate(mix_levels(mix, weighted, levels)):
                part_s[t, l, here, :] = value
        return carry

    lax.fori_loop(0, row_tiles + 2, second, 0, unroll=3)

    for i in range(row_tiles):
        row = pl.ds(base + i * SUB, SUB)
        here = pl.ds(i * SUB, SUB)
        entries = [None] * (LANES // 4)
        for t in range(blocks):
            lanes = pl.ds(t * LANES, LANES)
            for q, field in enumerate((dir_s, part_s)):
                surface = field[t, 0, row, :]
                for k in range(mode_count):
                    entries[(2 * t + q) * SUB + k] = modes[k, here, lanes] * surface
        sums_s[here, :] = lane_sums(entries, lane)

    def third(i, totals):
        row = pl.multiple_of(i * SUB + base, SUB)
        here = pl.ds(row, SUB)
        image = stencil(
            part_s, row, range(blocks), tiles, levels, coefs_at(row, blocks), lane, True
        )
        totals = list(totals)
        for t, image_t in image:
            for l in range(levels):
                residual = res_s[t, l, here, :]
                img1 = img_s[t, l, here, :]
                img2 = image_t[l]
                products = (residual * img1, img1 * img1, residual * img2, img1 * img2, img2 * img2)
                totals = [total + product for total, product in zip(totals, products)]
        return tuple(totals)

    zero = jnp.zeros((SUB, LANES), F32)
    totals = lax.fori_loop(0, row_tiles, third, (zero,) * 5, unroll=2)

    width = message.shape[1]
    sums_t = sums_s[...].T
    sums_t = sum(sums_t[n * (LANES // 4) : (n + 1) * (LANES // 4), :] for n in range(4))
    forces = jnp.zeros((SUB, width), F32)
    for t in range(blocks):
        hits = body_hits(bodies_t, t, body_total, width)
        first_sums = sums_t[2 * t * SUB : (2 * t + 1) * SUB, :]
        second_sums = sums_t[(2 * t + 1) * SUB : (2 * t + 2) * SUB, :]
        forces = forces + dot_nt(first_sums, hits)
        forces = forces + pltpu.roll(dot_nt(second_sums, hits), body_total, 1)
    wide_sub = iota((SUB, width), 0)
    gathered = jnp.zeros((SUB, LANES), F32)
    for q, total in enumerate(totals):
        gathered = jnp.where(lane == q, jnp.sum(total, axis=1, keepdims=True), gathered)
    gathered = jnp.sum(gathered, axis=0, keepdims=True)
    if width > LANES:
        gathered = jnp.concatenate([gathered, jnp.zeros((1, width - LANES), F32)], axis=1)
    message[0:SUB, :] = jnp.where(wide_sub == SUB - 2, gathered, forces)
    message[SUB:, :] = table[...]


def mix_levels(mix, weighted, levels):
    out = []
    for l in range(levels):
        total = (mix[l, l] + 1.0) * weighted[l]
        for m in range(levels):
            if m != l:
                total = total + mix[l, m] * weighted[m]
        out.append(total)
    return out


def body_hits(bodies_t, block, count, width):
    ids = bodies_t[block : block + 1, :]
    ids = jnp.where(ids < count, ids, -1)
    wanted = lax.broadcasted_iota(jnp.int32, (width, ids.shape[1]), 0)
    return (jnp.broadcast_to(ids, wanted.shape) == wanted).astype(F32)


def dot_nt(a, b):
    return lax.dot_general(
        a, b, (((1,), (1,)), ((), ())), precision=lax.Precision.HIGHEST, preferred_element_type=F32
    )


def last_kernel(
    body_total,
    message,
    phi,
    direction,
    part,
    modes,
    bodies_t,
    potential,
    velocity_t,
    flux,
    phi_s,
    flux_s,
    out_sems,
):
    levels, rows, cols = phi.shape
    mode_count = modes.shape[0]
    blocks = cols // LANES
    width = message.shape[1]
    owned = velocity_t.shape[0]
    main = pl.ds(2 * SUB, rows)
    top = message[0:SUB, :]

    def scalar(q):
        return top[SUB - 2 : SUB - 1, q : q + 1]

    cross_first, square_first, cross_mixed, square_mixed, square_second = [
        scalar(q) for q in range(5)
    ]
    first_step = cross_first / square_first
    next_top = (
        cross_first
        - first_step * cross_mixed
        - first_step * square_first
        + first_step * first_step * square_mixed
    )
    next_bottom = (
        square_first - 2.0 * first_step * square_mixed + first_step * first_step * square_second
    )
    second_step = next_top / next_bottom
    on_dir = first_step + second_step
    on_part = first_step * second_step

    outgoing = []
    for l in range(levels):
        for t in range(blocks):
            lanes = pl.ds(t * LANES, LANES)
            change = on_dir * direction[t, l, main, :] - on_part * part[t, l, main, :]
            phi_s[l, :, lanes] = phi[l, :, lanes] + change
        copy = pltpu.make_async_copy(phi_s.at[l], potential.at[l], out_sems.at[l])
        copy.start()
        outgoing.append(copy)

    wide_sub = lax.broadcasted_iota(jnp.int32, (SUB, width), 0)
    wide_lane = lax.broadcasted_iota(jnp.int32, (SUB, width), 1)
    foot_scale = 1.0 / math.sqrt(FOOT)
    forces = foot_scale * (on_part * pltpu.roll(top, body_total, 1) - on_dir * top)
    forces = jnp.where(wide_sub == mode_count, 1.0, forces)
    forces = jnp.where(wide_lane < body_total, forces, 0.0)
    velocity = jnp.zeros((SUB, width), F32)
    for k in range(mode_count):
        table = message[(k // 2 + 1) * SUB : (k // 2 + 2) * SUB, :]
        if k % 2:
            table = pltpu.roll(table, body_total, 1)
        value = jnp.sum(table * forces, axis=0, keepdims=True)
        velocity = jnp.where(wide_sub == k, value, velocity)

    me = (lax.axis_index("gx") * lax.axis_size("gy") + lax.axis_index("gy")) * owned
    mine = ((wide_lane == me + wide_sub) & (wide_sub < owned)).astype(F32)
    velocity_t[...] = dot_nt(mine, velocity)[0:owned, 0:mode_count]

    per_row = []
    for t in range(blocks):
        hits = body_hits(bodies_t, t, body_total, width)
        per_row.append(
            lax.dot_general(
                velocity,
                hits,
                (((1,), (0,)), ((), ())),
                precision=lax.Precision.HIGHEST,
                preferred_element_type=F32,
            )
        )
    per_row.append(jnp.zeros((LANES - blocks * SUB, rows), F32))
    spread = jnp.concatenate(per_row, axis=0).T

    for t in range(blocks):
        lanes = pl.ds(t * LANES, LANES)
        total = jnp.zeros((rows, LANES), F32)
        for k in range(mode_count):
            total = total + modes[k, :, lanes] * spread[:, t * SUB + k : t * SUB + k + 1]
        flux_s[:, lanes] = total
    flux_copy = pltpu.make_async_copy(flux_s, flux, out_sems.at[levels])
    flux_copy.start()
    outgoing.append(flux_copy)
    for copy in outgoing:
        copy.wait()


def swap_near(value, axis):
    size = lax.axis_size(axis)
    return lax.ppermute(value, axis, [(i, i ^ 1) for i in range(size)])


def swap_far(value, axis):
    size = lax.axis_size(axis)
    pairs = [(i, i + 1) for i in range(1, size - 1, 2)]
    return lax.ppermute(value, axis, pairs + [(j, i) for i, j in pairs])


def sum_over(value, axes):
    for axis in axes:
        size = lax.axis_size(axis)
        step = 1
        while step < size:
            value = value + lax.ppermute(value, axis, [(i, i ^ step) for i in range(size)])
            step *= 2
    return value


def per_device(
    forcing,
    start_potential,
    horiz_coef,
    vert_coef,
    vert_mix,
    mode_shapes,
    block_body,
    response,
    velocity_old,
):
    levels, rows, cols = forcing.shape
    mode_count = mode_shapes.shape[0]
    blocks = cols // LANES
    tiles = blocks + 1
    padded = rows + 4 * SUB
    owned = velocity_old.shape[1]
    body_total = owned * lax.axis_size(("gx", "gy"))
    width = 2 * body_total
    bodies_t = block_body.T
    response_t = jnp.swapaxes(response, 1, 2)
    old_t = velocity_old.T
    limit = pltpu.CompilerParams(vmem_limit_bytes=24 * 2**20)

    def call(kernel, name, outs, ins, args, scratch=()):
        return pl.pallas_call(
            kernel,
            out_shape=tuple(jax.ShapeDtypeStruct(shape, F32) for shape, _ in outs),
            in_specs=ins,
            out_specs=tuple(spec for _, spec in outs),
            scratch_shapes=list(scratch),
            compiler_params=limit,
            name=name,
        )(*args)

    strip = (levels + 1, SUB, cols)
    inner = (blocks, levels, rows, LANES)
    near, far = call(
        strip_kernel,
        "strip_kernel",
        [(strip, VMEM), (strip, VMEM)],
        [HBM] * 4,
        [
            pltpu.with_memory_space_constraint(value, pltpu.HBM)
            for value in (start_potential, forcing, horiz_coef, vert_coef)
        ],
        [
            pltpu.VMEM((2, blocks, levels, 3 * SUB, LANES), F32),
            pltpu.VMEM((2, blocks, levels, SUB, LANES), F32),
            pltpu.VMEM((2, SUB, cols), F32),
            pltpu.VMEM((2, SUB, cols), F32),
            pltpu.SemaphoreType.DMA((4 + 4 * blocks,)),
        ],
    )
    row_near, row_far = swap_near(near, "gx"), swap_far(far, "gx")
    packed_shape = (rows + 2 * SUB, LANES)
    res, packed, table = call(
        functools.partial(inner_kernel, body_total),
        "inner_kernel",
        [(inner, VMEM), (packed_shape, VMEM), ((3 * SUB, width), VMEM)],
        [VMEM] * 6,
        (start_potential, forcing, horiz_coef, vert_coef, response_t, old_t),
        [
            pltpu.VMEM((blocks, levels, rows + 2 * SUB, LANES), F32),
            pltpu.VMEM((LANES, LANES), F32),
        ],
    )
    strip = (rows // 2 + SUB, LANES)
    edge, edge_coef, own, near, far = call(
        edge_kernel,
        "edge_kernel",
        [
            ((4, blocks, levels, SUB, LANES), VMEM),
            ((2, 2, blocks, SUB, LANES), VMEM),
            (packed_shape, VMEM),
            (strip, VMEM),
            (strip, VMEM),
        ],
        [VMEM] * 7,
        (res, start_potential, horiz_coef, vert_coef, row_near, row_far, packed),
    )
    col_near, col_far = swap_near(near, "gy"), swap_far(far, "gy")

    field = (tiles, levels, padded, LANES)
    plane = pltpu.VMEM((tiles, padded, LANES), F32)
    direction, part, message = call(
        functools.partial(main_kernel, body_total),
        "main_kernel",
        [(field, VMEM), (field, VMEM), ((4 * SUB, width), VMEM)],
        [VMEM] * 9 + [SMEM] + [VMEM] * 2,
        (
            res,
            edge,
            horiz_coef,
            vert_coef,
            edge_coef,
            own,
            col_near,
            col_far,
            table,
            vert_mix,
            mode_shapes,
            bodies_t,
        ),
        [
            pltpu.VMEM((blocks, levels, padded, LANES), F32),
            pltpu.VMEM(field, F32),
            plane,
            plane,
            plane,
            pltpu.VMEM(packed_shape, F32),
            pltpu.VMEM((rows, LANES), F32),
        ],
    )
    message = sum_over(message, ("gx", "gy"))

    potential, velocity_t, flux = call(
        functools.partial(last_kernel, body_total),
        "last_kernel",
        [((levels, rows, cols), HBM), ((owned, mode_count), VMEM), ((rows, cols), HBM)],
        [VMEM] * 6,
        (message, start_potential, direction, part, mode_shapes, bodies_t),
        [
            pltpu.VMEM((levels, rows, cols), F32),
            pltpu.VMEM((rows, cols), F32),
            pltpu.SemaphoreType.DMA((levels + 1,)),
        ],
    )
    return (potential, velocity_t.T, flux)


def solution(mesh):
    return jax.shard_map(
        per_device,
        mesh=mesh,
        in_specs=(
            P(None, "gx", "gy"),
            P(None, "gx", "gy"),
            P("gx", "gy"),
            P("gx", "gy"),
            P(),
            P(None, "gx", "gy"),
            P("gx", "gy"),
            P(None, None, ("gx", "gy")),
            P(None, ("gx", "gy")),
        ),
        out_specs=(P(None, "gx", "gy"), P(None, ("gx", "gy")), P("gx", "gy")),
        check_vma=False,
    )
```

```python
import functools
import math

import jax
import jax.numpy as jnp
from jax import lax
from jax.experimental import pallas as pl
from jax.experimental.pallas import tpu as pltpu
from jax.sharding import PartitionSpec as P

FOOT = 8192
LANES = 128
SUB = 8
FAR = 16.0
F32 = jnp.float32
HBM = pl.BlockSpec(memory_space=pltpu.HBM)
VMEM = pl.BlockSpec(memory_space=pltpu.VMEM)
SMEM = pl.BlockSpec(memory_space=pltpu.SMEM)


def iota(shape, dim):
    return lax.broadcasted_iota(jnp.int32, shape, dim)


def tile_at(index):
    return pl.ds(pl.multiple_of(index * SUB, SUB), SUB)


def stencil(ref, row, wanted, tiles, levels, coefs, lane, wrap):
    for t in wanted:
        center = {
            u: [ref[u % tiles, l, pl.ds(row, SUB), :] for l in range(levels)]
            for u in (t - 1, t, t + 1)
        }
        horiz, vert = coefs[t]
        last_coef = 5.0 * horiz + vert
        mid_coef = last_coef + vert
        horiz12 = horiz * (1.0 / 12.0)
        per_level = []
        for l in range(levels):
            x = center[t][l]
            after = center[t + 1][l] if wrap or t + 1 < tiles else 0.0
            before = center[t - 1][l] if wrap or t > 0 else 0.0

            def rows_at(offset):
                return ref[t, l, pl.ds(row + offset, SUB), :]

            right1 = pltpu.roll(jnp.where(lane < 1, after, x), LANES - 1, 1)
            right2 = pltpu.roll(jnp.where(lane < 2, after, x), LANES - 2, 1)
            left1 = pltpu.roll(jnp.where(lane >= LANES - 1, before, x), 1, 1)
            left2 = pltpu.roll(jnp.where(lane >= LANES - 2, before, x), 2, 1)
            nearest = (rows_at(-1) + rows_at(1)) + (right1 + left1)
            farther = (rows_at(-2) + rows_at(2)) + (right2 + left2)
            if l == 0:
                beside = center[t][1]
            elif l == levels - 1:
                beside = center[t][l - 1]
            else:
                beside = center[t][l - 1] + center[t][l + 1]
            coef = last_coef if l == levels - 1 else mid_coef
            per_level.append(coef * x + horiz12 * (farther - FAR * nearest) - vert * beside)
        yield t, per_level


def strip_kernel(phi, forcing, horiz_in, vert_in, near_out, far_out, phi_s, res_s, horiz, vert, sems):
    levels, rows, cols = phi.shape
    blocks = cols // LANES
    lane, sub = iota((SUB, LANES), 1), iota((SUB, LANES), 0)
    pairs = []
    for end, row in enumerate((0, rows - SUB)):
        here = pl.ds(row, SUB)
        pairs.append((horiz_in.at[here], horiz.at[end]))
        pairs.append((vert_in.at[here], vert.at[end]))
        for t in range(blocks):
            lanes = pl.ds(t * LANES, LANES)
            pairs.append((phi.at[:, here, lanes], phi_s.at[end, t, :, pl.ds(SUB, SUB)]))
            pairs.append((forcing.at[:, here, lanes], res_s.at[end, t]))
    copies = [pltpu.make_async_copy(a, b, sems.at[n]) for n, (a, b) in enumerate(pairs)]
    for copy in copies:
        copy.start()
    zero = jnp.zeros((SUB, LANES), F32)
    for end in range(2):
        for t in range(blocks):
            for l in range(levels):
                phi_s[end, t, l, 0:SUB, :] = zero
                phi_s[end, t, l, 2 * SUB : 3 * SUB, :] = zero
    for copy in copies:
        copy.wait()
    even = lax.rem(lax.axis_index("gx"), 2) == 0
    upper = sub < SUB // 2
    kept = []
    for end in range(2):
        coefs = [
            (horiz[end, :, t * LANES : (t + 1) * LANES], vert[end, :, t * LANES : (t + 1) * LANES])
            for t in range(blocks)
        ]
        image = stencil(phi_s.at[end], SUB, range(blocks), blocks, levels, coefs, lane, False)
        strips = {}
        for t, image_t in image:
            for l in range(levels):
                potential = phi_s[end, t, l, SUB : 2 * SUB, :]
                strips[t, l] = (res_s[end, t, l] - image_t[l], potential)
            strips[t, levels] = coefs[t]
        kept.append(strips)
    for place, (a_top, b_top) in kept[0].items():
        a_low, b_low = kept[1][place]
        t, l = place
        lanes = pl.ds(t * LANES, LANES)
        top = jnp.where(upper, a_top, pltpu.roll(b_top, SUB // 2, 0))
        low = jnp.where(upper, pltpu.roll(b_low, SUB // 2, 0), a_low)
        near_out[l, :, lanes] = jnp.where(even, low, top)
        far_out[l, :, lanes] = jnp.where(even, top, low)


def lane_kinds(lane, levels):
    pair = (lane >= 8 * levels) & (lane < 12 * levels)
    from_left = jnp.where(pair, lane & 2, 4 - (lane & 4)) != 0
    return pair, from_left


def coef_slot(levels):
    return (12 * levels + 7) // 8 * 8


def pack_tile(res, phi, coefs, lane):
    levels = len(res)
    packed = jnp.zeros((SUB, LANES), F32)
    slots = [(8 * l, 8, value) for l, value in enumerate(res)]
    slots += [(coef_slot(levels) + 8 * n, 8, value) for n, value in enumerate(coefs)]
    slots += [(8 * levels + 4 * l, 4, value) for l, value in enumerate(phi)]
    for low, size, value in slots:
        here = (lane >= low) & (lane < low + size)
        packed = jnp.where(here, pltpu.roll(value, low + size // 2, 1), packed)
    pair = (lane >= 8 * levels) & (lane < 12 * levels)
    after = jnp.where(pair & ((lane & 3) == 0), pltpu.roll(packed, LANES - 1, 1), 0.0)
    before = jnp.where(pair & ((lane & 3) == 3), pltpu.roll(packed, 1, 1), 0.0)
    return packed - FAR * (after + before)


def inner_kernel(
    body_total, phi, forcing, horiz, vert, response_t, old_t, res, packed, table, phi_s, small_s
):
    blocks, levels, rows, _ = res.shape
    cols = phi.shape[2]
    zero = jnp.zeros((SUB, LANES), F32)
    for t in range(blocks):
        for l in range(levels):
            phi_s[t, l, 0:SUB, :] = zero
            phi_s[t, l, rows + SUB : rows + 2 * SUB, :] = zero
            phi_s[t, l, SUB : rows + SUB, :] = phi[l, :, t * LANES : (t + 1) * LANES]
    right = pl.ds(cols - LANES, LANES)
    left = pl.ds(0, LANES)
    lane = iota((SUB, LANES), 1)
    first = lane < LANES // 2

    def residual(i, carry):
        here = tile_at(i)
        row = pl.multiple_of(i * SUB + SUB, SUB)
        coefs = []
        for t in range(blocks):
            lanes = pl.ds(t * LANES, LANES)
            coefs.append((horiz[here, lanes], vert[here, lanes]))
        image = stencil(phi_s, row, range(blocks), blocks, levels, coefs, lane, False)
        for t, image_t in image:
            for l in range(levels):
                own = forcing[l, here, pl.ds(t * LANES, LANES)]
                res[t, l, here, :] = own - image_t[l]
        return carry

    lax.fori_loop(0, rows // SUB, residual, 0, unroll=2)

    def body(i, carry):
        here = tile_at(i)
        packed[tile_at(i + 1), :] = pack_tile(
            [jnp.where(first, res[0, l, here, :], res[blocks - 1, l, here, :]) for l in range(levels)],
            [jnp.where(first, phi[l, here, left], phi[l, here, right]) for l in range(levels)],
            [jnp.where(first, ref[here, left], ref[here, right]) for ref in (horiz, vert)],
            lane,
        )
        return carry

    lax.fori_loop(1, rows // SUB - 1, body, 0, unroll=7)

    owned, mode_count = old_t.shape
    width = table.shape[1]
    small_s[...] = jnp.zeros((LANES, LANES), F32)
    for k in range(mode_count):
        small_s[k * SUB : k * SUB + owned, 0:mode_count] = response_t[k]
        small_s[k * SUB : k * SUB + owned, mode_count : mode_count + 1] = old_t[:, k : k + 1]
    values = small_s[...].T[0:SUB, :]
    if width > LANES:
        values = jnp.concatenate([values, jnp.zeros((SUB, width - LANES), F32)], axis=1)
    wide_lane = iota((SUB, width), 1)
    me = (lax.axis_index("gx") * lax.axis_size("gy") + lax.axis_index("gy")) * owned
    for pair in range(mode_count // 2):
        tile = jnp.zeros((SUB, width), F32)
        for half in range(2):
            place = half * body_total + me
            shift = lax.rem(place - (2 * pair + half) * SUB + width, width)
            here = (wide_lane >= place) & (wide_lane < place + owned)
            tile = jnp.where(here, pltpu.roll(values, shift, 1), tile)
        table[pair * SUB : (pair + 1) * SUB, :] = tile


def edge_kernel(
    res, phi, horiz, vert, row_near, row_far, packed, edge, edge_coef, own, near_out, far_out
):
    blocks, levels, rows, _ = res.shape
    row_tiles = rows // SUB
    lane, sub = iota((SUB, LANES), 1), iota((SUB, LANES), 0)
    even = lax.rem(lax.axis_index("gx"), 2) == 0
    upper = sub < SUB // 2
    half = SUB // 2
    values = {}
    for t in range(blocks):
        lanes = pl.ds(t * LANES, LANES)
        near, far = row_near[levels, :, lanes], row_far[levels, :, lanes]
        above, below = jnp.where(even, far, near), jnp.where(even, near, far)
        h_up, v_up = jnp.where(upper, 0.0, above), jnp.where(upper, 0.0, pltpu.roll(above, half, 0))
        h_down = jnp.where(upper, below, 0.0)
        v_down = jnp.where(upper, pltpu.roll(below, half, 0), 0.0)
        edge_coef[0, 0, t], edge_coef[0, 1, t] = h_up, v_up
        edge_coef[1, 0, t], edge_coef[1, 1, t] = h_down, v_down
        first, last = pl.ds(0, SUB), pl.ds(rows - SUB, SUB)
        h_first, h_last = horiz[first, lanes], horiz[last, lanes]
        coefs = [(h_up, v_up), (h_first, vert[first, lanes]), (h_last, vert[last, lanes])]
        coefs.append((h_down, v_down))
        for n, pair in enumerate(coefs):
            values[n, t, "coef"] = pair
        scaled = [h * (1.0 / 12.0) for h, _ in coefs]

        def from_above(value):
            near_row = jnp.where(sub < 1, pltpu.roll(value, 1, 0), 0.0)
            far_row = jnp.where(sub < 2, pltpu.roll(value, 2, 0), 0.0)
            return far_row - FAR * near_row

        def from_below(value):
            near_row = jnp.where(sub >= SUB - 1, pltpu.roll(value, SUB - 1, 0), 0.0)
            far_row = jnp.where(sub >= SUB - 2, pltpu.roll(value, SUB - 2, 0), 0.0)
            return far_row - FAR * near_row

        for l in range(levels):
            near, far = row_near[l, :, lanes], row_far[l, :, lanes]
            above, below = jnp.where(even, far, near), jnp.where(even, near, far)
            res_up = jnp.where(upper, 0.0, above)
            phi_up = jnp.where(upper, 0.0, pltpu.roll(above, half, 0))
            res_down = jnp.where(upper, below, 0.0)
            phi_down = jnp.where(upper, pltpu.roll(below, half, 0), 0.0)
            phi_first, phi_last = phi[l, first, lanes], phi[l, last, lanes]
            fixed = (
                res_up - scaled[0] * from_below(phi_first),
                res[t, l, first, :] - scaled[1] * from_above(phi_up),
                res[t, l, last, :] - scaled[2] * from_below(phi_down),
                res_down - scaled[3] * from_above(phi_last),
            )
            for n, value in enumerate(fixed):
                edge[n, t, l] = value
                values[n, t, l] = value
            for n, value in enumerate((phi_up, phi_first, phi_last, phi_down)):
                values[n, t, l, "phi"] = value

    start = lane < LANES // 2
    end = blocks - 1
    tiles = [packed[i * SUB : (i + 1) * SUB, :] for i in range(row_tiles + 2)]
    for n, place in enumerate((0, 1, row_tiles, row_tiles + 1)):
        tiles[place] = pack_tile(
            [jnp.where(start, values[n, 0, l], values[n, end, l]) for l in range(levels)],
            [
                jnp.where(start, values[n, 0, l, "phi"], values[n, end, l, "phi"])
                for l in range(levels)
            ],
            [jnp.where(start, values[n, 0, "coef"][c], values[n, end, "coef"][c]) for c in range(2)],
            lane,
        )
    pair, from_left = lane_kinds(lane, levels)
    col_even = lax.rem(lax.axis_index("gy"), 2) == 0
    turned = []
    for i, tile in enumerate(tiles):
        moved = jnp.where((lane & 2) == 0, pltpu.roll(tile, LANES - 2, 1), pltpu.roll(tile, 2, 1))
        turned.append(jnp.where(pair, moved, tile))
        own[i * SUB : (i + 1) * SUB, :] = turned[i]
    fold = (row_tiles + 2) // 2
    for i in range(fold):
        other = tiles[i + fold]
        to_right = jnp.where(pair, other, pltpu.roll(other, 4, 1))
        to_right = jnp.where(from_left, turned[i], to_right)
        to_left = jnp.where(pair, other, pltpu.roll(other, LANES - 4, 1))
        to_left = jnp.where(from_left, to_left, turned[i])
        near_out[i * SUB : (i + 1) * SUB, :] = jnp.where(col_even, to_right, to_left)
        far_out[i * SUB : (i + 1) * SUB, :] = jnp.where(col_even, to_left, to_right)


def ahead_kernel(body_total, after, modes, bodies_t, modes_t, hits):
    mode_count = modes.shape[0]
    for t in range(hits.shape[0]):
        for k in range(mode_count):
            modes_t[t, k] = modes[k, :, t * LANES : (t + 1) * LANES].T
        hits[t] = body_hits(bodies_t, t, body_total, hits.shape[1])


def main_kernel(
    body_total,
    res,
    edge,
    horiz,
    vert,
    edge_coef,
    own,
    col_near,
    col_far,
    table,
    mix,
    modes_t,
    hits,
    dir_s,
    part_s,
    message,
    res_s,
    img_s,
    horiz_s,
    vert_s,
    scale_s,
    got_s,
):
    blocks, levels, rows, _ = res.shape
    mode_count = modes_t.shape[1]
    tiles = blocks + 1
    side = blocks
    row_tiles = rows // SUB
    base = 2 * SUB
    lane = iota((SUB, LANES), 1)
    everything = range(tiles)

    pair, from_left = lane_kinds(lane, levels)
    even = lax.rem(lax.axis_index("gy"), 2) == 0
    fold = (row_tiles + 2) // 2
    for i in range(fold):
        here = pl.ds(i * SUB, SUB)
        near, far = col_near[here, :], col_far[here, :]
        left, right = jnp.where(even, far, near), jnp.where(even, near, far)
        got_s[here, :] = jnp.where(from_left, left, right)
        left = jnp.where(pair, pltpu.roll(left, 2, 1), pltpu.roll(left, LANES - 4, 1))
        right = jnp.where(pair, pltpu.roll(right, LANES - 2, 1), pltpu.roll(right, 4, 1))
        there = pl.ds((i + fold) * SUB, SUB)
        got_s[there, :] = jnp.where(from_left, left, right)

    def first(i, inner, residuals, coefs):
        here = tile_at(i)
        there = tile_at(i + 1)
        got, mine = got_s[here, :], own[here, :]
        halo = (lane < 4) | (lane >= LANES - 4)
        slot = coef_slot(levels)
        side_coef = [
            jnp.where(halo, pltpu.roll(got, (LANES - 4 - slot - 8 * n) % LANES, 1), 0.0) for n in range(2)
        ]
        coefs = list(coefs) + [tuple(side_coef)]
        outer = (lane < 2, lane >= LANES - 2, (lane < 2) | (lane >= LANES - 2))
        scales, edges = [], []
        for t in everything:
            h, v = coefs[t]
            bottom = 5.0 * h + 2.0 * v
            inside = bottom > 0.0
            scale = jnp.where(inside, 1.0 / jnp.where(inside, bottom, 1.0), 0.0)
            scales.append(scale)
            scale_s[t, there, :] = scale
            horiz_s[t, there, :] = h
            vert_s[t, there, :] = v
            if t == side:
                mask = outer[2]
            elif blocks == 1:
                mask = outer[2]
            elif t == 0:
                mask = outer[0]
            elif t == blocks - 1:
                mask = outer[1]
            else:
                mask = None
            edges.append(None if mask is None else jnp.where(mask, h * (1.0 / 12.0), 0.0))
        weighted = [[] for _ in everything]
        for l in range(levels):
            place = (LANES - 2 - 8 * levels - 4 * l) % LANES
            theirs = pltpu.roll(got, place, 1)
            ours = pltpu.roll(mine, place, 1)
            for t in everything:
                if t == side:
                    value = pltpu.roll(got, (LANES - 4 - 8 * l) % LANES, 1) - edges[t] * ours
                else:
                    value = residuals[t][l]
                    if edges[t] is not None:
                        value = value - edges[t] * theirs
                    if inner:
                        res_s[t, l, there, :] = value
                weighted[t].append(value * scales[t])
        for t in everything:
            for l, value in enumerate(mix_levels(mix, weighted[t], levels)):
                dir_s[t, l, there, :] = value

    def own_coefs(i):
        here = tile_at(i)
        result = []
        for t in range(blocks):
            lanes = pl.ds(t * LANES, LANES)
            result.append((horiz[here, lanes], vert[here, lanes]))
        return result

    for n, i in enumerate((0, 1, row_tiles, row_tiles + 1)):
        residuals = [[edge[n, t, l] for l in range(levels)] for t in range(blocks)]
        if 1 <= i <= row_tiles:
            coefs = own_coefs(i - 1)
        else:
            coefs = [(edge_coef[n // 2, 0, t], edge_coef[n // 2, 1, t]) for t in range(blocks)]
        first(i, 1 <= i <= row_tiles, residuals, coefs)

    def first_body(i, carry):
        here = tile_at(i - 1)
        residuals = [[res[t, l, here, :] for l in range(levels)] for t in range(blocks)]
        first(i, True, residuals, own_coefs(i - 1))
        return carry

    lax.fori_loop(2, row_tiles, first_body, 0, unroll=7)

    def coefs_at(row, count):
        here = pl.ds(row, SUB)
        return [(horiz_s[t, here, :], vert_s[t, here, :]) for t in range(count)]

    def second(i, carry):
        row = pl.multiple_of(i * SUB + SUB, SUB)
        here = pl.ds(row, SUB)
        image = stencil(
            dir_s, row, everything, tiles, levels, coefs_at(row, tiles), lane, True
        )
        for t, image_t in image:
            scale = scale_s[t, here, :]
            weighted = []
            for l in range(levels):
                img_s[t, l, here, :] = image_t[l]
                weighted.append(image_t[l] * scale)
            for l, value in enumerate(mix_levels(mix, weighted, levels)):
                part_s[t, l, here, :] = value
        return carry

    def third(i, totals):
        row = pl.multiple_of(i * SUB + SUB, SUB)
        here = pl.ds(row, SUB)
        image = stencil(
            part_s, row, range(blocks), tiles, levels, coefs_at(row, blocks), lane, True
        )
        totals = list(totals)
        for t, image_t in image:
            for l in range(levels):
                residual = res_s[t, l, here, :]
                img1 = img_s[t, l, here, :]
                img2 = image_t[l]
                products = (residual * img1, img1 * img1, residual * img2, img1 * img2, img2 * img2)
                totals = [total + product for total, product in zip(totals, products)]
        return tuple(totals)

    zero = jnp.zeros((SUB, LANES), F32)
    lax.fori_loop(0, row_tiles + 2, second, 0, unroll=3)
    totals = lax.fori_loop(1, row_tiles + 1, third, (zero,) * 5, unroll=4)

    width = message.shape[1]
    surface_rows = pl.ds(base, rows)
    forces = jnp.zeros((SUB, width), F32)
    for t in range(blocks):
        for q, field in enumerate((dir_s, part_s)):
            surface = field[t, 0, surface_rows, :].T
            sums = [
                jnp.sum(modes_t[t, k] * surface, axis=0, keepdims=True) for k in range(mode_count)
            ]
            sums.append(jnp.zeros((SUB - mode_count, rows), F32))
            share = dot_nt(jnp.concatenate(sums, axis=0), hits[t])
            forces = forces + (pltpu.roll(share, body_total, 1) if q else share)
    wide_sub = iota((SUB, width), 0)
    gathered = jnp.zeros((SUB, LANES), F32)
    for q, total in enumerate(totals):
        gathered = jnp.where(lane == q, jnp.sum(total, axis=1, keepdims=True), gathered)
    gathered = jnp.sum(gathered, axis=0, keepdims=True)
    if width > LANES:
        gathered = jnp.concatenate([gathered, jnp.zeros((1, width - LANES), F32)], axis=1)
    message[0:SUB, :] = jnp.where(wide_sub == SUB - 2, gathered, forces)
    message[SUB:, :] = table[...]


def mix_levels(mix, weighted, levels):
    out = []
    for l in range(levels):
        total = (mix[l, l] + 1.0) * weighted[l]
        for m in range(levels):
            if m != l:
                total = total + mix[l, m] * weighted[m]
        out.append(total)
    return out


def body_hits(bodies_t, block, count, width):
    ids = bodies_t[block : block + 1, :]
    ids = jnp.where(ids < count, ids, -1)
    wanted = lax.broadcasted_iota(jnp.int32, (width, ids.shape[1]), 0)
    return (jnp.broadcast_to(ids, wanted.shape) == wanted).astype(F32)


def dot_nt(a, b):
    return lax.dot_general(
        a, b, (((1,), (1,)), ((), ())), precision=lax.Precision.HIGHEST, preferred_element_type=F32
    )


def last_kernel(
    body_total,
    message,
    phi,
    direction,
    part,
    modes,
    bodies_t,
    potential,
    velocity_t,
    flux,
    phi_s,
    flux_s,
    out_sems,
):
    levels, rows, cols = phi.shape
    mode_count = modes.shape[0]
    blocks = cols // LANES
    width = message.shape[1]
    owned = velocity_t.shape[0]
    main = pl.ds(2 * SUB, rows)
    top = message[0:SUB, :]

    def scalar(q):
        return top[SUB - 2 : SUB - 1, q : q + 1]

    cross_first, square_first, cross_mixed, square_mixed, square_second = [
        scalar(q) for q in range(5)
    ]
    first_step = cross_first / square_first
    next_top = (
        cross_first
        - first_step * cross_mixed
        - first_step * square_first
        + first_step * first_step * square_mixed
    )
    next_bottom = (
        square_first - 2.0 * first_step * square_mixed + first_step * first_step * square_second
    )
    second_step = next_top / next_bottom
    on_dir = first_step + second_step
    on_part = first_step * second_step

    outgoing = []
    for l in range(levels):
        for t in range(blocks):
            lanes = pl.ds(t * LANES, LANES)
            change = on_dir * direction[t, l, main, :] - on_part * part[t, l, main, :]
            phi_s[l, :, lanes] = phi[l, :, lanes] + change
        copy = pltpu.make_async_copy(phi_s.at[l], potential.at[l], out_sems.at[l])
        copy.start()
        outgoing.append(copy)

    wide_sub = lax.broadcasted_iota(jnp.int32, (SUB, width), 0)
    wide_lane = lax.broadcasted_iota(jnp.int32, (SUB, width), 1)
    foot_scale = 1.0 / math.sqrt(FOOT)
    forces = foot_scale * (on_part * pltpu.roll(top, body_total, 1) - on_dir * top)
    forces = jnp.where(wide_sub == mode_count, 1.0, forces)
    forces = jnp.where(wide_lane < body_total, forces, 0.0)
    velocity = jnp.zeros((SUB, width), F32)
    for k in range(mode_count):
        table = message[(k // 2 + 1) * SUB : (k // 2 + 2) * SUB, :]
        if k % 2:
            table = pltpu.roll(table, body_total, 1)
        value = jnp.sum(table * forces, axis=0, keepdims=True)
        velocity = jnp.where(wide_sub == k, value, velocity)

    me = (lax.axis_index("gx") * lax.axis_size("gy") + lax.axis_index("gy")) * owned
    mine = ((wide_lane == me + wide_sub) & (wide_sub < owned)).astype(F32)
    velocity_t[...] = dot_nt(mine, velocity)[0:owned, 0:mode_count]

    per_row = []
    for t in range(blocks):
        hits = body_hits(bodies_t, t, body_total, width)
        per_row.append(
            lax.dot_general(
                velocity,
                hits,
                (((1,), (0,)), ((), ())),
                precision=lax.Precision.HIGHEST,
                preferred_element_type=F32,
            )
        )
    per_row.append(jnp.zeros((LANES - blocks * SUB, rows), F32))
    spread = jnp.concatenate(per_row, axis=0).T

    for t in range(blocks):
        lanes = pl.ds(t * LANES, LANES)
        total = jnp.zeros((rows, LANES), F32)
        for k in range(mode_count):
            total = total + modes[k, :, lanes] * spread[:, t * SUB + k : t * SUB + k + 1]
        flux_s[:, lanes] = total
    flux_copy = pltpu.make_async_copy(flux_s, flux, out_sems.at[levels])
    flux_copy.start()
    outgoing.append(flux_copy)
    for copy in outgoing:
        copy.wait()


def swap_near(value, axis):
    size = lax.axis_size(axis)
    return lax.ppermute(value, axis, [(i, i ^ 1) for i in range(size)])


def swap_far(value, axis):
    size = lax.axis_size(axis)
    pairs = [(i, i + 1) for i in range(1, size - 1, 2)]
    return lax.ppermute(value, axis, pairs + [(j, i) for i, j in pairs])


def sum_over(value, axis, together):
    size = lax.axis_size(axis)
    step = 1
    while step < size:
        count = min(together, size // step)
        total = value
        for n in range(1, count):
            pairs = [(i, i ^ (n * step)) for i in range(size)]
            total = total + lax.ppermute(value, axis, pairs)
        value = total
        step *= count
    return value


def per_device(
    forcing,
    start_potential,
    horiz_coef,
    vert_coef,
    vert_mix,
    mode_shapes,
    block_body,
    response,
    velocity_old,
):
    levels, rows, cols = forcing.shape
    mode_count = mode_shapes.shape[0]
    blocks = cols // LANES
    tiles = blocks + 1
    padded = rows + 4 * SUB
    owned = velocity_old.shape[1]
    body_total = owned * lax.axis_size(("gx", "gy"))
    width = 2 * body_total
    bodies_t = block_body.T
    response_t = jnp.swapaxes(response, 1, 2)
    old_t = velocity_old.T
    limit = pltpu.CompilerParams(vmem_limit_bytes=24 * 2**20)

    def call(kernel, name, outs, ins, args, scratch=()):
        return pl.pallas_call(
            kernel,
            out_shape=tuple(jax.ShapeDtypeStruct(shape, F32) for shape, _ in outs),
            in_specs=ins,
            out_specs=tuple(spec for _, spec in outs),
            scratch_shapes=list(scratch),
            compiler_params=limit,
            name=name,
        )(*args)

    strip = (levels + 1, SUB, cols)
    inner = (blocks, levels, rows, LANES)
    near, far = call(
        strip_kernel,
        "strip_kernel",
        [(strip, VMEM), (strip, VMEM)],
        [HBM] * 4,
        [
            pltpu.with_memory_space_constraint(value, pltpu.HBM)
            for value in (start_potential, forcing, horiz_coef, vert_coef)
        ],
        [
            pltpu.VMEM((2, blocks, levels, 3 * SUB, LANES), F32),
            pltpu.VMEM((2, blocks, levels, SUB, LANES), F32),
            pltpu.VMEM((2, SUB, cols), F32),
            pltpu.VMEM((2, SUB, cols), F32),
            pltpu.SemaphoreType.DMA((4 + 4 * blocks,)),
        ],
    )
    row_near, row_far = swap_near(near, "gx"), swap_far(far, "gx")
    packed_shape = (rows + 2 * SUB, LANES)
    res, packed, table = call(
        functools.partial(inner_kernel, body_total),
        "inner_kernel",
        [(inner, VMEM), (packed_shape, VMEM), ((3 * SUB, width), VMEM)],
        [VMEM] * 6,
        (start_potential, forcing, horiz_coef, vert_coef, response_t, old_t),
        [
            pltpu.VMEM((blocks, levels, rows + 2 * SUB, LANES), F32),
            pltpu.VMEM((LANES, LANES), F32),
        ],
    )
    strip = (rows // 2 + SUB, LANES)
    edge, edge_coef, own, near, far = call(
        edge_kernel,
        "edge_kernel",
        [
            ((4, blocks, levels, SUB, LANES), VMEM),
            ((2, 2, blocks, SUB, LANES), VMEM),
            (packed_shape, VMEM),
            (strip, VMEM),
            (strip, VMEM),
        ],
        [VMEM] * 7,
        (res, start_potential, horiz_coef, vert_coef, row_near, row_far, packed),
    )
    col_near, col_far = swap_near(near, "gy"), swap_far(far, "gy")
    modes_t, hits = call(
        functools.partial(ahead_kernel, body_total),
        "ahead_kernel",
        [((blocks, mode_count, LANES, rows), VMEM), ((blocks, width, rows), VMEM)],
        [VMEM] * 3,
        (edge_coef, mode_shapes, bodies_t),
    )

    field = (tiles, levels, padded, LANES)
    plane = pltpu.VMEM((tiles, padded, LANES), F32)
    direction, part, message = call(
        functools.partial(main_kernel, body_total),
        "main_kernel",
        [(field, VMEM), (field, VMEM), ((4 * SUB, width), VMEM)],
        [VMEM] * 9 + [SMEM] + [VMEM] * 2,
        (
            res,
            edge,
            horiz_coef,
            vert_coef,
            edge_coef,
            own,
            col_near,
            col_far,
            table,
            vert_mix,
            modes_t,
            hits,
        ),
        [
            pltpu.VMEM((blocks, levels, padded, LANES), F32),
            pltpu.VMEM(field, F32),
            plane,
            plane,
            plane,
            pltpu.VMEM(packed_shape, F32),
        ],
    )
    message = sum_over(sum_over(message, "gx", 2), "gy", 4)

    potential, velocity_t, flux = call(
        functools.partial(last_kernel, body_total),
        "last_kernel",
        [((levels, rows, cols), HBM), ((owned, mode_count), VMEM), ((rows, cols), HBM)],
        [VMEM] * 6,
        (message, start_potential, direction, part, mode_shapes, bodies_t),
        [
            pltpu.VMEM((levels, rows, cols), F32),
            pltpu.VMEM((rows, cols), F32),
            pltpu.SemaphoreType.DMA((levels + 1,)),
        ],
    )
    return (potential, velocity_t.T, flux)


def solution(mesh):
    return jax.shard_map(
        per_device,
        mesh=mesh,
        in_specs=(
            P(None, "gx", "gy"),
            P(None, "gx", "gy"),
            P("gx", "gy"),
            P("gx", "gy"),
            P(),
            P(None, "gx", "gy"),
            P("gx", "gy"),
            P(None, None, ("gx", "gy")),
            P(None, ("gx", "gy")),
        ),
        out_specs=(P(None, "gx", "gy"), P(None, ("gx", "gy")), P("gx", "gy")),
        check_vma=False,
    )
```

```python
import functools
import math

import jax
import jax.numpy as jnp
from jax import lax
from jax.experimental import pallas as pl
from jax.experimental.pallas import tpu as pltpu
from jax.sharding import PartitionSpec as P

FOOT = 8192
LANES = 128
SUB = 8
FAR = 16.0
F32 = jnp.float32
HBM = pl.BlockSpec(memory_space=pltpu.HBM)
VMEM = pl.BlockSpec(memory_space=pltpu.VMEM)
SMEM = pl.BlockSpec(memory_space=pltpu.SMEM)


def iota(shape, dim):
    return lax.broadcasted_iota(jnp.int32, shape, dim)


def tile_at(index):
    return pl.ds(pl.multiple_of(index * SUB, SUB), SUB)


def stencil(ref, row, wanted, tiles, levels, coefs, lane, wrap):
    for t in wanted:
        center = {
            u: [ref[u % tiles, l, pl.ds(row, SUB), :] for l in range(levels)]
            for u in (t - 1, t, t + 1)
        }
        horiz, vert = coefs[t]
        last_coef = 5.0 * horiz + vert
        mid_coef = last_coef + vert
        horiz12 = horiz * (1.0 / 12.0)
        per_level = []
        for l in range(levels):
            x = center[t][l]
            after = center[t + 1][l] if wrap or t + 1 < tiles else 0.0
            before = center[t - 1][l] if wrap or t > 0 else 0.0

            def rows_at(offset):
                return ref[t, l, pl.ds(row + offset, SUB), :]

            right1 = pltpu.roll(jnp.where(lane < 1, after, x), LANES - 1, 1)
            right2 = pltpu.roll(jnp.where(lane < 2, after, x), LANES - 2, 1)
            left1 = pltpu.roll(jnp.where(lane >= LANES - 1, before, x), 1, 1)
            left2 = pltpu.roll(jnp.where(lane >= LANES - 2, before, x), 2, 1)
            nearest = (rows_at(-1) + rows_at(1)) + (right1 + left1)
            farther = (rows_at(-2) + rows_at(2)) + (right2 + left2)
            if l == 0:
                beside = center[t][1]
            elif l == levels - 1:
                beside = center[t][l - 1]
            else:
                beside = center[t][l - 1] + center[t][l + 1]
            coef = last_coef if l == levels - 1 else mid_coef
            per_level.append(coef * x + horiz12 * (farther - FAR * nearest) - vert * beside)
        yield t, per_level


def strip_kernel(phi, forcing, horiz_in, vert_in, near_out, far_out, phi_s, res_s, horiz, vert, sems):
    levels, rows, cols = phi.shape
    blocks = cols // LANES
    lane, sub = iota((SUB, LANES), 1), iota((SUB, LANES), 0)
    pairs = []
    for end, row in enumerate((0, rows - SUB)):
        here = pl.ds(row, SUB)
        pairs.append((horiz_in.at[here], horiz.at[end]))
        pairs.append((vert_in.at[here], vert.at[end]))
        for t in range(blocks):
            lanes = pl.ds(t * LANES, LANES)
            pairs.append((phi.at[:, here, lanes], phi_s.at[end, t, :, pl.ds(SUB, SUB)]))
            pairs.append((forcing.at[:, here, lanes], res_s.at[end, t]))
    copies = [pltpu.make_async_copy(a, b, sems.at[n]) for n, (a, b) in enumerate(pairs)]
    for copy in copies:
        copy.start()
    zero = jnp.zeros((SUB, LANES), F32)
    for end in range(2):
        for t in range(blocks):
            for l in range(levels):
                phi_s[end, t, l, 0:SUB, :] = zero
                phi_s[end, t, l, 2 * SUB : 3 * SUB, :] = zero
    for copy in copies:
        copy.wait()
    even = lax.rem(lax.axis_index("gx"), 2) == 0
    upper = sub < SUB // 2
    kept = []
    for end in range(2):
        coefs = [
            (horiz[end, :, t * LANES : (t + 1) * LANES], vert[end, :, t * LANES : (t + 1) * LANES])
            for t in range(blocks)
        ]
        image = stencil(phi_s.at[end], SUB, range(blocks), blocks, levels, coefs, lane, False)
        strips = {}
        for t, image_t in image:
            for l in range(levels):
                potential = phi_s[end, t, l, SUB : 2 * SUB, :]
                strips[t, l] = (res_s[end, t, l] - image_t[l], potential)
            strips[t, levels] = coefs[t]
        kept.append(strips)
    for place, (a_top, b_top) in kept[0].items():
        a_low, b_low = kept[1][place]
        t, l = place
        lanes = pl.ds(t * LANES, LANES)
        top = jnp.where(upper, a_top, pltpu.roll(b_top, SUB // 2, 0))
        low = jnp.where(upper, pltpu.roll(b_low, SUB // 2, 0), a_low)
        near_out[l, :, lanes] = jnp.where(even, low, top)
        far_out[l, :, lanes] = jnp.where(even, top, low)


def lane_kinds(lane, levels):
    pair = (lane >= 8 * levels) & (lane < 12 * levels)
    from_left = jnp.where(pair, lane & 2, 4 - (lane & 4)) != 0
    return pair, from_left


def coef_slot(levels):
    return (12 * levels + 7) // 8 * 8


def pack_tile(res, phi, coefs, lane):
    levels = len(res)
    packed = jnp.zeros((SUB, LANES), F32)
    slots = [(8 * l, 8, value) for l, value in enumerate(res)]
    slots += [(coef_slot(levels) + 8 * n, 8, value) for n, value in enumerate(coefs)]
    slots += [(8 * levels + 4 * l, 4, value) for l, value in enumerate(phi)]
    for low, size, value in slots:
        here = (lane >= low) & (lane < low + size)
        packed = jnp.where(here, pltpu.roll(value, low + size // 2, 1), packed)
    pair = (lane >= 8 * levels) & (lane < 12 * levels)
    after = jnp.where(pair & ((lane & 3) == 0), pltpu.roll(packed, LANES - 1, 1), 0.0)
    before = jnp.where(pair & ((lane & 3) == 3), pltpu.roll(packed, 1, 1), 0.0)
    return packed - FAR * (after + before)


def inner_kernel(
    body_total, phi, forcing, horiz, vert, response_t, old_t, res, packed, table, phi_s, small_s
):
    blocks, levels, rows, _ = res.shape
    cols = phi.shape[2]
    zero = jnp.zeros((SUB, LANES), F32)
    for t in range(blocks):
        for l in range(levels):
            phi_s[t, l, 0:SUB, :] = zero
            phi_s[t, l, rows + SUB : rows + 2 * SUB, :] = zero
            phi_s[t, l, SUB : rows + SUB, :] = phi[l, :, t * LANES : (t + 1) * LANES]
    right = pl.ds(cols - LANES, LANES)
    left = pl.ds(0, LANES)
    lane = iota((SUB, LANES), 1)
    first = lane < LANES // 2

    def residual(i, carry):
        here = tile_at(i)
        row = pl.multiple_of(i * SUB + SUB, SUB)
        coefs = []
        for t in range(blocks):
            lanes = pl.ds(t * LANES, LANES)
            coefs.append((horiz[here, lanes], vert[here, lanes]))
        image = stencil(phi_s, row, range(blocks), blocks, levels, coefs, lane, False)
        for t, image_t in image:
            for l in range(levels):
                own = forcing[l, here, pl.ds(t * LANES, LANES)]
                res[t, l, here, :] = own - image_t[l]
        return carry

    lax.fori_loop(0, rows // SUB, residual, 0, unroll=2)

    def body(i, carry):
        here = tile_at(i)
        packed[tile_at(i + 1), :] = pack_tile(
            [jnp.where(first, res[0, l, here, :], res[blocks - 1, l, here, :]) for l in range(levels)],
            [jnp.where(first, phi[l, here, left], phi[l, here, right]) for l in range(levels)],
            [jnp.where(first, ref[here, left], ref[here, right]) for ref in (horiz, vert)],
            lane,
        )
        return carry

    lax.fori_loop(1, rows // SUB - 1, body, 0, unroll=7)

    owned, mode_count = old_t.shape
    width = table.shape[1]
    small_s[...] = jnp.zeros((LANES, LANES), F32)
    for k in range(mode_count):
        small_s[k * SUB : k * SUB + owned, 0:mode_count] = response_t[k]
        small_s[k * SUB : k * SUB + owned, mode_count : mode_count + 1] = old_t[:, k : k + 1]
    values = small_s[...].T[0:SUB, :]
    if width > LANES:
        values = jnp.concatenate([values, jnp.zeros((SUB, width - LANES), F32)], axis=1)
    wide_lane = iota((SUB, width), 1)
    me = (lax.axis_index("gx") * lax.axis_size("gy") + lax.axis_index("gy")) * owned
    for pair in range(mode_count // 2):
        tile = jnp.zeros((SUB, width), F32)
        for half in range(2):
            place = half * body_total + me
            shift = lax.rem(place - (2 * pair + half) * SUB + width, width)
            here = (wide_lane >= place) & (wide_lane < place + owned)
            tile = jnp.where(here, pltpu.roll(values, shift, 1), tile)
        table[pair * SUB : (pair + 1) * SUB, :] = tile


def edge_kernel(
    res, phi, horiz, vert, row_near, row_far, packed, edge, edge_coef, own, near_out, far_out
):
    blocks, levels, rows, _ = res.shape
    row_tiles = rows // SUB
    lane, sub = iota((SUB, LANES), 1), iota((SUB, LANES), 0)
    even = lax.rem(lax.axis_index("gx"), 2) == 0
    upper = sub < SUB // 2
    half = SUB // 2
    values = {}
    for t in range(blocks):
        lanes = pl.ds(t * LANES, LANES)
        near, far = row_near[levels, :, lanes], row_far[levels, :, lanes]
        above, below = jnp.where(even, far, near), jnp.where(even, near, far)
        h_up, v_up = jnp.where(upper, 0.0, above), jnp.where(upper, 0.0, pltpu.roll(above, half, 0))
        h_down = jnp.where(upper, below, 0.0)
        v_down = jnp.where(upper, pltpu.roll(below, half, 0), 0.0)
        edge_coef[0, 0, t], edge_coef[0, 1, t] = h_up, v_up
        edge_coef[1, 0, t], edge_coef[1, 1, t] = h_down, v_down
        first, last = pl.ds(0, SUB), pl.ds(rows - SUB, SUB)
        h_first, h_last = horiz[first, lanes], horiz[last, lanes]
        coefs = [(h_up, v_up), (h_first, vert[first, lanes]), (h_last, vert[last, lanes])]
        coefs.append((h_down, v_down))
        for n, pair in enumerate(coefs):
            values[n, t, "coef"] = pair
        scaled = [h * (1.0 / 12.0) for h, _ in coefs]

        def from_above(value):
            near_row = jnp.where(sub < 1, pltpu.roll(value, 1, 0), 0.0)
            far_row = jnp.where(sub < 2, pltpu.roll(value, 2, 0), 0.0)
            return far_row - FAR * near_row

        def from_below(value):
            near_row = jnp.where(sub >= SUB - 1, pltpu.roll(value, SUB - 1, 0), 0.0)
            far_row = jnp.where(sub >= SUB - 2, pltpu.roll(value, SUB - 2, 0), 0.0)
            return far_row - FAR * near_row

        for l in range(levels):
            near, far = row_near[l, :, lanes], row_far[l, :, lanes]
            above, below = jnp.where(even, far, near), jnp.where(even, near, far)
            res_up = jnp.where(upper, 0.0, above)
            phi_up = jnp.where(upper, 0.0, pltpu.roll(above, half, 0))
            res_down = jnp.where(upper, below, 0.0)
            phi_down = jnp.where(upper, pltpu.roll(below, half, 0), 0.0)
            phi_first, phi_last = phi[l, first, lanes], phi[l, last, lanes]
            fixed = (
                res_up - scaled[0] * from_below(phi_first),
                res[t, l, first, :] - scaled[1] * from_above(phi_up),
                res[t, l, last, :] - scaled[2] * from_below(phi_down),
                res_down - scaled[3] * from_above(phi_last),
            )
            for n, value in enumerate(fixed):
                edge[n, t, l] = value
                values[n, t, l] = value
            for n, value in enumerate((phi_up, phi_first, phi_last, phi_down)):
                values[n, t, l, "phi"] = value

    start = lane < LANES // 2
    end = blocks - 1
    tiles = [packed[i * SUB : (i + 1) * SUB, :] for i in range(row_tiles + 2)]
    for n, place in enumerate((0, 1, row_tiles, row_tiles + 1)):
        tiles[place] = pack_tile(
            [jnp.where(start, values[n, 0, l], values[n, end, l]) for l in range(levels)],
            [
                jnp.where(start, values[n, 0, l, "phi"], values[n, end, l, "phi"])
                for l in range(levels)
            ],
            [jnp.where(start, values[n, 0, "coef"][c], values[n, end, "coef"][c]) for c in range(2)],
            lane,
        )
    pair, from_left = lane_kinds(lane, levels)
    col_even = lax.rem(lax.axis_index("gy"), 2) == 0
    turned = []
    for i, tile in enumerate(tiles):
        moved = jnp.where((lane & 2) == 0, pltpu.roll(tile, LANES - 2, 1), pltpu.roll(tile, 2, 1))
        turned.append(jnp.where(pair, moved, tile))
        own[i * SUB : (i + 1) * SUB, :] = turned[i]
    fold = (row_tiles + 2) // 2
    for i in range(fold):
        other = tiles[i + fold]
        to_right = jnp.where(pair, other, pltpu.roll(other, 4, 1))
        to_right = jnp.where(from_left, turned[i], to_right)
        to_left = jnp.where(pair, other, pltpu.roll(other, LANES - 4, 1))
        to_left = jnp.where(from_left, to_left, turned[i])
        near_out[i * SUB : (i + 1) * SUB, :] = jnp.where(col_even, to_right, to_left)
        far_out[i * SUB : (i + 1) * SUB, :] = jnp.where(col_even, to_left, to_right)


def ahead_kernel(body_total, after, modes, bodies_t, modes_t, hits, hits_t):
    mode_count = modes.shape[0]
    for t in range(hits.shape[0]):
        for k in range(mode_count):
            modes_t[t, k] = modes[k, :, t * LANES : (t + 1) * LANES].T
        found = body_hits(bodies_t, t, body_total, hits.shape[1])
        hits[t] = found
        hits_t[t] = found.T


def main_kernel(
    body_total,
    res,
    edge,
    horiz,
    vert,
    edge_coef,
    own,
    col_near,
    col_far,
    table,
    mix,
    modes_t,
    hits_t,
    dir_s,
    part_s,
    message,
    res_s,
    img_s,
    horiz_s,
    vert_s,
    scale_s,
    got_s,
):
    blocks, levels, rows, _ = res.shape
    mode_count = modes_t.shape[1]
    tiles = blocks + 1
    side = blocks
    row_tiles = rows // SUB
    base = 2 * SUB
    lane = iota((SUB, LANES), 1)
    everything = range(tiles)

    pair, from_left = lane_kinds(lane, levels)
    even = lax.rem(lax.axis_index("gy"), 2) == 0
    fold = (row_tiles + 2) // 2
    for i in range(fold):
        here = pl.ds(i * SUB, SUB)
        near, far = col_near[here, :], col_far[here, :]
        left, right = jnp.where(even, far, near), jnp.where(even, near, far)
        got_s[here, :] = jnp.where(from_left, left, right)
        left = jnp.where(pair, pltpu.roll(left, 2, 1), pltpu.roll(left, LANES - 4, 1))
        right = jnp.where(pair, pltpu.roll(right, LANES - 2, 1), pltpu.roll(right, 4, 1))
        there = pl.ds((i + fold) * SUB, SUB)
        got_s[there, :] = jnp.where(from_left, left, right)

    def first(i, inner, residuals, coefs):
        here = tile_at(i)
        there = tile_at(i + 1)
        got, mine = got_s[here, :], own[here, :]
        halo = (lane < 4) | (lane >= LANES - 4)
        slot = coef_slot(levels)
        side_coef = [
            jnp.where(halo, pltpu.roll(got, (LANES - 4 - slot - 8 * n) % LANES, 1), 0.0) for n in range(2)
        ]
        coefs = list(coefs) + [tuple(side_coef)]
        outer = (lane < 2, lane >= LANES - 2, (lane < 2) | (lane >= LANES - 2))
        scales, edges = [], []
        for t in everything:
            h, v = coefs[t]
            bottom = 5.0 * h + 2.0 * v
            inside = bottom > 0.0
            scale = jnp.where(inside, 1.0 / jnp.where(inside, bottom, 1.0), 0.0)
            scales.append(scale)
            scale_s[t, there, :] = scale
            horiz_s[t, there, :] = h
            vert_s[t, there, :] = v
            if t == side:
                mask = outer[2]
            elif blocks == 1:
                mask = outer[2]
            elif t == 0:
                mask = outer[0]
            elif t == blocks - 1:
                mask = outer[1]
            else:
                mask = None
            edges.append(None if mask is None else jnp.where(mask, h * (1.0 / 12.0), 0.0))
        weighted = [[] for _ in everything]
        for l in range(levels):
            place = (LANES - 2 - 8 * levels - 4 * l) % LANES
            theirs = pltpu.roll(got, place, 1)
            ours = pltpu.roll(mine, place, 1)
            for t in everything:
                if t == side:
                    value = pltpu.roll(got, (LANES - 4 - 8 * l) % LANES, 1) - edges[t] * ours
                else:
                    value = residuals[t][l]
                    if edges[t] is not None:
                        value = value - edges[t] * theirs
                    if inner:
                        res_s[t, l, there, :] = value
                weighted[t].append(value * scales[t])
        for t in everything:
            for l, value in enumerate(mix_levels(mix, weighted[t], levels)):
                dir_s[t, l, there, :] = value

    def own_coefs(i):
        here = tile_at(i)
        result = []
        for t in range(blocks):
            lanes = pl.ds(t * LANES, LANES)
            result.append((horiz[here, lanes], vert[here, lanes]))
        return result

    for n, i in enumerate((0, 1, row_tiles, row_tiles + 1)):
        residuals = [[edge[n, t, l] for l in range(levels)] for t in range(blocks)]
        if 1 <= i <= row_tiles:
            coefs = own_coefs(i - 1)
        else:
            coefs = [(edge_coef[n // 2, 0, t], edge_coef[n // 2, 1, t]) for t in range(blocks)]
        first(i, 1 <= i <= row_tiles, residuals, coefs)

    def first_body(i, carry):
        here = tile_at(i - 1)
        residuals = [[res[t, l, here, :] for l in range(levels)] for t in range(blocks)]
        first(i, True, residuals, own_coefs(i - 1))
        return carry

    lax.fori_loop(2, row_tiles, first_body, 0, unroll=7)

    def coefs_at(row, count):
        here = pl.ds(row, SUB)
        return [(horiz_s[t, here, :], vert_s[t, here, :]) for t in range(count)]

    def second(i, carry):
        row = pl.multiple_of(i * SUB + SUB, SUB)
        here = pl.ds(row, SUB)
        image = stencil(
            dir_s, row, everything, tiles, levels, coefs_at(row, tiles), lane, True
        )
        for t, image_t in image:
            scale = scale_s[t, here, :]
            weighted = []
            for l in range(levels):
                img_s[t, l, here, :] = image_t[l]
                weighted.append(image_t[l] * scale)
            for l, value in enumerate(mix_levels(mix, weighted, levels)):
                part_s[t, l, here, :] = value
        return carry

    def third(i, totals):
        row = pl.multiple_of(i * SUB + SUB, SUB)
        here = pl.ds(row, SUB)
        image = stencil(
            part_s, row, range(blocks), tiles, levels, coefs_at(row, blocks), lane, True
        )
        totals = list(totals)
        for t, image_t in image:
            for l in range(levels):
                residual = res_s[t, l, here, :]
                img1 = img_s[t, l, here, :]
                img2 = image_t[l]
                products = (residual * img1, img1 * img1, residual * img2, img1 * img2, img2 * img2)
                totals = [total + product for total, product in zip(totals, products)]
        return tuple(totals)

    zero = jnp.zeros((SUB, LANES), F32)
    lax.fori_loop(0, row_tiles + 2, second, 0, unroll=3)
    totals = lax.fori_loop(1, row_tiles + 1, third, (zero,) * 5, unroll=4)

    width = message.shape[1]
    surface_rows = pl.ds(base, rows)
    forces = jnp.zeros((SUB, width), F32)
    for t in range(blocks):
        for q, field in enumerate((dir_s, part_s)):
            surface = field[t, 0, surface_rows, :].T
            sums = [
                jnp.sum(modes_t[t, k] * surface, axis=0, keepdims=True) for k in range(mode_count)
            ]
            sums.append(jnp.zeros((SUB - mode_count, rows), F32))
            share = exact_dot(jnp.concatenate(sums, axis=0), hits_t[t])
            forces = forces + (pltpu.roll(share, body_total, 1) if q else share)
    wide_sub = iota((SUB, width), 0)
    gathered = jnp.zeros((SUB, LANES), F32)
    for q, total in enumerate(totals):
        gathered = jnp.where(lane == q, jnp.sum(total, axis=1, keepdims=True), gathered)
    gathered = jnp.sum(gathered, axis=0, keepdims=True)
    if width > LANES:
        gathered = jnp.concatenate([gathered, jnp.zeros((1, width - LANES), F32)], axis=1)
    message[0:SUB, :] = jnp.where(wide_sub == SUB - 2, gathered, forces)
    message[SUB:, :] = table[...]


def mix_levels(mix, weighted, levels):
    out = []
    for l in range(levels):
        total = (mix[l, l] + 1.0) * weighted[l]
        for m in range(levels):
            if m != l:
                total = total + mix[l, m] * weighted[m]
        out.append(total)
    return out


def body_hits(bodies_t, block, count, width):
    ids = bodies_t[block : block + 1, :]
    ids = jnp.where(ids < count, ids, -1)
    wanted = lax.broadcasted_iota(jnp.int32, (width, ids.shape[1]), 0)
    return (jnp.broadcast_to(ids, wanted.shape) == wanted).astype(F32)


def dot_nt(a, b):
    return lax.dot_general(
        a, b, (((1,), (1,)), ((), ())), precision=lax.Precision.HIGHEST, preferred_element_type=F32
    )


def exact_dot(values, ones):
    high = values.astype(jnp.bfloat16).astype(F32)
    rest = values - high
    middle = rest.astype(jnp.bfloat16).astype(F32)
    parts = jnp.concatenate([high, middle, rest - middle, jnp.zeros_like(high)], axis=0)
    shares = jnp.dot(
        parts.astype(jnp.bfloat16), ones.astype(jnp.bfloat16), preferred_element_type=F32
    )
    return shares[0:SUB] + (shares[SUB : 2 * SUB] + shares[2 * SUB : 3 * SUB])


def last_kernel(
    body_total,
    message,
    phi,
    direction,
    part,
    modes_t,
    hits,
    potential,
    velocity_t,
    flux,
    phi_s,
    flux_s,
    velocity_s,
    out_sems,
):
    levels, rows, cols = phi.shape
    blocks, mode_count = modes_t.shape[0:2]
    width = message.shape[1]
    owned = velocity_t.shape[0]
    main = pl.ds(2 * SUB, rows)
    top = message[0:SUB, :]

    def scalar(q):
        return top[SUB - 2 : SUB - 1, q : q + 1]

    cross_first, square_first, cross_mixed, square_mixed, square_second = [
        scalar(q) for q in range(5)
    ]
    first_step = cross_first / square_first
    next_top = (
        cross_first
        - first_step * cross_mixed
        - first_step * square_first
        + first_step * first_step * square_mixed
    )
    next_bottom = (
        square_first - 2.0 * first_step * square_mixed + first_step * first_step * square_second
    )
    second_step = next_top / next_bottom
    on_dir = first_step + second_step
    on_part = first_step * second_step
    outgoing = []

    def send(src, dst):
        copy = pltpu.make_async_copy(src, dst, out_sems.at[len(outgoing)])
        copy.start()
        outgoing.append(copy)


    for l in range(levels):
        for t in range(blocks):
            lanes = pl.ds(t * LANES, LANES)
            change = on_dir * direction[t, l, main, :] - on_part * part[t, l, main, :]
            phi_s[l, :, lanes] = phi[l, :, lanes] + change
        send(phi_s.at[l], potential.at[l])

    wide_sub, wide_lane = iota((SUB, width), 0), iota((SUB, width), 1)
    foot_scale = 1.0 / math.sqrt(FOOT)
    forces = foot_scale * (on_part * pltpu.roll(top, body_total, 1) - on_dir * top)
    forces = jnp.where(wide_sub == mode_count, 1.0, forces)
    forces = jnp.where(wide_lane < body_total, forces, 0.0)
    velocity = jnp.zeros((SUB, width), F32)
    for k in range(mode_count):
        table = message[(k // 2 + 1) * SUB : (k // 2 + 2) * SUB, :]
        if k % 2:
            table = pltpu.roll(table, body_total, 1)
        value = jnp.sum(table * forces, axis=0, keepdims=True)
        velocity = jnp.where(wide_sub == k, value, velocity)
    per_row = [exact_dot(velocity, hits[t]) for t in range(blocks)]

    me = (lax.axis_index("gx") * lax.axis_size("gy") + lax.axis_index("gy")) * owned
    mine = ((wide_lane == me + wide_sub) & (wide_sub < owned)).astype(F32)
    velocity_s[...] = dot_nt(mine, velocity)[0:owned, 0:mode_count]
    send(velocity_s, velocity_t)
    for t in range(blocks):
        total = modes_t[t, 0] * per_row[t][0:1, :]
        for k in range(1, mode_count):
            total = total + modes_t[t, k] * per_row[t][k : k + 1, :]
        flux_s[:, t * LANES : (t + 1) * LANES] = total.T
    send(flux_s, flux)
    for copy in outgoing:
        copy.wait()


def swap_near(value, axis):
    size = lax.axis_size(axis)
    return lax.ppermute(value, axis, [(i, i ^ 1) for i in range(size)])


def swap_far(value, axis):
    size = lax.axis_size(axis)
    pairs = [(i, i + 1) for i in range(1, size - 1, 2)]
    return lax.ppermute(value, axis, pairs + [(j, i) for i, j in pairs])


def sum_over(value, axis, together):
    size = lax.axis_size(axis)
    step = 1
    while step < size:
        count = min(together, size // step)
        total = value
        for n in range(1, count):
            pairs = [(i, i ^ (n * step)) for i in range(size)]
            total = total + lax.ppermute(value, axis, pairs)
        value = total
        step *= count
    return value


def per_device(
    forcing,
    start_potential,
    horiz_coef,
    vert_coef,
    vert_mix,
    mode_shapes,
    block_body,
    response,
    velocity_old,
):
    levels, rows, cols = forcing.shape
    mode_count = mode_shapes.shape[0]
    blocks = cols // LANES
    tiles = blocks + 1
    padded = rows + 4 * SUB
    owned = velocity_old.shape[1]
    body_total = owned * lax.axis_size(("gx", "gy"))
    width = 2 * body_total
    bodies_t = block_body.T
    response_t = jnp.swapaxes(response, 1, 2)
    old_t = velocity_old.T
    limit = pltpu.CompilerParams(vmem_limit_bytes=24 * 2**20)

    def call(kernel, name, outs, ins, args, scratch=()):
        return pl.pallas_call(
            kernel,
            out_shape=tuple(jax.ShapeDtypeStruct(shape, F32) for shape, _ in outs),
            in_specs=ins,
            out_specs=tuple(spec for _, spec in outs),
            scratch_shapes=list(scratch),
            compiler_params=limit,
            name=name,
        )(*args)

    strip = (levels + 1, SUB, cols)
    inner = (blocks, levels, rows, LANES)
    near, far = call(
        strip_kernel,
        "strip_kernel",
        [(strip, VMEM), (strip, VMEM)],
        [HBM] * 4,
        [
            pltpu.with_memory_space_constraint(value, pltpu.HBM)
            for value in (start_potential, forcing, horiz_coef, vert_coef)
        ],
        [
            pltpu.VMEM((2, blocks, levels, 3 * SUB, LANES), F32),
            pltpu.VMEM((2, blocks, levels, SUB, LANES), F32),
            pltpu.VMEM((2, SUB, cols), F32),
            pltpu.VMEM((2, SUB, cols), F32),
            pltpu.SemaphoreType.DMA((4 + 4 * blocks,)),
        ],
    )
    row_near, row_far = swap_near(near, "gx"), swap_far(far, "gx")
    packed_shape = (rows + 2 * SUB, LANES)
    res, packed, table = call(
        functools.partial(inner_kernel, body_total),
        "inner_kernel",
        [(inner, VMEM), (packed_shape, VMEM), ((3 * SUB, width), VMEM)],
        [VMEM] * 6,
        (start_potential, forcing, horiz_coef, vert_coef, response_t, old_t),
        [
            pltpu.VMEM((blocks, levels, rows + 2 * SUB, LANES), F32),
            pltpu.VMEM((LANES, LANES), F32),
        ],
    )
    strip = (rows // 2 + SUB, LANES)
    edge, edge_coef, own, near, far = call(
        edge_kernel,
        "edge_kernel",
        [
            ((4, blocks, levels, SUB, LANES), VMEM),
            ((2, 2, blocks, SUB, LANES), VMEM),
            (packed_shape, VMEM),
            (strip, VMEM),
            (strip, VMEM),
        ],
        [VMEM] * 7,
        (res, start_potential, horiz_coef, vert_coef, row_near, row_far, packed),
    )
    col_near, col_far = swap_near(near, "gy"), swap_far(far, "gy")
    modes_t, hits, hits_t = call(
        functools.partial(ahead_kernel, body_total),
        "ahead_kernel",
        [((blocks, mode_count, LANES, rows), VMEM), ((blocks, width, rows), VMEM), ((blocks, rows, width), VMEM)],
        [VMEM] * 3,
        (edge_coef, mode_shapes, bodies_t),
    )

    field = (tiles, levels, padded, LANES)
    plane = pltpu.VMEM((tiles, padded, LANES), F32)
    direction, part, message = call(
        functools.partial(main_kernel, body_total),
        "main_kernel",
        [(field, VMEM), (field, VMEM), ((4 * SUB, width), VMEM)],
        [VMEM] * 9 + [SMEM] + [VMEM] * 2,
        (
            res,
            edge,
            horiz_coef,
            vert_coef,
            edge_coef,
            own,
            col_near,
            col_far,
            table,
            vert_mix,
            modes_t,
            hits_t,
        ),
        [
            pltpu.VMEM((blocks, levels, padded, LANES), F32),
            pltpu.VMEM(field, F32),
            plane,
            plane,
            plane,
            pltpu.VMEM(packed_shape, F32),
        ],
    )
    message = sum_over(sum_over(message, "gx", 2), "gy", 4)

    potential, velocity_t, flux = call(
        functools.partial(last_kernel, body_total),
        "last_kernel",
        [((levels, rows, cols), HBM), ((owned, mode_count), HBM), ((rows, cols), HBM)],
        [VMEM] * 6,
        (message, start_potential, direction, part, modes_t, hits),
        [
            pltpu.VMEM((levels, rows, cols), F32),
            pltpu.VMEM((rows, cols), F32),
            pltpu.VMEM((owned, mode_count), F32),
            pltpu.SemaphoreType.DMA((levels + 2,)),
        ],
    )
    return (potential, velocity_t.T, flux)


def solution(mesh):
    return jax.shard_map(
        per_device,
        mesh=mesh,
        in_specs=(
            P(None, "gx", "gy"),
            P(None, "gx", "gy"),
            P("gx", "gy"),
            P("gx", "gy"),
            P(),
            P(None, "gx", "gy"),
            P("gx", "gy"),
            P(None, None, ("gx", "gy")),
            P(None, ("gx", "gy")),
        ),
        out_specs=(P(None, "gx", "gy"), P(None, ("gx", "gy")), P("gx", "gy")),
        check_vma=False,
    )
```

```python
import functools
import math

import jax
import jax.numpy as jnp
from jax import lax
from jax.experimental import pallas as pl
from jax.experimental.pallas import tpu as pltpu
from jax.sharding import PartitionSpec as P

FOOT = 8192
LANES = 128
SUB = 8
FAR = 16.0
F32 = jnp.float32
HBM = pl.BlockSpec(memory_space=pltpu.HBM)
VMEM = pl.BlockSpec(memory_space=pltpu.VMEM)
SMEM = pl.BlockSpec(memory_space=pltpu.SMEM)


def iota(shape, dim):
    return lax.broadcasted_iota(jnp.int32, shape, dim)


def tile_at(index):
    return pl.ds(pl.multiple_of(index * SUB, SUB), SUB)


def stencil(ref, row, t, tiles, levels, coefs, lane, wrap):
    here = pl.ds(row, SUB)
    horiz, vert = coefs
    last_coef = 5.0 * horiz + vert
    mid_coef = last_coef + vert
    horiz12 = horiz * (1.0 / 12.0)
    for l in range(levels):
        x = ref[t, l, here, :]
        after = ref[(t + 1) % tiles, l, here, :] if wrap or t + 1 < tiles else 0.0
        before = ref[(t - 1) % tiles, l, here, :] if wrap or t > 0 else 0.0

        def rows_at(offset):
            return ref[t, l, pl.ds(row + offset, SUB), :]

        right1 = pltpu.roll(jnp.where(lane < 1, after, x), LANES - 1, 1)
        right2 = pltpu.roll(jnp.where(lane < 2, after, x), LANES - 2, 1)
        left1 = pltpu.roll(jnp.where(lane >= LANES - 1, before, x), 1, 1)
        left2 = pltpu.roll(jnp.where(lane >= LANES - 2, before, x), 2, 1)
        nearest = (rows_at(-1) + rows_at(1)) + (right1 + left1)
        farther = (rows_at(-2) + rows_at(2)) + (right2 + left2)
        if l == 0:
            beside = ref[t, 1, here, :]
        elif l == levels - 1:
            beside = ref[t, l - 1, here, :]
        else:
            beside = ref[t, l - 1, here, :] + ref[t, l + 1, here, :]
        coef = last_coef if l == levels - 1 else mid_coef
        yield coef * x + horiz12 * (farther - FAR * nearest) - vert * beside


def strip_kernel(phi, forcing, horiz_in, vert_in, near_out, far_out, phi_s, res_s, horiz, vert, sems):
    levels, rows, cols = phi.shape
    blocks = cols // LANES
    lane, sub = iota((SUB, LANES), 1), iota((SUB, LANES), 0)
    pairs = []
    for end, row in enumerate((0, rows - SUB)):
        here = pl.ds(row, SUB)
        pairs.append((horiz_in.at[here], horiz.at[end]))
        pairs.append((vert_in.at[here], vert.at[end]))
        for t in range(blocks):
            lanes = pl.ds(t * LANES, LANES)
            pairs.append((phi.at[:, here, lanes], phi_s.at[end, t, :, pl.ds(SUB, SUB)]))
            pairs.append((forcing.at[:, here, lanes], res_s.at[end, t]))
    copies = [pltpu.make_async_copy(a, b, sems.at[n]) for n, (a, b) in enumerate(pairs)]
    for copy in copies:
        copy.start()
    zero = jnp.zeros((SUB, LANES), F32)
    for end in range(2):
        for t in range(blocks):
            for l in range(levels):
                phi_s[end, t, l, 0:SUB, :] = zero
                phi_s[end, t, l, 2 * SUB : 3 * SUB, :] = zero
    for copy in copies:
        copy.wait()
    even = lax.rem(lax.axis_index("gx"), 2) == 0
    upper = sub < SUB // 2
    kept = []
    for end in range(2):
        coefs = [
            (horiz[end, :, t * LANES : (t + 1) * LANES], vert[end, :, t * LANES : (t + 1) * LANES])
            for t in range(blocks)
        ]
        strips = {}
        for t in range(blocks):
            image = stencil(phi_s.at[end], SUB, t, blocks, levels, coefs[t], lane, False)
            for l, value in enumerate(image):
                potential = phi_s[end, t, l, SUB : 2 * SUB, :]
                strips[t, l] = (res_s[end, t, l] - value, potential)
            strips[t, levels] = coefs[t]
        kept.append(strips)
    for place, (a_top, b_top) in kept[0].items():
        a_low, b_low = kept[1][place]
        t, l = place
        lanes = pl.ds(t * LANES, LANES)
        top = jnp.where(upper, a_top, pltpu.roll(b_top, SUB // 2, 0))
        low = jnp.where(upper, pltpu.roll(b_low, SUB // 2, 0), a_low)
        near_out[l, :, lanes] = jnp.where(even, low, top)
        far_out[l, :, lanes] = jnp.where(even, top, low)


def lane_kinds(lane, levels):
    pair = (lane >= 8 * levels) & (lane < 12 * levels)
    from_left = jnp.where(pair, lane & 2, 4 - (lane & 4)) != 0
    return pair, from_left


def coef_slot(levels):
    return (12 * levels + 7) // 8 * 8


def pack_tile(res, phi, coefs, lane):
    levels = len(res)
    packed = jnp.zeros((SUB, LANES), F32)
    slots = [(8 * l, 8, value) for l, value in enumerate(res)]
    slots += [(coef_slot(levels) + 8 * n, 8, value) for n, value in enumerate(coefs)]
    slots += [(8 * levels + 4 * l, 4, value) for l, value in enumerate(phi)]
    for low, size, value in slots:
        here = (lane >= low) & (lane < low + size)
        packed = jnp.where(here, pltpu.roll(value, low + size // 2, 1), packed)
    pair = (lane >= 8 * levels) & (lane < 12 * levels)
    after = jnp.where(pair & ((lane & 3) == 0), pltpu.roll(packed, LANES - 1, 1), 0.0)
    before = jnp.where(pair & ((lane & 3) == 3), pltpu.roll(packed, 1, 1), 0.0)
    return packed - FAR * (after + before)


def inner_kernel(
    body_total, phi, forcing, horiz, vert, response_t, old_t, res, packed, table, phi_s, small_s
):
    blocks, levels, rows, _ = res.shape
    cols = phi.shape[2]
    zero = jnp.zeros((SUB, LANES), F32)
    for t in range(blocks):
        for l in range(levels):
            phi_s[t, l, 0:SUB, :] = zero
            phi_s[t, l, rows + SUB : rows + 2 * SUB, :] = zero
            phi_s[t, l, SUB : rows + SUB, :] = phi[l, :, t * LANES : (t + 1) * LANES]
    right = pl.ds(cols - LANES, LANES)
    left = pl.ds(0, LANES)
    lane = iota((SUB, LANES), 1)
    first = lane < LANES // 2

    def residual(i, carry):
        here = tile_at(i)
        row = pl.multiple_of(i * SUB + SUB, SUB)
        for t in range(blocks):
            lanes = pl.ds(t * LANES, LANES)
            coefs = (horiz[here, lanes], vert[here, lanes])
            image = stencil(phi_s, row, t, blocks, levels, coefs, lane, False)
            for l, value in enumerate(image):
                res[t, l, here, :] = forcing[l, here, lanes] - value
        return carry

    lax.fori_loop(0, rows // SUB, residual, 0, unroll=2)

    def body(i, carry):
        here = tile_at(i)
        packed[tile_at(i + 1), :] = pack_tile(
            [jnp.where(first, res[0, l, here, :], res[blocks - 1, l, here, :]) for l in range(levels)],
            [jnp.where(first, phi[l, here, left], phi[l, here, right]) for l in range(levels)],
            [jnp.where(first, ref[here, left], ref[here, right]) for ref in (horiz, vert)],
            lane,
        )
        return carry

    lax.fori_loop(1, rows // SUB - 1, body, 0, unroll=7)

    owned, mode_count = old_t.shape
    width = table.shape[1]
    small_s[...] = jnp.zeros((LANES, LANES), F32)
    for k in range(mode_count):
        small_s[k * SUB : k * SUB + owned, 0:mode_count] = response_t[k]
        small_s[k * SUB : k * SUB + owned, mode_count : mode_count + 1] = old_t[:, k : k + 1]
    values = small_s[...].T[0:SUB, :]
    if width > LANES:
        values = jnp.concatenate([values, jnp.zeros((SUB, width - LANES), F32)], axis=1)
    wide_lane = iota((SUB, width), 1)
    me = (lax.axis_index("gx") * lax.axis_size("gy") + lax.axis_index("gy")) * owned
    for pair in range(mode_count // 2):
        tile = jnp.zeros((SUB, width), F32)
        for half in range(2):
            place = half * body_total + me
            shift = lax.rem(place - (2 * pair + half) * SUB + width, width)
            here = (wide_lane >= place) & (wide_lane < place + owned)
            tile = jnp.where(here, pltpu.roll(values, shift, 1), tile)
        table[pair * SUB : (pair + 1) * SUB, :] = tile


def edge_kernel(
    res, phi, horiz, vert, row_near, row_far, packed, edge, edge_coef, own, near_out, far_out
):
    blocks, levels, rows, _ = res.shape
    row_tiles = rows // SUB
    lane, sub = iota((SUB, LANES), 1), iota((SUB, LANES), 0)
    even = lax.rem(lax.axis_index("gx"), 2) == 0
    upper = sub < SUB // 2
    half = SUB // 2
    values = {}
    for t in range(blocks):
        lanes = pl.ds(t * LANES, LANES)
        near, far = row_near[levels, :, lanes], row_far[levels, :, lanes]
        above, below = jnp.where(even, far, near), jnp.where(even, near, far)
        h_up, v_up = jnp.where(upper, 0.0, above), jnp.where(upper, 0.0, pltpu.roll(above, half, 0))
        h_down = jnp.where(upper, below, 0.0)
        v_down = jnp.where(upper, pltpu.roll(below, half, 0), 0.0)
        edge_coef[0, 0, t], edge_coef[0, 1, t] = h_up, v_up
        edge_coef[1, 0, t], edge_coef[1, 1, t] = h_down, v_down
        first, last = pl.ds(0, SUB), pl.ds(rows - SUB, SUB)
        h_first, h_last = horiz[first, lanes], horiz[last, lanes]
        coefs = [(h_up, v_up), (h_first, vert[first, lanes]), (h_last, vert[last, lanes])]
        coefs.append((h_down, v_down))
        for n, pair in enumerate(coefs):
            values[n, t, "coef"] = pair
        scaled = [h * (1.0 / 12.0) for h, _ in coefs]

        def from_above(value):
            near_row = jnp.where(sub < 1, pltpu.roll(value, 1, 0), 0.0)
            far_row = jnp.where(sub < 2, pltpu.roll(value, 2, 0), 0.0)
            return far_row - FAR * near_row

        def from_below(value):
            near_row = jnp.where(sub >= SUB - 1, pltpu.roll(value, SUB - 1, 0), 0.0)
            far_row = jnp.where(sub >= SUB - 2, pltpu.roll(value, SUB - 2, 0), 0.0)
            return far_row - FAR * near_row

        for l in range(levels):
            near, far = row_near[l, :, lanes], row_far[l, :, lanes]
            above, below = jnp.where(even, far, near), jnp.where(even, near, far)
            res_up = jnp.where(upper, 0.0, above)
            phi_up = jnp.where(upper, 0.0, pltpu.roll(above, half, 0))
            res_down = jnp.where(upper, below, 0.0)
            phi_down = jnp.where(upper, pltpu.roll(below, half, 0), 0.0)
            phi_first, phi_last = phi[l, first, lanes], phi[l, last, lanes]
            fixed = (
                res_up - scaled[0] * from_below(phi_first),
                res[t, l, first, :] - scaled[1] * from_above(phi_up),
                res[t, l, last, :] - scaled[2] * from_below(phi_down),
                res_down - scaled[3] * from_above(phi_last),
            )
            for n, value in enumerate(fixed):
                edge[n, t, l] = value
                values[n, t, l] = value
            for n, value in enumerate((phi_up, phi_first, phi_last, phi_down)):
                values[n, t, l, "phi"] = value

    start = lane < LANES // 2
    end = blocks - 1
    tiles = [packed[i * SUB : (i + 1) * SUB, :] for i in range(row_tiles + 2)]
    for n, place in enumerate((0, 1, row_tiles, row_tiles + 1)):
        tiles[place] = pack_tile(
            [jnp.where(start, values[n, 0, l], values[n, end, l]) for l in range(levels)],
            [
                jnp.where(start, values[n, 0, l, "phi"], values[n, end, l, "phi"])
                for l in range(levels)
            ],
            [jnp.where(start, values[n, 0, "coef"][c], values[n, end, "coef"][c]) for c in range(2)],
            lane,
        )
    pair, from_left = lane_kinds(lane, levels)
    col_even = lax.rem(lax.axis_index("gy"), 2) == 0
    turned = []
    for i, tile in enumerate(tiles):
        moved = jnp.where((lane & 2) == 0, pltpu.roll(tile, LANES - 2, 1), pltpu.roll(tile, 2, 1))
        turned.append(jnp.where(pair, moved, tile))
        own[i * SUB : (i + 1) * SUB, :] = turned[i]
    fold = (row_tiles + 2) // 2
    for i in range(fold):
        other = tiles[i + fold]
        to_right = jnp.where(pair, other, pltpu.roll(other, 4, 1))
        to_right = jnp.where(from_left, turned[i], to_right)
        to_left = jnp.where(pair, other, pltpu.roll(other, LANES - 4, 1))
        to_left = jnp.where(from_left, to_left, turned[i])
        near_out[i * SUB : (i + 1) * SUB, :] = jnp.where(col_even, to_right, to_left)
        far_out[i * SUB : (i + 1) * SUB, :] = jnp.where(col_even, to_left, to_right)


def ahead_kernel(
    body_total,
    res,
    edge,
    horiz_in,
    vert_in,
    edge_coef,
    mix,
    modes,
    bodies_t,
    modes_t,
    hits,
    hits_t,
    early,
    res_own,
    horiz,
    vert,
    scale,
):
    blocks, levels, rows, _ = res.shape
    row_tiles = rows // SUB
    mode_count = modes.shape[0]
    for t in range(blocks):
        for k in range(mode_count):
            modes_t[t, k] = modes[k, :, t * LANES : (t + 1) * LANES].T
        found = body_hits(bodies_t, t, body_total, hits.shape[1])
        hits[t] = found
        hits_t[t] = found.T

    def direction(i, own, residuals, coefs):
        there = tile_at(i + 1)
        for t in range(blocks):
            h, v = coefs[t]
            bottom = 5.0 * h + 2.0 * v
            inside = bottom > 0.0
            factor = jnp.where(inside, 1.0 / jnp.where(inside, bottom, 1.0), 0.0)
            scale[t, there, :] = factor
            horiz[t, there, :] = h
            vert[t, there, :] = v
            if own:
                for l in range(levels):
                    res_own[t, l, there, :] = residuals[t][l]
            weighted = [value * factor for value in residuals[t]]
            for l, value in enumerate(mix_levels(mix, weighted, levels)):
                early[t, l, there, :] = value

    def own_coefs(i):
        here = tile_at(i)
        result = []
        for t in range(blocks):
            lanes = pl.ds(t * LANES, LANES)
            result.append((horiz_in[here, lanes], vert_in[here, lanes]))
        return result

    for n, i in enumerate((0, 1, row_tiles, row_tiles + 1)):
        own = 1 <= i <= row_tiles
        residuals = [[edge[n, t, l] for l in range(levels)] for t in range(blocks)]
        if own:
            coefs = own_coefs(i - 1)
        else:
            coefs = [(edge_coef[n // 2, 0, t], edge_coef[n // 2, 1, t]) for t in range(blocks)]
        direction(i, own, residuals, coefs)

    def body(i, carry):
        here = tile_at(i - 1)
        residuals = [[res[t, l, here, :] for l in range(levels)] for t in range(blocks)]
        direction(i, True, residuals, own_coefs(i - 1))
        return carry

    lax.fori_loop(2, row_tiles, body, 0, unroll=2)


def main_kernel(
    body_total,
    early,
    res_own,
    horiz,
    vert,
    scale,
    own,
    col_near,
    col_far,
    table,
    mix,
    modes_t,
    hits_t,
    dir_s,
    part_s,
    message,
    res_s,
    img_s,
    horiz_s,
    vert_s,
    scale_s,
    got_s,
):
    blocks, levels, padded, _ = early.shape
    rows = padded - 4 * SUB
    mode_count = modes_t.shape[1]
    tiles = blocks + 1
    side = blocks
    row_tiles = rows // SUB
    base = 2 * SUB
    lane = iota((SUB, LANES), 1)
    everything = range(tiles)

    pair, from_left = lane_kinds(lane, levels)
    even = lax.rem(lax.axis_index("gy"), 2) == 0
    fold = (row_tiles + 2) // 2
    for i in range(fold):
        here = pl.ds(i * SUB, SUB)
        near, far = col_near[here, :], col_far[here, :]
        left, right = jnp.where(even, far, near), jnp.where(even, near, far)
        got_s[here, :] = jnp.where(from_left, left, right)
        left = jnp.where(pair, pltpu.roll(left, 2, 1), pltpu.roll(left, LANES - 4, 1))
        right = jnp.where(pair, pltpu.roll(right, LANES - 2, 1), pltpu.roll(right, 4, 1))
        there = pl.ds((i + fold) * SUB, SUB)
        got_s[there, :] = jnp.where(from_left, left, right)

    halo = (lane < 4) | (lane >= LANES - 4)
    half = LANES // 2
    slot = coef_slot(levels)

    def first(group, inner):
        starts, ends = lane < 2, lane >= LANES - 2
        weighted = []
        for i in group:
            there, here = tile_at(i + 1), tile_at(i)
            got, mine = got_s[here, :], own[here, :]
            h, v = [
                jnp.where(halo, pltpu.roll(got, (LANES - 4 - slot - 8 * n) % LANES, 1), 0.0)
                for n in range(2)
            ]
            bottom = 5.0 * h + 2.0 * v
            inside = bottom > 0.0
            factor = jnp.where(inside, 1.0 / jnp.where(inside, bottom, 1.0), 0.0)
            scale_s[there, :] = factor
            horiz_s[there, :] = h
            vert_s[there, :] = v
            side_edge = jnp.where(starts | ends, h * (factor * (1.0 / 12.0)), 0.0)
            first_edge = jnp.where(starts, horiz[0, there, :] * (1.0 / 12.0), 0.0)
            last_edge = jnp.where(ends, horiz[side - 1, there, :] * (1.0 / 12.0), 0.0)
            both = first_edge * scale[0, there, :] + last_edge * scale[side - 1, there, :]
            both = pltpu.roll(both, half, 1)
            values = []
            for l in range(levels):
                place = (LANES - 2 - 8 * levels - 4 * l) % LANES
                ours = pltpu.roll(mine, place, 1)
                beyond = pltpu.roll(got, (LANES - 4 - 8 * l) % LANES, 1)
                across = pltpu.roll(got, (place + half) % LANES, 1)
                values.append(beyond * factor - side_edge * ours - both * across)
                if inner:
                    theirs = pltpu.roll(got, place, 1)
                    terms = [jnp.zeros_like(theirs)] * blocks
                    terms[0] = terms[0] + first_edge * theirs
                    terms[-1] = terms[-1] + last_edge * theirs
                    for t in range(blocks):
                        res_s[t, l, there, :] = res_own[t, l, there, :] - terms[t]
            weighted.append(values)
        mixed = [mix_levels(mix, values, levels) for values in weighted]
        turned = [[pltpu.roll(value, half, 1) for value in values] for values in mixed]
        for n, i in enumerate(group):
            there = tile_at(i + 1)
            for l in range(levels):
                dir_s[side, l, there, :] = mixed[n][l]
                changes = [jnp.zeros((SUB, LANES), F32)] * blocks
                changes[0] = changes[0] + jnp.where(starts, turned[n][l], 0.0)
                changes[-1] = changes[-1] + jnp.where(ends, turned[n][l], 0.0)
                for t in range(blocks):
                    dir_s[t, l, there, :] = early[t, l, there, :] + changes[t]

    def first_body(i, carry):
        first([8 * i + n + 1 for n in range(8)], True)
        return carry

    first([0, row_tiles + 1], False)
    lax.fori_loop(0, row_tiles // 8, first_body, 0, unroll=1)

    def coefs_at(t, row):
        here = pl.ds(row, SUB)
        if t == side:
            return horiz_s[here, :], vert_s[here, :]
        return horiz[t, here, :], vert[t, here, :]

    def second(group):
        rows_of = [pl.multiple_of(i * SUB + SUB, SUB) for i in group]
        waiting = None
        for row in rows_of:
            for t in everything:
                here = pl.ds(row, SUB)
                factor = scale_s[here, :] if t == side else scale[t, here, :]
                weighted = []
                image = stencil(dir_s, row, t, tiles, levels, coefs_at(t, row), lane, True)
                for l, value in enumerate(image):
                    img_s[t, l, here, :] = value
                    weighted.append(value * factor)
                    if waiting:
                        part_s[waiting[0], l, waiting[1], :] = mix_level(mix, waiting[2], l)
                waiting = (t, here, weighted)
        for l in range(levels):
            part_s[waiting[0], l, waiting[1], :] = mix_level(mix, waiting[2], l)

    def second_body(i, carry):
        second([9 * i + n for n in range(9)])
        return carry

    lax.fori_loop(0, (row_tiles + 2) // 9, second_body, 0, unroll=1)
    for i in range((row_tiles + 2) // 9 * 9, row_tiles + 2):
        second([i])

    def third(i, totals):
        totals = list(totals)
        waiting = None

        def add(t, l, here, img2):
            residual = res_s[t, l, here, :]
            img1 = img_s[t, l, here, :]
            products = (residual * img1, img1 * img1, residual * img2, img1 * img2, img2 * img2)
            for n, product in enumerate(products):
                totals[n] = totals[n] + product

        for n in range(16):
            row = pl.multiple_of((16 * i + n) * SUB + base, SUB)
            here = pl.ds(row, SUB)
            for t in range(blocks):
                values = []
                image = stencil(part_s, row, t, tiles, levels, coefs_at(t, row), lane, True)
                for l, value in enumerate(image):
                    values.append(value)
                    if waiting:
                        add(waiting[0], l, waiting[1], waiting[2][l])
                waiting = (t, here, values)
        for l in range(levels):
            add(waiting[0], l, waiting[1], waiting[2][l])
        return tuple(totals)

    zero = jnp.zeros((SUB, LANES), F32)
    totals = lax.fori_loop(0, row_tiles // 16, third, (zero,) * 5, unroll=1)

    width = message.shape[1]
    surface_rows = pl.ds(base, rows)
    forces = jnp.zeros((SUB, width), F32)
    for t in range(blocks):
        for q, field in enumerate((dir_s, part_s)):
            surface = field[t, 0, surface_rows, :].T
            sums = [
                jnp.sum(modes_t[t, k] * surface, axis=0, keepdims=True) for k in range(mode_count)
            ]
            sums.append(jnp.zeros((SUB - mode_count, rows), F32))
            share = exact_dot(jnp.concatenate(sums, axis=0), hits_t[t])
            forces = forces + (pltpu.roll(share, body_total, 1) if q else share)
    wide_sub = iota((SUB, width), 0)
    gathered = jnp.zeros((SUB, LANES), F32)
    for q, total in enumerate(totals):
        gathered = jnp.where(lane == q, jnp.sum(total, axis=1, keepdims=True), gathered)
    gathered = jnp.sum(gathered, axis=0, keepdims=True)
    if width > LANES:
        gathered = jnp.concatenate([gathered, jnp.zeros((1, width - LANES), F32)], axis=1)
    message[0:SUB, :] = jnp.where(wide_sub == SUB - 2, gathered, forces)
    message[SUB:, :] = table[...]


def mix_level(mix, weighted, l):
    total = (mix[l, l] + 1.0) * weighted[l]
    for m, value in enumerate(weighted):
        if m != l:
            total = total + mix[l, m] * value
    return total


def mix_levels(mix, weighted, levels):
    return [mix_level(mix, weighted, l) for l in range(levels)]


def body_hits(bodies_t, block, count, width):
    ids = bodies_t[block : block + 1, :]
    ids = jnp.where(ids < count, ids, -1)
    wanted = lax.broadcasted_iota(jnp.int32, (width, ids.shape[1]), 0)
    return (jnp.broadcast_to(ids, wanted.shape) == wanted).astype(F32)


def dot_nt(a, b):
    return lax.dot_general(
        a, b, (((1,), (1,)), ((), ())), precision=lax.Precision.HIGHEST, preferred_element_type=F32
    )


def exact_dot(values, ones):
    high = values.astype(jnp.bfloat16).astype(F32)
    rest = values - high
    middle = rest.astype(jnp.bfloat16).astype(F32)
    parts = jnp.concatenate([high, middle, rest - middle, jnp.zeros_like(high)], axis=0)
    shares = jnp.dot(
        parts.astype(jnp.bfloat16), ones.astype(jnp.bfloat16), preferred_element_type=F32
    )
    return shares[0:SUB] + (shares[SUB : 2 * SUB] + shares[2 * SUB : 3 * SUB])


def last_kernel(
    body_total,
    message,
    phi,
    direction,
    part,
    modes_t,
    hits,
    potential,
    velocity_t,
    flux,
    phi_s,
    flux_s,
    velocity_s,
    out_sems,
):
    levels, rows, cols = phi.shape
    blocks, mode_count = modes_t.shape[0:2]
    width = message.shape[1]
    owned = velocity_t.shape[0]
    main = pl.ds(2 * SUB, rows)
    top = message[0:SUB, :]

    def scalar(q):
        return top[SUB - 2 : SUB - 1, q : q + 1]

    cross_first, square_first, cross_mixed, square_mixed, square_second = [
        scalar(q) for q in range(5)
    ]
    first_step = cross_first / square_first
    next_top = (
        cross_first
        - first_step * cross_mixed
        - first_step * square_first
        + first_step * first_step * square_mixed
    )
    next_bottom = (
        square_first - 2.0 * first_step * square_mixed + first_step * first_step * square_second
    )
    second_step = next_top / next_bottom
    on_dir = first_step + second_step
    on_part = first_step * second_step
    outgoing = []

    def send(src, dst):
        copy = pltpu.make_async_copy(src, dst, out_sems.at[len(outgoing)])
        copy.start()
        outgoing.append(copy)


    for l in range(levels):
        for t in range(blocks):
            lanes = pl.ds(t * LANES, LANES)
            change = on_dir * direction[t, l, main, :] - on_part * part[t, l, main, :]
            phi_s[l, :, lanes] = phi[l, :, lanes] + change
        send(phi_s.at[l], potential.at[l])

    wide_sub, wide_lane = iota((SUB, width), 0), iota((SUB, width), 1)
    foot_scale = 1.0 / math.sqrt(FOOT)
    forces = foot_scale * (on_part * pltpu.roll(top, body_total, 1) - on_dir * top)
    forces = jnp.where(wide_sub == mode_count, 1.0, forces)
    forces = jnp.where(wide_lane < body_total, forces, 0.0)
    velocity = jnp.zeros((SUB, width), F32)
    for k in range(mode_count):
        table = message[(k // 2 + 1) * SUB : (k // 2 + 2) * SUB, :]
        if k % 2:
            table = pltpu.roll(table, body_total, 1)
        value = jnp.sum(table * forces, axis=0, keepdims=True)
        velocity = jnp.where(wide_sub == k, value, velocity)
    per_row = [exact_dot(velocity, hits[t]) for t in range(blocks)]

    me = (lax.axis_index("gx") * lax.axis_size("gy") + lax.axis_index("gy")) * owned
    mine = ((wide_lane == me + wide_sub) & (wide_sub < owned)).astype(F32)
    velocity_s[...] = dot_nt(mine, velocity)[0:owned, 0:mode_count]
    send(velocity_s, velocity_t)
    for t in range(blocks):
        total = modes_t[t, 0] * per_row[t][0:1, :]
        for k in range(1, mode_count):
            total = total + modes_t[t, k] * per_row[t][k : k + 1, :]
        flux_s[:, t * LANES : (t + 1) * LANES] = total.T
    send(flux_s, flux)
    for copy in outgoing:
        copy.wait()


def swap_near(value, axis):
    size = lax.axis_size(axis)
    return lax.ppermute(value, axis, [(i, i ^ 1) for i in range(size)])


def swap_far(value, axis):
    size = lax.axis_size(axis)
    pairs = [(i, i + 1) for i in range(1, size - 1, 2)]
    return lax.ppermute(value, axis, pairs + [(j, i) for i, j in pairs])


def sum_over(value, axis, together):
    size = lax.axis_size(axis)
    step = 1
    while step < size:
        count = min(together, size // step)
        total = value
        for n in range(1, count):
            pairs = [(i, i ^ (n * step)) for i in range(size)]
            total = total + lax.ppermute(value, axis, pairs)
        value = total
        step *= count
    return value


def per_device(
    forcing,
    start_potential,
    horiz_coef,
    vert_coef,
    vert_mix,
    mode_shapes,
    block_body,
    response,
    velocity_old,
):
    levels, rows, cols = forcing.shape
    mode_count = mode_shapes.shape[0]
    blocks = cols // LANES
    tiles = blocks + 1
    padded = rows + 4 * SUB
    owned = velocity_old.shape[1]
    body_total = owned * lax.axis_size(("gx", "gy"))
    width = 2 * body_total
    bodies_t = block_body.T
    response_t = jnp.swapaxes(response, 1, 2)
    old_t = velocity_old.T
    limit = pltpu.CompilerParams(vmem_limit_bytes=24 * 2**20)

    def call(kernel, name, outs, ins, args, scratch=()):
        return pl.pallas_call(
            kernel,
            out_shape=tuple(jax.ShapeDtypeStruct(shape, F32) for shape, _ in outs),
            in_specs=ins,
            out_specs=tuple(spec for _, spec in outs),
            scratch_shapes=list(scratch),
            compiler_params=limit,
            name=name,
        )(*args)

    strip = (levels + 1, SUB, cols)
    inner = (blocks, levels, rows, LANES)
    near, far = call(
        strip_kernel,
        "strip_kernel",
        [(strip, VMEM), (strip, VMEM)],
        [HBM] * 4,
        [
            pltpu.with_memory_space_constraint(value, pltpu.HBM)
            for value in (start_potential, forcing, horiz_coef, vert_coef)
        ],
        [
            pltpu.VMEM((2, blocks, levels, 3 * SUB, LANES), F32),
            pltpu.VMEM((2, blocks, levels, SUB, LANES), F32),
            pltpu.VMEM((2, SUB, cols), F32),
            pltpu.VMEM((2, SUB, cols), F32),
            pltpu.SemaphoreType.DMA((4 + 4 * blocks,)),
        ],
    )
    row_near, row_far = swap_near(near, "gx"), swap_far(far, "gx")
    packed_shape = (rows + 2 * SUB, LANES)
    res, packed, table = call(
        functools.partial(inner_kernel, body_total),
        "inner_kernel",
        [(inner, VMEM), (packed_shape, VMEM), ((3 * SUB, width), VMEM)],
        [VMEM] * 6,
        (start_potential, forcing, horiz_coef, vert_coef, response_t, old_t),
        [
            pltpu.VMEM((blocks, levels, rows + 2 * SUB, LANES), F32),
            pltpu.VMEM((LANES, LANES), F32),
        ],
    )
    strip = (rows // 2 + SUB, LANES)
    edge, edge_coef, own, near, far = call(
        edge_kernel,
        "edge_kernel",
        [
            ((4, blocks, levels, SUB, LANES), VMEM),
            ((2, 2, blocks, SUB, LANES), VMEM),
            (packed_shape, VMEM),
            (strip, VMEM),
            (strip, VMEM),
        ],
        [VMEM] * 7,
        (res, start_potential, horiz_coef, vert_coef, row_near, row_far, packed),
    )
    col_near, col_far = swap_near(near, "gy"), swap_far(far, "gy")
    field = (tiles, levels, padded, LANES)
    early_field = (blocks, levels, padded, LANES)
    plane = (blocks, padded, LANES)
    modes_t, hits, hits_t, early, res_own, horiz, vert, scale = call(
        functools.partial(ahead_kernel, body_total),
        "ahead_kernel",
        [((blocks, mode_count, LANES, rows), VMEM), ((blocks, width, rows), VMEM), ((blocks, rows, width), VMEM)]
        + [(early_field, VMEM)] * 2
        + [(plane, VMEM)] * 3,
        [VMEM] * 5 + [SMEM] + [VMEM] * 2,
        (res, edge, horiz_coef, vert_coef, edge_coef, vert_mix, mode_shapes, bodies_t),
    )

    side_plane = pltpu.VMEM((padded, LANES), F32)
    direction, part, message = call(
        functools.partial(main_kernel, body_total),
        "main_kernel",
        [(field, VMEM), (field, VMEM), ((4 * SUB, width), VMEM)],
        [VMEM] * 9 + [SMEM] + [VMEM] * 2,
        (
            early,
            res_own,
            horiz,
            vert,
            scale,
            own,
            col_near,
            col_far,
            table,
            vert_mix,
            modes_t,
            hits_t,
        ),
        [
            pltpu.VMEM((blocks, levels, padded, LANES), F32),
            pltpu.VMEM(field, F32),
            side_plane,
            side_plane,
            side_plane,
            pltpu.VMEM(packed_shape, F32),
        ],
    )
    message = sum_over(sum_over(message, "gx", 2), "gy", 4)

    potential, velocity_t, flux = call(
        functools.partial(last_kernel, body_total),
        "last_kernel",
        [((levels, rows, cols), HBM), ((owned, mode_count), HBM), ((rows, cols), HBM)],
        [VMEM] * 6,
        (message, start_potential, direction, part, modes_t, hits),
        [
            pltpu.VMEM((levels, rows, cols), F32),
            pltpu.VMEM((rows, cols), F32),
            pltpu.VMEM((owned, mode_count), F32),
            pltpu.SemaphoreType.DMA((levels + 2,)),
        ],
    )
    return (potential, velocity_t.T, flux)


def solution(mesh):
    return jax.shard_map(
        per_device,
        mesh=mesh,
        in_specs=(
            P(None, "gx", "gy"),
            P(None, "gx", "gy"),
            P("gx", "gy"),
            P("gx", "gy"),
            P(),
            P(None, "gx", "gy"),
            P("gx", "gy"),
            P(None, None, ("gx", "gy")),
            P(None, ("gx", "gy")),
        ),
        out_specs=(P(None, "gx", "gy"), P(None, ("gx", "gy")), P("gx", "gy")),
        check_vma=False,
    )
```

```python
import functools
import math

import jax
import jax.numpy as jnp
from jax import lax
from jax.experimental import pallas as pl
from jax.experimental.pallas import tpu as pltpu
from jax.sharding import PartitionSpec as P

FOOT = 8192
LANES = 128
SUB = 8
FAR = 16.0
F32 = jnp.float32
HBM = pl.BlockSpec(memory_space=pltpu.HBM)
VMEM = pl.BlockSpec(memory_space=pltpu.VMEM)
SMEM = pl.BlockSpec(memory_space=pltpu.SMEM)


def iota(shape, dim):
    return lax.broadcasted_iota(jnp.int32, shape, dim)


def tile_at(index):
    return pl.ds(pl.multiple_of(index * SUB, SUB), SUB)


def stencil(ref, row, t, tiles, levels, coefs, lane, wrap):
    here = pl.ds(row, SUB)
    horiz, vert = coefs
    last_coef = 5.0 * horiz + vert
    mid_coef = last_coef + vert
    horiz12 = horiz * (1.0 / 12.0)
    for l in range(levels):
        x = ref[t, l, here, :]
        after = ref[(t + 1) % tiles, l, here, :] if wrap or t + 1 < tiles else 0.0
        before = ref[(t - 1) % tiles, l, here, :] if wrap or t > 0 else 0.0

        def rows_at(offset):
            return ref[t, l, pl.ds(row + offset, SUB), :]

        right1 = pltpu.roll(jnp.where(lane < 1, after, x), LANES - 1, 1)
        right2 = pltpu.roll(jnp.where(lane < 2, after, x), LANES - 2, 1)
        left1 = pltpu.roll(jnp.where(lane >= LANES - 1, before, x), 1, 1)
        left2 = pltpu.roll(jnp.where(lane >= LANES - 2, before, x), 2, 1)
        nearest = (rows_at(-1) + rows_at(1)) + (right1 + left1)
        farther = (rows_at(-2) + rows_at(2)) + (right2 + left2)
        if l == 0:
            beside = ref[t, 1, here, :]
        elif l == levels - 1:
            beside = ref[t, l - 1, here, :]
        else:
            beside = ref[t, l - 1, here, :] + ref[t, l + 1, here, :]
        coef = last_coef if l == levels - 1 else mid_coef
        yield coef * x + horiz12 * (farther - FAR * nearest) - vert * beside


def strip_kernel(phi, forcing, horiz_in, vert_in, near_out, far_out, phi_s, res_s, horiz, vert, sems):
    levels, rows, cols = phi.shape
    blocks = cols // LANES
    lane, sub = iota((SUB, LANES), 1), iota((SUB, LANES), 0)
    pairs = []
    for end, row in enumerate((0, rows - SUB)):
        here = pl.ds(row, SUB)
        pairs.append((horiz_in.at[here], horiz.at[end]))
        pairs.append((vert_in.at[here], vert.at[end]))
        for t in range(blocks):
            lanes = pl.ds(t * LANES, LANES)
            pairs.append((phi.at[:, here, lanes], phi_s.at[end, t, :, pl.ds(SUB, SUB)]))
            pairs.append((forcing.at[:, here, lanes], res_s.at[end, t]))
    copies = [pltpu.make_async_copy(a, b, sems.at[n]) for n, (a, b) in enumerate(pairs)]
    for copy in copies:
        copy.start()
    zero = jnp.zeros((SUB, LANES), F32)
    for end in range(2):
        for t in range(blocks):
            for l in range(levels):
                phi_s[end, t, l, 0:SUB, :] = zero
                phi_s[end, t, l, 2 * SUB : 3 * SUB, :] = zero
    for copy in copies:
        copy.wait()
    even = lax.rem(lax.axis_index("gx"), 2) == 0
    upper = sub < SUB // 2
    kept = []
    for end in range(2):
        coefs = [
            (horiz[end, :, t * LANES : (t + 1) * LANES], vert[end, :, t * LANES : (t + 1) * LANES])
            for t in range(blocks)
        ]
        strips = {}
        for t in range(blocks):
            image = stencil(phi_s.at[end], SUB, t, blocks, levels, coefs[t], lane, False)
            for l, value in enumerate(image):
                potential = phi_s[end, t, l, SUB : 2 * SUB, :]
                strips[t, l] = (res_s[end, t, l] - value, potential)
            strips[t, levels] = coefs[t]
        kept.append(strips)
    for place, (a_top, b_top) in kept[0].items():
        a_low, b_low = kept[1][place]
        t, l = place
        lanes = pl.ds(t * LANES, LANES)
        top = jnp.where(upper, a_top, pltpu.roll(b_top, SUB // 2, 0))
        low = jnp.where(upper, pltpu.roll(b_low, SUB // 2, 0), a_low)
        near_out[l, :, lanes] = jnp.where(even, low, top)
        far_out[l, :, lanes] = jnp.where(even, top, low)


def lane_kinds(lane, levels):
    pair = (lane >= 8 * levels) & (lane < 12 * levels)
    from_left = jnp.where(pair, lane & 2, 4 - (lane & 4)) != 0
    return pair, from_left


def coef_slot(levels):
    return (12 * levels + 7) // 8 * 8


def pack_tile(res, phi, coefs, lane):
    levels = len(res)
    packed = jnp.zeros((SUB, LANES), F32)
    slots = [(8 * l, 8, value) for l, value in enumerate(res)]
    slots += [(coef_slot(levels) + 8 * n, 8, value) for n, value in enumerate(coefs)]
    slots += [(8 * levels + 4 * l, 4, value) for l, value in enumerate(phi)]
    for low, size, value in slots:
        here = (lane >= low) & (lane < low + size)
        packed = jnp.where(here, pltpu.roll(value, low + size // 2, 1), packed)
    pair = (lane >= 8 * levels) & (lane < 12 * levels)
    after = jnp.where(pair & ((lane & 3) == 0), pltpu.roll(packed, LANES - 1, 1), 0.0)
    before = jnp.where(pair & ((lane & 3) == 3), pltpu.roll(packed, 1, 1), 0.0)
    return packed - FAR * (after + before)


def inner_kernel(
    body_total, phi, forcing, horiz, vert, response_t, old_t, res, packed, table, phi_s, small_s
):
    blocks, levels, rows, _ = res.shape
    cols = phi.shape[2]
    zero = jnp.zeros((SUB, LANES), F32)
    for t in range(blocks):
        for l in range(levels):
            phi_s[t, l, 0:SUB, :] = zero
            phi_s[t, l, rows + SUB : rows + 2 * SUB, :] = zero
            phi_s[t, l, SUB : rows + SUB, :] = phi[l, :, t * LANES : (t + 1) * LANES]
    right = pl.ds(cols - LANES, LANES)
    left = pl.ds(0, LANES)
    lane = iota((SUB, LANES), 1)
    first = lane < LANES // 2

    def residual(i, carry):
        here = tile_at(i)
        row = pl.multiple_of(i * SUB + SUB, SUB)
        for t in range(blocks):
            lanes = pl.ds(t * LANES, LANES)
            coefs = (horiz[here, lanes], vert[here, lanes])
            image = stencil(phi_s, row, t, blocks, levels, coefs, lane, False)
            for l, value in enumerate(image):
                res[t, l, here, :] = forcing[l, here, lanes] - value
        return carry

    lax.fori_loop(0, rows // SUB, residual, 0, unroll=8)

    def body(i, carry):
        here = tile_at(i)
        packed[tile_at(i + 1), :] = pack_tile(
            [jnp.where(first, res[0, l, here, :], res[blocks - 1, l, here, :]) for l in range(levels)],
            [jnp.where(first, phi[l, here, left], phi[l, here, right]) for l in range(levels)],
            [jnp.where(first, ref[here, left], ref[here, right]) for ref in (horiz, vert)],
            lane,
        )
        return carry

    lax.fori_loop(1, rows // SUB - 1, body, 0, unroll=7)

    owned, mode_count = old_t.shape
    width = table.shape[1]
    small_s[...] = jnp.zeros((LANES, LANES), F32)
    for k in range(mode_count):
        small_s[k * SUB : k * SUB + owned, 0:mode_count] = response_t[k]
        small_s[k * SUB : k * SUB + owned, mode_count : mode_count + 1] = old_t[:, k : k + 1]
    values = small_s[...].T[0:SUB, :]
    if width > LANES:
        values = jnp.concatenate([values, jnp.zeros((SUB, width - LANES), F32)], axis=1)
    wide_lane = iota((SUB, width), 1)
    me = (lax.axis_index("gx") * lax.axis_size("gy") + lax.axis_index("gy")) * owned
    for pair in range(mode_count // 2):
        tile = jnp.zeros((SUB, width), F32)
        for half in range(2):
            place = half * body_total + me
            shift = lax.rem(place - (2 * pair + half) * SUB + width, width)
            here = (wide_lane >= place) & (wide_lane < place + owned)
            tile = jnp.where(here, pltpu.roll(values, shift, 1), tile)
        table[pair * SUB : (pair + 1) * SUB, :] = tile


def edge_kernel(
    res, phi, horiz, vert, row_near, row_far, packed, edge, edge_coef, own, near_out, far_out
):
    blocks, levels, rows, _ = res.shape
    row_tiles = rows // SUB
    lane, sub = iota((SUB, LANES), 1), iota((SUB, LANES), 0)
    even = lax.rem(lax.axis_index("gx"), 2) == 0
    upper = sub < SUB // 2
    half = SUB // 2
    values = {}
    for t in range(blocks):
        lanes = pl.ds(t * LANES, LANES)
        near, far = row_near[levels, :, lanes], row_far[levels, :, lanes]
        above, below = jnp.where(even, far, near), jnp.where(even, near, far)
        h_up, v_up = jnp.where(upper, 0.0, above), jnp.where(upper, 0.0, pltpu.roll(above, half, 0))
        h_down = jnp.where(upper, below, 0.0)
        v_down = jnp.where(upper, pltpu.roll(below, half, 0), 0.0)
        edge_coef[0, 0, t], edge_coef[0, 1, t] = h_up, v_up
        edge_coef[1, 0, t], edge_coef[1, 1, t] = h_down, v_down
        first, last = pl.ds(0, SUB), pl.ds(rows - SUB, SUB)
        h_first, h_last = horiz[first, lanes], horiz[last, lanes]
        coefs = [(h_up, v_up), (h_first, vert[first, lanes]), (h_last, vert[last, lanes])]
        coefs.append((h_down, v_down))
        for n, pair in enumerate(coefs):
            values[n, t, "coef"] = pair
        scaled = [h * (1.0 / 12.0) for h, _ in coefs]

        def from_above(value):
            near_row = jnp.where(sub < 1, pltpu.roll(value, 1, 0), 0.0)
            far_row = jnp.where(sub < 2, pltpu.roll(value, 2, 0), 0.0)
            return far_row - FAR * near_row

        def from_below(value):
            near_row = jnp.where(sub >= SUB - 1, pltpu.roll(value, SUB - 1, 0), 0.0)
            far_row = jnp.where(sub >= SUB - 2, pltpu.roll(value, SUB - 2, 0), 0.0)
            return far_row - FAR * near_row

        for l in range(levels):
            near, far = row_near[l, :, lanes], row_far[l, :, lanes]
            above, below = jnp.where(even, far, near), jnp.where(even, near, far)
            res_up = jnp.where(upper, 0.0, above)
            phi_up = jnp.where(upper, 0.0, pltpu.roll(above, half, 0))
            res_down = jnp.where(upper, below, 0.0)
            phi_down = jnp.where(upper, pltpu.roll(below, half, 0), 0.0)
            phi_first, phi_last = phi[l, first, lanes], phi[l, last, lanes]
            fixed = (
                res_up - scaled[0] * from_below(phi_first),
                res[t, l, first, :] - scaled[1] * from_above(phi_up),
                res[t, l, last, :] - scaled[2] * from_below(phi_down),
                res_down - scaled[3] * from_above(phi_last),
            )
            for n, value in enumerate(fixed):
                edge[n, t, l] = value
                values[n, t, l] = value
            for n, value in enumerate((phi_up, phi_first, phi_last, phi_down)):
                values[n, t, l, "phi"] = value

    start = lane < LANES // 2
    end = blocks - 1
    tiles = [packed[i * SUB : (i + 1) * SUB, :] for i in range(row_tiles + 2)]
    for n, place in enumerate((0, 1, row_tiles, row_tiles + 1)):
        tiles[place] = pack_tile(
            [jnp.where(start, values[n, 0, l], values[n, end, l]) for l in range(levels)],
            [
                jnp.where(start, values[n, 0, l, "phi"], values[n, end, l, "phi"])
                for l in range(levels)
            ],
            [jnp.where(start, values[n, 0, "coef"][c], values[n, end, "coef"][c]) for c in range(2)],
            lane,
        )
    pair, from_left = lane_kinds(lane, levels)
    col_even = lax.rem(lax.axis_index("gy"), 2) == 0
    turned = []
    for i, tile in enumerate(tiles):
        moved = jnp.where((lane & 2) == 0, pltpu.roll(tile, LANES - 2, 1), pltpu.roll(tile, 2, 1))
        turned.append(jnp.where(pair, moved, tile))
        own[i * SUB : (i + 1) * SUB, :] = turned[i]
    fold = (row_tiles + 2) // 2
    for i in range(fold):
        other = tiles[i + fold]
        to_right = jnp.where(pair, other, pltpu.roll(other, 4, 1))
        to_right = jnp.where(from_left, turned[i], to_right)
        to_left = jnp.where(pair, other, pltpu.roll(other, LANES - 4, 1))
        to_left = jnp.where(from_left, to_left, turned[i])
        near_out[i * SUB : (i + 1) * SUB, :] = jnp.where(col_even, to_right, to_left)
        far_out[i * SUB : (i + 1) * SUB, :] = jnp.where(col_even, to_left, to_right)


def ahead_kernel(
    body_total,
    res,
    edge,
    horiz_in,
    vert_in,
    edge_coef,
    mix,
    modes,
    bodies_t,
    modes_t,
    hits,
    hits_t,
    early,
    res_own,
    horiz,
    vert,
    scale,
):
    blocks, levels, rows, _ = res.shape
    row_tiles = rows // SUB
    mode_count = modes.shape[0]
    for t in range(blocks):
        for k in range(mode_count):
            modes_t[t, k] = modes[k, :, t * LANES : (t + 1) * LANES].T
        found = body_hits(bodies_t, t, body_total, hits.shape[1])
        hits[t] = found
        hits_t[t] = found.T

    def direction(i, own, residuals, coefs):
        there = tile_at(i + 1)
        for t in range(blocks):
            h, v = coefs[t]
            bottom = 5.0 * h + 2.0 * v
            inside = bottom > 0.0
            factor = jnp.where(inside, 1.0 / jnp.where(inside, bottom, 1.0), 0.0)
            scale[t, there, :] = factor
            horiz[t, there, :] = h
            vert[t, there, :] = v
            if own:
                for l in range(levels):
                    res_own[t, l, there, :] = residuals[t][l]
            weighted = [value * factor for value in residuals[t]]
            for l, value in enumerate(mix_levels(mix, weighted, levels)):
                early[t, l, there, :] = value

    def own_coefs(i):
        here = tile_at(i)
        result = []
        for t in range(blocks):
            lanes = pl.ds(t * LANES, LANES)
            result.append((horiz_in[here, lanes], vert_in[here, lanes]))
        return result

    for n, i in enumerate((0, 1, row_tiles, row_tiles + 1)):
        own = 1 <= i <= row_tiles
        residuals = [[edge[n, t, l] for l in range(levels)] for t in range(blocks)]
        if own:
            coefs = own_coefs(i - 1)
        else:
            coefs = [(edge_coef[n // 2, 0, t], edge_coef[n // 2, 1, t]) for t in range(blocks)]
        direction(i, own, residuals, coefs)

    def body(i, carry):
        here = tile_at(i - 1)
        residuals = [[res[t, l, here, :] for l in range(levels)] for t in range(blocks)]
        direction(i, True, residuals, own_coefs(i - 1))
        return carry

    lax.fori_loop(2, row_tiles, body, 0, unroll=2)


def main_kernel(
    body_total,
    early,
    res_own,
    horiz,
    vert,
    scale,
    own,
    col_near,
    col_far,
    table,
    mix,
    modes_t,
    hits_t,
    dir_s,
    part_s,
    message,
    res_s,
    img_s,
    horiz_s,
    vert_s,
    scale_s,
    got_s,
):
    blocks, levels, padded, _ = early.shape
    rows = padded - 4 * SUB
    mode_count = modes_t.shape[1]
    tiles = blocks + 1
    side = blocks
    row_tiles = rows // SUB
    base = 2 * SUB
    lane = iota((SUB, LANES), 1)
    everything = range(tiles)

    pair, from_left = lane_kinds(lane, levels)
    even = lax.rem(lax.axis_index("gy"), 2) == 0
    fold = (row_tiles + 2) // 2
    for i in range(fold):
        here = pl.ds(i * SUB, SUB)
        near, far = col_near[here, :], col_far[here, :]
        left, right = jnp.where(even, far, near), jnp.where(even, near, far)
        got_s[here, :] = jnp.where(from_left, left, right)
        left = jnp.where(pair, pltpu.roll(left, 2, 1), pltpu.roll(left, LANES - 4, 1))
        right = jnp.where(pair, pltpu.roll(right, LANES - 2, 1), pltpu.roll(right, 4, 1))
        there = pl.ds((i + fold) * SUB, SUB)
        got_s[there, :] = jnp.where(from_left, left, right)

    halo = (lane < 4) | (lane >= LANES - 4)
    half = LANES // 2
    slot = coef_slot(levels)

    def first(group, inner):
        starts, ends = lane < 2, lane >= LANES - 2
        weighted = []
        for i in group:
            there, here = tile_at(i + 1), tile_at(i)
            got, mine = got_s[here, :], own[here, :]
            h, v = [
                jnp.where(halo, pltpu.roll(got, (LANES - 4 - slot - 8 * n) % LANES, 1), 0.0)
                for n in range(2)
            ]
            bottom = 5.0 * h + 2.0 * v
            inside = bottom > 0.0
            factor = jnp.where(inside, 1.0 / jnp.where(inside, bottom, 1.0), 0.0)
            scale_s[there, :] = factor
            horiz_s[there, :] = h
            vert_s[there, :] = v
            side_edge = jnp.where(starts | ends, h * (factor * (1.0 / 12.0)), 0.0)
            first_edge = jnp.where(starts, horiz[0, there, :] * (1.0 / 12.0), 0.0)
            last_edge = jnp.where(ends, horiz[side - 1, there, :] * (1.0 / 12.0), 0.0)
            both = first_edge * scale[0, there, :] + last_edge * scale[side - 1, there, :]
            both = pltpu.roll(both, half, 1)
            values = []
            for l in range(levels):
                place = (LANES - 2 - 8 * levels - 4 * l) % LANES
                ours = pltpu.roll(mine, place, 1)
                beyond = pltpu.roll(got, (LANES - 4 - 8 * l) % LANES, 1)
                across = pltpu.roll(got, (place + half) % LANES, 1)
                values.append(beyond * factor - side_edge * ours - both * across)
                if inner:
                    theirs = pltpu.roll(got, place, 1)
                    terms = [jnp.zeros_like(theirs)] * blocks
                    terms[0] = terms[0] + first_edge * theirs
                    terms[-1] = terms[-1] + last_edge * theirs
                    for t in range(blocks):
                        res_s[t, l, there, :] = res_own[t, l, there, :] - terms[t]
            weighted.append(values)
        mixed = [mix_levels(mix, values, levels) for values in weighted]
        turned = [[pltpu.roll(value, half, 1) for value in values] for values in mixed]
        for n, i in enumerate(group):
            there = tile_at(i + 1)
            for l in range(levels):
                dir_s[side, l, there, :] = mixed[n][l]
                changes = [jnp.zeros((SUB, LANES), F32)] * blocks
                changes[0] = changes[0] + jnp.where(starts, turned[n][l], 0.0)
                changes[-1] = changes[-1] + jnp.where(ends, turned[n][l], 0.0)
                for t in range(blocks):
                    dir_s[t, l, there, :] = early[t, l, there, :] + changes[t]

    first([0, row_tiles + 1], False)
    first(range(1, row_tiles + 1), True)

    def coefs_at(t, row):
        here = pl.ds(row, SUB)
        if t == side:
            return horiz_s[here, :], vert_s[here, :]
        return horiz[t, here, :], vert[t, here, :]

    def second(group):
        rows_of = [pl.multiple_of(i * SUB + SUB, SUB) for i in group]
        waiting = None
        for row in rows_of:
            for t in everything:
                here = pl.ds(row, SUB)
                factor = scale_s[here, :] if t == side else scale[t, here, :]
                weighted = []
                image = stencil(dir_s, row, t, tiles, levels, coefs_at(t, row), lane, True)
                for l, value in enumerate(image):
                    img_s[t, l, here, :] = value
                    weighted.append(value * factor)
                    if waiting:
                        part_s[waiting[0], l, waiting[1], :] = mix_level(mix, waiting[2], l)
                waiting = (t, here, weighted)
        for l in range(levels):
            part_s[waiting[0], l, waiting[1], :] = mix_level(mix, waiting[2], l)

    def second_body(i, carry):
        second([9 * i + n for n in range(9)])
        return carry

    lax.fori_loop(0, (row_tiles + 2) // 9, second_body, 0, unroll=1)
    for i in range((row_tiles + 2) // 9 * 9, row_tiles + 2):
        second([i])

    def third(totals):
        totals = list(totals)
        waiting = None

        def add(t, l, here, img2):
            residual = res_s[t, l, here, :]
            img1 = img_s[t, l, here, :]
            products = (residual * img1, img1 * img1, residual * img2, img1 * img2, img2 * img2)
            for n, product in enumerate(products):
                totals[n] = totals[n] + product

        for i in range(row_tiles):
            row = i * SUB + base
            here = pl.ds(row, SUB)
            for t in range(blocks):
                values = []
                image = stencil(part_s, row, t, tiles, levels, coefs_at(t, row), lane, True)
                for l, value in enumerate(image):
                    values.append(value)
                    if waiting:
                        add(waiting[0], l, waiting[1], waiting[2][l])
                waiting = (t, here, values)
        for l in range(levels):
            add(waiting[0], l, waiting[1], waiting[2][l])
        return tuple(totals)

    zero = jnp.zeros((SUB, LANES), F32)
    totals = third((zero,) * 5)

    width = message.shape[1]
    surface_rows = pl.ds(base, rows)
    forces = jnp.zeros((SUB, width), F32)
    for t in range(blocks):
        for q, field in enumerate((dir_s, part_s)):
            surface = field[t, 0, surface_rows, :].T
            sums = [
                jnp.sum(modes_t[t, k] * surface, axis=0, keepdims=True) for k in range(mode_count)
            ]
            sums.append(jnp.zeros((SUB - mode_count, rows), F32))
            share = exact_dot(jnp.concatenate(sums, axis=0), hits_t[t])
            forces = forces + (pltpu.roll(share, body_total, 1) if q else share)
    wide_sub = iota((SUB, width), 0)
    gathered = jnp.zeros((SUB, LANES), F32)
    for q, total in enumerate(totals):
        gathered = jnp.where(lane == q, jnp.sum(total, axis=1, keepdims=True), gathered)
    gathered = jnp.sum(gathered, axis=0, keepdims=True)
    if width > LANES:
        gathered = jnp.concatenate([gathered, jnp.zeros((1, width - LANES), F32)], axis=1)
    message[0:SUB, :] = jnp.where(wide_sub == SUB - 2, gathered, forces)
    message[SUB:, :] = table[...]


def mix_level(mix, weighted, l):
    total = (mix[l, l] + 1.0) * weighted[l]
    for m, value in enumerate(weighted):
        if m != l:
            total = total + mix[l, m] * value
    return total


def mix_levels(mix, weighted, levels):
    return [mix_level(mix, weighted, l) for l in range(levels)]


def body_hits(bodies_t, block, count, width):
    ids = bodies_t[block : block + 1, :]
    ids = jnp.where(ids < count, ids, -1)
    wanted = lax.broadcasted_iota(jnp.int32, (width, ids.shape[1]), 0)
    return (jnp.broadcast_to(ids, wanted.shape) == wanted).astype(F32)


def dot_nt(a, b):
    return lax.dot_general(
        a, b, (((1,), (1,)), ((), ())), precision=lax.Precision.HIGHEST, preferred_element_type=F32
    )


def exact_dot(values, ones):
    high = values.astype(jnp.bfloat16).astype(F32)
    rest = values - high
    middle = rest.astype(jnp.bfloat16).astype(F32)
    parts = jnp.concatenate([high, middle, rest - middle, jnp.zeros_like(high)], axis=0)
    shares = jnp.dot(
        parts.astype(jnp.bfloat16), ones.astype(jnp.bfloat16), preferred_element_type=F32
    )
    return shares[0:SUB] + (shares[SUB : 2 * SUB] + shares[2 * SUB : 3 * SUB])


def last_kernel(
    body_total,
    message,
    phi,
    direction,
    part,
    modes_t,
    hits,
    potential,
    velocity_t,
    flux,
    phi_s,
    flux_s,
    velocity_s,
    out_sems,
):
    levels, rows, cols = phi.shape
    blocks, mode_count = modes_t.shape[0:2]
    width = message.shape[1]
    owned = velocity_t.shape[0]
    main = pl.ds(2 * SUB, rows)
    top = message[0:SUB, :]

    def scalar(q):
        return top[SUB - 2 : SUB - 1, q : q + 1]

    cross_first, square_first, cross_mixed, square_mixed, square_second = [
        scalar(q) for q in range(5)
    ]
    first_step = cross_first / square_first
    next_top = (
        cross_first
        - first_step * cross_mixed
        - first_step * square_first
        + first_step * first_step * square_mixed
    )
    next_bottom = (
        square_first - 2.0 * first_step * square_mixed + first_step * first_step * square_second
    )
    second_step = next_top / next_bottom
    on_dir = first_step + second_step
    on_part = first_step * second_step
    outgoing = []

    def send(src, dst):
        copy = pltpu.make_async_copy(src, dst, out_sems.at[len(outgoing)])
        copy.start()
        outgoing.append(copy)


    for l in range(levels):
        for t in range(blocks):
            lanes = pl.ds(t * LANES, LANES)
            change = on_dir * direction[t, l, main, :] - on_part * part[t, l, main, :]
            phi_s[l, :, lanes] = phi[l, :, lanes] + change
        send(phi_s.at[l], potential.at[l])

    wide_sub, wide_lane = iota((SUB, width), 0), iota((SUB, width), 1)
    foot_scale = 1.0 / math.sqrt(FOOT)
    forces = foot_scale * (on_part * pltpu.roll(top, body_total, 1) - on_dir * top)
    forces = jnp.where(wide_sub == mode_count, 1.0, forces)
    forces = jnp.where(wide_lane < body_total, forces, 0.0)
    velocity = jnp.zeros((SUB, width), F32)
    for k in range(mode_count):
        table = message[(k // 2 + 1) * SUB : (k // 2 + 2) * SUB, :]
        if k % 2:
            table = pltpu.roll(table, body_total, 1)
        value = jnp.sum(table * forces, axis=0, keepdims=True)
        velocity = jnp.where(wide_sub == k, value, velocity)
    per_row = [exact_dot(velocity, hits[t]) for t in range(blocks)]

    me = (lax.axis_index("gx") * lax.axis_size("gy") + lax.axis_index("gy")) * owned
    mine = ((wide_lane == me + wide_sub) & (wide_sub < owned)).astype(F32)
    velocity_s[...] = dot_nt(mine, velocity)[0:owned, 0:mode_count]
    send(velocity_s, velocity_t)
    for t in range(blocks):
        total = modes_t[t, 0] * per_row[t][0:1, :]
        for k in range(1, mode_count):
            total = total + modes_t[t, k] * per_row[t][k : k + 1, :]
        flux_s[:, t * LANES : (t + 1) * LANES] = total.T
    send(flux_s, flux)
    for copy in outgoing:
        copy.wait()


def swap_near(value, axis):
    size = lax.axis_size(axis)
    return lax.ppermute(value, axis, [(i, i ^ 1) for i in range(size)])


def swap_far(value, axis):
    size = lax.axis_size(axis)
    pairs = [(i, i + 1) for i in range(1, size - 1, 2)]
    return lax.ppermute(value, axis, pairs + [(j, i) for i, j in pairs])


def sum_over(value, axis, together):
    size = lax.axis_size(axis)
    step = 1
    while step < size:
        count = min(together, size // step)
        total = value
        for n in range(1, count):
            pairs = [(i, i ^ (n * step)) for i in range(size)]
            total = total + lax.ppermute(value, axis, pairs)
        value = total
        step *= count
    return value


def per_device(
    forcing,
    start_potential,
    horiz_coef,
    vert_coef,
    vert_mix,
    mode_shapes,
    block_body,
    response,
    velocity_old,
):
    levels, rows, cols = forcing.shape
    mode_count = mode_shapes.shape[0]
    blocks = cols // LANES
    tiles = blocks + 1
    padded = rows + 4 * SUB
    owned = velocity_old.shape[1]
    body_total = owned * lax.axis_size(("gx", "gy"))
    width = 2 * body_total
    bodies_t = block_body.T
    response_t = jnp.swapaxes(response, 1, 2)
    old_t = velocity_old.T
    limit = pltpu.CompilerParams(vmem_limit_bytes=24 * 2**20)

    def call(kernel, name, outs, ins, args, scratch=()):
        return pl.pallas_call(
            kernel,
            out_shape=tuple(jax.ShapeDtypeStruct(shape, F32) for shape, _ in outs),
            in_specs=ins,
            out_specs=tuple(spec for _, spec in outs),
            scratch_shapes=list(scratch),
            compiler_params=limit,
            name=name,
        )(*args)

    strip = (levels + 1, SUB, cols)
    inner = (blocks, levels, rows, LANES)
    near, far = call(
        strip_kernel,
        "strip_kernel",
        [(strip, VMEM), (strip, VMEM)],
        [HBM] * 4,
        [
            pltpu.with_memory_space_constraint(value, pltpu.HBM)
            for value in (start_potential, forcing, horiz_coef, vert_coef)
        ],
        [
            pltpu.VMEM((2, blocks, levels, 3 * SUB, LANES), F32),
            pltpu.VMEM((2, blocks, levels, SUB, LANES), F32),
            pltpu.VMEM((2, SUB, cols), F32),
            pltpu.VMEM((2, SUB, cols), F32),
            pltpu.SemaphoreType.DMA((4 + 4 * blocks,)),
        ],
    )
    row_near, row_far = swap_near(near, "gx"), swap_far(far, "gx")
    packed_shape = (rows + 2 * SUB, LANES)
    res, packed, table = call(
        functools.partial(inner_kernel, body_total),
        "inner_kernel",
        [(inner, VMEM), (packed_shape, VMEM), ((3 * SUB, width), VMEM)],
        [VMEM] * 6,
        (start_potential, forcing, horiz_coef, vert_coef, response_t, old_t),
        [
            pltpu.VMEM((blocks, levels, rows + 2 * SUB, LANES), F32),
            pltpu.VMEM((LANES, LANES), F32),
        ],
    )
    strip = (rows // 2 + SUB, LANES)
    edge, edge_coef, own, near, far = call(
        edge_kernel,
        "edge_kernel",
        [
            ((4, blocks, levels, SUB, LANES), VMEM),
            ((2, 2, blocks, SUB, LANES), VMEM),
            (packed_shape, VMEM),
            (strip, VMEM),
            (strip, VMEM),
        ],
        [VMEM] * 7,
        (res, start_potential, horiz_coef, vert_coef, row_near, row_far, packed),
    )
    col_near, col_far = swap_near(near, "gy"), swap_far(far, "gy")
    field = (tiles, levels, padded, LANES)
    early_field = (blocks, levels, padded, LANES)
    plane = (blocks, padded, LANES)
    modes_t, hits, hits_t, early, res_own, horiz, vert, scale = call(
        functools.partial(ahead_kernel, body_total),
        "ahead_kernel",
        [((blocks, mode_count, LANES, rows), VMEM), ((blocks, width, rows), VMEM), ((blocks, rows, width), VMEM)]
        + [(early_field, VMEM)] * 2
        + [(plane, VMEM)] * 3,
        [VMEM] * 5 + [SMEM] + [VMEM] * 2,
        (res, edge, horiz_coef, vert_coef, edge_coef, vert_mix, mode_shapes, bodies_t),
    )

    side_plane = pltpu.VMEM((padded, LANES), F32)
    direction, part, message = call(
        functools.partial(main_kernel, body_total),
        "main_kernel",
        [(field, VMEM), (field, VMEM), ((4 * SUB, width), VMEM)],
        [VMEM] * 9 + [SMEM] + [VMEM] * 2,
        (
            early,
            res_own,
            horiz,
            vert,
            scale,
            own,
            col_near,
            col_far,
            table,
            vert_mix,
            modes_t,
            hits_t,
        ),
        [
            pltpu.VMEM((blocks, levels, padded, LANES), F32),
            pltpu.VMEM(field, F32),
            side_plane,
            side_plane,
            side_plane,
            pltpu.VMEM(packed_shape, F32),
        ],
    )
    message = sum_over(sum_over(message, "gx", 2), "gy", 4)

    potential, velocity_t, flux = call(
        functools.partial(last_kernel, body_total),
        "last_kernel",
        [((levels, rows, cols), HBM), ((owned, mode_count), HBM), ((rows, cols), HBM)],
        [VMEM] * 6,
        (message, start_potential, direction, part, modes_t, hits),
        [
            pltpu.VMEM((levels, rows, cols), F32),
            pltpu.VMEM((rows, cols), F32),
            pltpu.VMEM((owned, mode_count), F32),
            pltpu.SemaphoreType.DMA((levels + 2,)),
        ],
    )
    return (potential, velocity_t.T, flux)


def solution(mesh):
    return jax.shard_map(
        per_device,
        mesh=mesh,
        in_specs=(
            P(None, "gx", "gy"),
            P(None, "gx", "gy"),
            P("gx", "gy"),
            P("gx", "gy"),
            P(),
            P(None, "gx", "gy"),
            P("gx", "gy"),
            P(None, None, ("gx", "gy")),
            P(None, ("gx", "gy")),
        ),
        out_specs=(P(None, "gx", "gy"), P(None, ("gx", "gy")), P("gx", "gy")),
        check_vma=False,
    )
```

```python
import functools
import math

import jax
import jax.numpy as jnp
from jax import lax
from jax.experimental import pallas as pl
from jax.experimental.pallas import tpu as pltpu
from jax.sharding import PartitionSpec as P

FOOT = 8192
LANES = 128
SUB = 8
FAR = 16.0
F32 = jnp.float32
HBM = pl.BlockSpec(memory_space=pltpu.HBM)
VMEM = pl.BlockSpec(memory_space=pltpu.VMEM)
SMEM = pl.BlockSpec(memory_space=pltpu.SMEM)


def iota(shape, dim):
    return lax.broadcasted_iota(jnp.int32, shape, dim)


def tile_at(index):
    return pl.ds(pl.multiple_of(index * SUB, SUB), SUB)


def stencil(ref, row, t, tiles, levels, coefs, lane, wrap):
    here = pl.ds(row, SUB)
    horiz, vert = coefs
    last_coef = 5.0 * horiz + vert
    mid_coef = last_coef + vert
    horiz12 = horiz * (1.0 / 12.0)
    for l in range(levels):
        x = ref[t, l, here, :]
        after = ref[(t + 1) % tiles, l, here, :] if wrap or t + 1 < tiles else 0.0
        before = ref[(t - 1) % tiles, l, here, :] if wrap or t > 0 else 0.0

        def rows_at(offset):
            return ref[t, l, pl.ds(row + offset, SUB), :]

        right1 = pltpu.roll(jnp.where(lane < 1, after, x), LANES - 1, 1)
        right2 = pltpu.roll(jnp.where(lane < 2, after, x), LANES - 2, 1)
        left1 = pltpu.roll(jnp.where(lane >= LANES - 1, before, x), 1, 1)
        left2 = pltpu.roll(jnp.where(lane >= LANES - 2, before, x), 2, 1)
        nearest = (rows_at(-1) + rows_at(1)) + (right1 + left1)
        farther = (rows_at(-2) + rows_at(2)) + (right2 + left2)
        if l == 0:
            beside = ref[t, 1, here, :]
        elif l == levels - 1:
            beside = ref[t, l - 1, here, :]
        else:
            beside = ref[t, l - 1, here, :] + ref[t, l + 1, here, :]
        coef = last_coef if l == levels - 1 else mid_coef
        yield coef * x + horiz12 * (farther - FAR * nearest) - vert * beside


def strip_kernel(phi, forcing, horiz_in, vert_in, near_out, far_out, phi_s, res_s, horiz, vert, sems):
    levels, rows, cols = phi.shape
    blocks = cols // LANES
    lane, sub = iota((SUB, LANES), 1), iota((SUB, LANES), 0)
    pairs = []
    for end, row in enumerate((0, rows - SUB)):
        here = pl.ds(row, SUB)
        pairs.append((horiz_in.at[here], horiz.at[end]))
        pairs.append((vert_in.at[here], vert.at[end]))
        for t in range(blocks):
            lanes = pl.ds(t * LANES, LANES)
            pairs.append((phi.at[:, here, lanes], phi_s.at[end, t, :, pl.ds(SUB, SUB)]))
            pairs.append((forcing.at[:, here, lanes], res_s.at[end, t]))
    copies = [pltpu.make_async_copy(a, b, sems.at[n]) for n, (a, b) in enumerate(pairs)]
    for copy in copies:
        copy.start()
    zero = jnp.zeros((SUB, LANES), F32)
    for end in range(2):
        for t in range(blocks):
            for l in range(levels):
                phi_s[end, t, l, 0:SUB, :] = zero
                phi_s[end, t, l, 2 * SUB : 3 * SUB, :] = zero
    for copy in copies:
        copy.wait()
    even = lax.rem(lax.axis_index("gx"), 2) == 0
    upper = sub < SUB // 2
    kept = []
    for end in range(2):
        coefs = [
            (horiz[end, :, t * LANES : (t + 1) * LANES], vert[end, :, t * LANES : (t + 1) * LANES])
            for t in range(blocks)
        ]
        strips = {}
        for t in range(blocks):
            image = stencil(phi_s.at[end], SUB, t, blocks, levels, coefs[t], lane, False)
            for l, value in enumerate(image):
                potential = phi_s[end, t, l, SUB : 2 * SUB, :]
                strips[t, l] = (res_s[end, t, l] - value, potential)
            strips[t, levels] = coefs[t]
        kept.append(strips)
    for place, (a_top, b_top) in kept[0].items():
        a_low, b_low = kept[1][place]
        t, l = place
        lanes = pl.ds(t * LANES, LANES)
        top = jnp.where(upper, a_top, pltpu.roll(b_top, SUB // 2, 0))
        low = jnp.where(upper, pltpu.roll(b_low, SUB // 2, 0), a_low)
        near_out[l, :, lanes] = jnp.where(even, low, top)
        far_out[l, :, lanes] = jnp.where(even, top, low)


def lane_kinds(lane, levels):
    pair = (lane >= 8 * levels) & (lane < 12 * levels)
    from_left = jnp.where(pair, lane & 2, 4 - (lane & 4)) != 0
    return pair, from_left


def coef_slot(levels):
    return (12 * levels + 7) // 8 * 8


def pack_tile(res, phi, coefs, lane):
    levels = len(res)
    packed = jnp.zeros((SUB, LANES), F32)
    slots = [(8 * l, 8, value) for l, value in enumerate(res)]
    slots += [(coef_slot(levels) + 8 * n, 8, value) for n, value in enumerate(coefs)]
    slots += [(8 * levels + 4 * l, 4, value) for l, value in enumerate(phi)]
    for low, size, value in slots:
        here = (lane >= low) & (lane < low + size)
        packed = jnp.where(here, pltpu.roll(value, low + size // 2, 1), packed)
    pair = (lane >= 8 * levels) & (lane < 12 * levels)
    after = jnp.where(pair & ((lane & 3) == 0), pltpu.roll(packed, LANES - 1, 1), 0.0)
    before = jnp.where(pair & ((lane & 3) == 3), pltpu.roll(packed, 1, 1), 0.0)
    return packed - FAR * (after + before)


def inner_kernel(
    body_total, phi, forcing, horiz, vert, response_t, old_t, res, packed, table, phi_s, small_s
):
    blocks, levels, rows, _ = res.shape
    cols = phi.shape[2]
    zero = jnp.zeros((SUB, LANES), F32)
    for t in range(blocks):
        for l in range(levels):
            phi_s[t, l, 0:SUB, :] = zero
            phi_s[t, l, rows + SUB : rows + 2 * SUB, :] = zero
            phi_s[t, l, SUB : rows + SUB, :] = phi[l, :, t * LANES : (t + 1) * LANES]
    right = pl.ds(cols - LANES, LANES)
    left = pl.ds(0, LANES)
    lane = iota((SUB, LANES), 1)
    first = lane < LANES // 2

    def residual(i, carry):
        here = tile_at(i)
        row = pl.multiple_of(i * SUB + SUB, SUB)
        for t in range(blocks):
            lanes = pl.ds(t * LANES, LANES)
            coefs = (horiz[here, lanes], vert[here, lanes])
            image = stencil(phi_s, row, t, blocks, levels, coefs, lane, False)
            for l, value in enumerate(image):
                res[t, l, here, :] = forcing[l, here, lanes] - value
        return carry

    lax.fori_loop(0, rows // SUB, residual, 0, unroll=8)

    def body(i, carry):
        here = tile_at(i)
        packed[tile_at(i + 1), :] = pack_tile(
            [jnp.where(first, res[0, l, here, :], res[blocks - 1, l, here, :]) for l in range(levels)],
            [jnp.where(first, phi[l, here, left], phi[l, here, right]) for l in range(levels)],
            [jnp.where(first, ref[here, left], ref[here, right]) for ref in (horiz, vert)],
            lane,
        )
        return carry

    lax.fori_loop(1, rows // SUB - 1, body, 0, unroll=7)

    owned, mode_count = old_t.shape
    width = table.shape[1]
    small_s[...] = jnp.zeros((LANES, LANES), F32)
    for k in range(mode_count):
        small_s[k * SUB : k * SUB + owned, 0:mode_count] = response_t[k]
        small_s[k * SUB : k * SUB + owned, mode_count : mode_count + 1] = old_t[:, k : k + 1]
    values = small_s[...].T[0:SUB, :]
    if width > LANES:
        values = jnp.concatenate([values, jnp.zeros((SUB, width - LANES), F32)], axis=1)
    wide_lane = iota((SUB, width), 1)
    me = (lax.axis_index("gx") * lax.axis_size("gy") + lax.axis_index("gy")) * owned
    for pair in range(mode_count // 2):
        tile = jnp.zeros((SUB, width), F32)
        for half in range(2):
            place = half * body_total + me
            shift = lax.rem(place - (2 * pair + half) * SUB + width, width)
            here = (wide_lane >= place) & (wide_lane < place + owned)
            tile = jnp.where(here, pltpu.roll(values, shift, 1), tile)
        table[pair * SUB : (pair + 1) * SUB, :] = tile


def edge_kernel(
    res, phi, horiz, vert, row_near, row_far, packed, edge, edge_coef, own, near_out, far_out
):
    blocks, levels, rows, _ = res.shape
    row_tiles = rows // SUB
    lane, sub = iota((SUB, LANES), 1), iota((SUB, LANES), 0)
    even = lax.rem(lax.axis_index("gx"), 2) == 0
    upper = sub < SUB // 2
    half = SUB // 2
    values = {}
    for t in range(blocks):
        lanes = pl.ds(t * LANES, LANES)
        near, far = row_near[levels, :, lanes], row_far[levels, :, lanes]
        above, below = jnp.where(even, far, near), jnp.where(even, near, far)
        h_up, v_up = jnp.where(upper, 0.0, above), jnp.where(upper, 0.0, pltpu.roll(above, half, 0))
        h_down = jnp.where(upper, below, 0.0)
        v_down = jnp.where(upper, pltpu.roll(below, half, 0), 0.0)
        edge_coef[0, 0, t], edge_coef[0, 1, t] = h_up, v_up
        edge_coef[1, 0, t], edge_coef[1, 1, t] = h_down, v_down
        first, last = pl.ds(0, SUB), pl.ds(rows - SUB, SUB)
        h_first, h_last = horiz[first, lanes], horiz[last, lanes]
        coefs = [(h_up, v_up), (h_first, vert[first, lanes]), (h_last, vert[last, lanes])]
        coefs.append((h_down, v_down))
        for n, pair in enumerate(coefs):
            values[n, t, "coef"] = pair
        scaled = [h * (1.0 / 12.0) for h, _ in coefs]

        def from_above(value):
            near_row = jnp.where(sub < 1, pltpu.roll(value, 1, 0), 0.0)
            far_row = jnp.where(sub < 2, pltpu.roll(value, 2, 0), 0.0)
            return far_row - FAR * near_row

        def from_below(value):
            near_row = jnp.where(sub >= SUB - 1, pltpu.roll(value, SUB - 1, 0), 0.0)
            far_row = jnp.where(sub >= SUB - 2, pltpu.roll(value, SUB - 2, 0), 0.0)
            return far_row - FAR * near_row

        for l in range(levels):
            near, far = row_near[l, :, lanes], row_far[l, :, lanes]
            above, below = jnp.where(even, far, near), jnp.where(even, near, far)
            res_up = jnp.where(upper, 0.0, above)
            phi_up = jnp.where(upper, 0.0, pltpu.roll(above, half, 0))
            res_down = jnp.where(upper, below, 0.0)
            phi_down = jnp.where(upper, pltpu.roll(below, half, 0), 0.0)
            phi_first, phi_last = phi[l, first, lanes], phi[l, last, lanes]
            fixed = (
                res_up - scaled[0] * from_below(phi_first),
                res[t, l, first, :] - scaled[1] * from_above(phi_up),
                res[t, l, last, :] - scaled[2] * from_below(phi_down),
                res_down - scaled[3] * from_above(phi_last),
            )
            for n, value in enumerate(fixed):
                edge[n, t, l] = value
                values[n, t, l] = value
            for n, value in enumerate((phi_up, phi_first, phi_last, phi_down)):
                values[n, t, l, "phi"] = value

    start = lane < LANES // 2
    end = blocks - 1
    tiles = [packed[i * SUB : (i + 1) * SUB, :] for i in range(row_tiles + 2)]
    for n, place in enumerate((0, 1, row_tiles, row_tiles + 1)):
        tiles[place] = pack_tile(
            [jnp.where(start, values[n, 0, l], values[n, end, l]) for l in range(levels)],
            [
                jnp.where(start, values[n, 0, l, "phi"], values[n, end, l, "phi"])
                for l in range(levels)
            ],
            [jnp.where(start, values[n, 0, "coef"][c], values[n, end, "coef"][c]) for c in range(2)],
            lane,
        )
    pair, from_left = lane_kinds(lane, levels)
    col_even = lax.rem(lax.axis_index("gy"), 2) == 0
    turned = []
    for i, tile in enumerate(tiles):
        moved = jnp.where((lane & 2) == 0, pltpu.roll(tile, LANES - 2, 1), pltpu.roll(tile, 2, 1))
        turned.append(jnp.where(pair, moved, tile))
        own[i * SUB : (i + 1) * SUB, :] = turned[i]
    fold = (row_tiles + 2) // 2
    for i in range(fold):
        other = tiles[i + fold]
        to_right = jnp.where(pair, other, pltpu.roll(other, 4, 1))
        to_right = jnp.where(from_left, turned[i], to_right)
        to_left = jnp.where(pair, other, pltpu.roll(other, LANES - 4, 1))
        to_left = jnp.where(from_left, to_left, turned[i])
        near_out[i * SUB : (i + 1) * SUB, :] = jnp.where(col_even, to_right, to_left)
        far_out[i * SUB : (i + 1) * SUB, :] = jnp.where(col_even, to_left, to_right)


def ahead_kernel(
    body_total,
    res,
    edge,
    horiz_in,
    vert_in,
    edge_coef,
    mix,
    modes,
    bodies_t,
    modes_t,
    hits,
    hits_t,
    early,
    res_own,
    horiz,
    vert,
    scale,
):
    blocks, levels, rows, _ = res.shape
    row_tiles = rows // SUB
    mode_count = modes.shape[0]
    for t in range(blocks):
        for k in range(mode_count):
            modes_t[t, k] = modes[k, :, t * LANES : (t + 1) * LANES].T
        found = body_hits(bodies_t, t, body_total, hits.shape[1])
        hits[t] = found
        hits_t[t] = found.T

    def direction(i, own, residuals, coefs):
        there = tile_at(i + 1)
        for t in range(blocks):
            h, v = coefs[t]
            bottom = 5.0 * h + 2.0 * v
            inside = bottom > 0.0
            factor = jnp.where(inside, 1.0 / jnp.where(inside, bottom, 1.0), 0.0)
            scale[t, there, :] = factor
            horiz[t, there, :] = h
            vert[t, there, :] = v
            if own:
                for l in range(levels):
                    res_own[t, l, there, :] = residuals[t][l]
            weighted = [value * factor for value in residuals[t]]
            for l, value in enumerate(mix_levels(mix, weighted, levels)):
                early[t, l, there, :] = value

    def own_coefs(i):
        here = tile_at(i)
        result = []
        for t in range(blocks):
            lanes = pl.ds(t * LANES, LANES)
            result.append((horiz_in[here, lanes], vert_in[here, lanes]))
        return result

    for n, i in enumerate((0, 1, row_tiles, row_tiles + 1)):
        own = 1 <= i <= row_tiles
        residuals = [[edge[n, t, l] for l in range(levels)] for t in range(blocks)]
        if own:
            coefs = own_coefs(i - 1)
        else:
            coefs = [(edge_coef[n // 2, 0, t], edge_coef[n // 2, 1, t]) for t in range(blocks)]
        direction(i, own, residuals, coefs)

    def body(i, carry):
        here = tile_at(i - 1)
        residuals = [[res[t, l, here, :] for l in range(levels)] for t in range(blocks)]
        direction(i, True, residuals, own_coefs(i - 1))
        return carry

    lax.fori_loop(2, row_tiles, body, 0, unroll=2)


def main_kernel(
    body_total,
    early,
    res_own,
    horiz,
    vert,
    scale,
    own,
    col_near,
    col_far,
    table,
    mix,
    modes_t,
    hits_t,
    dir_s,
    part_s,
    message,
    res_s,
    img_s,
    horiz_s,
    vert_s,
    scale_s,
    got_s,
):
    blocks, levels, padded, _ = early.shape
    rows = padded - 4 * SUB
    mode_count = modes_t.shape[1]
    tiles = blocks + 1
    side = blocks
    row_tiles = rows // SUB
    base = 2 * SUB
    lane = iota((SUB, LANES), 1)
    everything = range(tiles)

    pair, from_left = lane_kinds(lane, levels)
    even = lax.rem(lax.axis_index("gy"), 2) == 0
    fold = (row_tiles + 2) // 2
    for i in range(fold):
        here = pl.ds(i * SUB, SUB)
        near, far = col_near[here, :], col_far[here, :]
        left, right = jnp.where(even, far, near), jnp.where(even, near, far)
        got_s[here, :] = jnp.where(from_left, left, right)
        left = jnp.where(pair, pltpu.roll(left, 2, 1), pltpu.roll(left, LANES - 4, 1))
        right = jnp.where(pair, pltpu.roll(right, LANES - 2, 1), pltpu.roll(right, 4, 1))
        there = pl.ds((i + fold) * SUB, SUB)
        got_s[there, :] = jnp.where(from_left, left, right)

    halo = (lane < 4) | (lane >= LANES - 4)
    half = LANES // 2
    slot = coef_slot(levels)

    def first(group, inner):
        starts, ends = lane < 2, lane >= LANES - 2
        weighted = []
        for i in group:
            there, here = tile_at(i + 1), tile_at(i)
            got, mine = got_s[here, :], own[here, :]
            h, v = [
                jnp.where(halo, pltpu.roll(got, (LANES - 4 - slot - 8 * n) % LANES, 1), 0.0)
                for n in range(2)
            ]
            bottom = 5.0 * h + 2.0 * v
            inside = bottom > 0.0
            factor = jnp.where(inside, 1.0 / jnp.where(inside, bottom, 1.0), 0.0)
            scale_s[there, :] = factor
            horiz_s[there, :] = h
            vert_s[there, :] = v
            side_edge = jnp.where(starts | ends, h * (factor * (1.0 / 12.0)), 0.0)
            first_edge = jnp.where(starts, horiz[0, there, :] * (1.0 / 12.0), 0.0)
            last_edge = jnp.where(ends, horiz[side - 1, there, :] * (1.0 / 12.0), 0.0)
            both = first_edge * scale[0, there, :] + last_edge * scale[side - 1, there, :]
            both = pltpu.roll(both, half, 1)
            values = []
            for l in range(levels):
                place = (LANES - 2 - 8 * levels - 4 * l) % LANES
                ours = pltpu.roll(mine, place, 1)
                beyond = pltpu.roll(got, (LANES - 4 - 8 * l) % LANES, 1)
                across = pltpu.roll(got, (place + half) % LANES, 1)
                values.append(beyond * factor - side_edge * ours - both * across)
                if inner:
                    theirs = pltpu.roll(got, place, 1)
                    terms = [jnp.zeros_like(theirs)] * blocks
                    terms[0] = terms[0] + first_edge * theirs
                    terms[-1] = terms[-1] + last_edge * theirs
                    for t in range(blocks):
                        res_s[t, l, there, :] = res_own[t, l, there, :] - terms[t]
            weighted.append(values)
        mixed = [mix_levels(mix, values, levels) for values in weighted]
        turned = [[pltpu.roll(value, half, 1) for value in values] for values in mixed]
        for n, i in enumerate(group):
            there = tile_at(i + 1)
            for l in range(levels):
                dir_s[side, l, there, :] = mixed[n][l]
                changes = [jnp.zeros((SUB, LANES), F32)] * blocks
                changes[0] = changes[0] + jnp.where(starts, turned[n][l], 0.0)
                changes[-1] = changes[-1] + jnp.where(ends, turned[n][l], 0.0)
                for t in range(blocks):
                    dir_s[t, l, there, :] = early[t, l, there, :] + changes[t]

    first([0, row_tiles + 1], False)
    first(range(1, row_tiles + 1), True)

    def coefs_at(t, row):
        here = pl.ds(row, SUB)
        if t == side:
            return horiz_s[here, :], vert_s[here, :]
        return horiz[t, here, :], vert[t, here, :]

    def second(group, wanted):
        rows_of = [pl.multiple_of(i * SUB + SUB, SUB) for i in group]
        waiting = None
        for row in rows_of:
            for t in wanted:
                here = pl.ds(row, SUB)
                factor = scale_s[here, :] if t == side else scale[t, here, :]
                weighted = []
                image = stencil(dir_s, row, t, tiles, levels, coefs_at(t, row), lane, True)
                for l, value in enumerate(image):
                    img_s[t, l, here, :] = value
                    weighted.append(value * factor)
                    if waiting:
                        part_s[waiting[0], l, waiting[1], :] = mix_level(mix, waiting[2], l)
                waiting = (t, here, weighted)
        for l in range(levels):
            part_s[waiting[0], l, waiting[1], :] = mix_level(mix, waiting[2], l)

    second([0, row_tiles + 1], range(blocks))

    def second_body(i, carry):
        second([8 * i + n + 1 for n in range(8)], everything)
        return carry

    lax.fori_loop(0, row_tiles // 8, second_body, 0)
    for i in range(row_tiles // 8 * 8 + 1, row_tiles + 1):
        second([i], everything)

    def third(totals):
        totals = list(totals)
        waiting = None

        def add(t, l, here, img2):
            residual = res_s[t, l, here, :]
            img1 = img_s[t, l, here, :]
            products = (residual * img1, img1 * img1, residual * img2, img1 * img2, img2 * img2)
            for n, product in enumerate(products):
                totals[n] = totals[n] + product

        for i in range(row_tiles):
            row = i * SUB + base
            here = pl.ds(row, SUB)
            for t in range(blocks):
                values = []
                image = stencil(part_s, row, t, tiles, levels, coefs_at(t, row), lane, True)
                for l, value in enumerate(image):
                    values.append(value)
                    if waiting:
                        add(waiting[0], l, waiting[1], waiting[2][l])
                waiting = (t, here, values)
        for l in range(levels):
            add(waiting[0], l, waiting[1], waiting[2][l])
        return tuple(totals)

    zero = jnp.zeros((SUB, LANES), F32)
    totals = third((zero,) * 5)

    width = message.shape[1]
    surface_rows = pl.ds(base, rows)
    forces = jnp.zeros((SUB, width), F32)
    for t in range(blocks):
        for q, field in enumerate((dir_s, part_s)):
            surface = field[t, 0, surface_rows, :].T
            sums = [
                jnp.sum(modes_t[t, k] * surface, axis=0, keepdims=True) for k in range(mode_count)
            ]
            sums.append(jnp.zeros((SUB - mode_count, rows), F32))
            share = exact_dot(jnp.concatenate(sums, axis=0), hits_t[t])
            forces = forces + (pltpu.roll(share, body_total, 1) if q else share)
    wide_sub = iota((SUB, width), 0)
    gathered = jnp.zeros((SUB, LANES), F32)
    for q, total in enumerate(totals):
        gathered = jnp.where(lane == q, jnp.sum(total, axis=1, keepdims=True), gathered)
    gathered = jnp.sum(gathered, axis=0, keepdims=True)
    if width > LANES:
        gathered = jnp.concatenate([gathered, jnp.zeros((1, width - LANES), F32)], axis=1)
    message[0:SUB, :] = jnp.where(wide_sub == SUB - 2, gathered, forces)
    message[SUB:, :] = table[...]


def mix_level(mix, weighted, l):
    total = (mix[l, l] + 1.0) * weighted[l]
    for m, value in enumerate(weighted):
        if m != l:
            total = total + mix[l, m] * value
    return total


def mix_levels(mix, weighted, levels):
    return [mix_level(mix, weighted, l) for l in range(levels)]


def body_hits(bodies_t, block, count, width):
    ids = bodies_t[block : block + 1, :]
    ids = jnp.where(ids < count, ids, -1)
    wanted = lax.broadcasted_iota(jnp.int32, (width, ids.shape[1]), 0)
    return (jnp.broadcast_to(ids, wanted.shape) == wanted).astype(F32)


def dot_nt(a, b):
    return lax.dot_general(
        a, b, (((1,), (1,)), ((), ())), precision=lax.Precision.HIGHEST, preferred_element_type=F32
    )


def exact_dot(values, ones):
    high = values.astype(jnp.bfloat16).astype(F32)
    rest = values - high
    middle = rest.astype(jnp.bfloat16).astype(F32)
    parts = jnp.concatenate([high, middle, rest - middle, jnp.zeros_like(high)], axis=0)
    shares = jnp.dot(
        parts.astype(jnp.bfloat16), ones.astype(jnp.bfloat16), preferred_element_type=F32
    )
    return shares[0:SUB] + (shares[SUB : 2 * SUB] + shares[2 * SUB : 3 * SUB])


def last_kernel(
    body_total,
    message,
    phi,
    direction,
    part,
    modes_t,
    hits,
    potential,
    velocity_t,
    flux,
    phi_s,
    flux_s,
    velocity_s,
    out_sems,
):
    levels, rows, cols = phi.shape
    blocks, mode_count = modes_t.shape[0:2]
    width = message.shape[1]
    owned = velocity_t.shape[0]
    main = pl.ds(2 * SUB, rows)
    top = message[0:SUB, :]

    def scalar(q):
        return top[SUB - 2 : SUB - 1, q : q + 1]

    cross_first, square_first, cross_mixed, square_mixed, square_second = [
        scalar(q) for q in range(5)
    ]
    first_step = cross_first / square_first
    next_top = (
        cross_first
        - first_step * cross_mixed
        - first_step * square_first
        + first_step * first_step * square_mixed
    )
    next_bottom = (
        square_first - 2.0 * first_step * square_mixed + first_step * first_step * square_second
    )
    second_step = next_top / next_bottom
    on_dir = first_step + second_step
    on_part = first_step * second_step
    outgoing = []

    def send(src, dst):
        copy = pltpu.make_async_copy(src, dst, out_sems.at[len(outgoing)])
        copy.start()
        outgoing.append(copy)


    for l in range(levels):
        for t in range(blocks):
            lanes = pl.ds(t * LANES, LANES)
            change = on_dir * direction[t, l, main, :] - on_part * part[t, l, main, :]
            phi_s[l, :, lanes] = phi[l, :, lanes] + change
        send(phi_s.at[l], potential.at[l])

    wide_sub, wide_lane = iota((SUB, width), 0), iota((SUB, width), 1)
    foot_scale = 1.0 / math.sqrt(FOOT)
    forces = foot_scale * (on_part * pltpu.roll(top, body_total, 1) - on_dir * top)
    forces = jnp.where(wide_sub == mode_count, 1.0, forces)
    forces = jnp.where(wide_lane < body_total, forces, 0.0)
    velocity = jnp.zeros((SUB, width), F32)
    for k in range(mode_count):
        table = message[(k // 2 + 1) * SUB : (k // 2 + 2) * SUB, :]
        if k % 2:
            table = pltpu.roll(table, body_total, 1)
        value = jnp.sum(table * forces, axis=0, keepdims=True)
        velocity = jnp.where(wide_sub == k, value, velocity)
    per_row = [exact_dot(velocity, hits[t]) for t in range(blocks)]

    me = (lax.axis_index("gx") * lax.axis_size("gy") + lax.axis_index("gy")) * owned
    mine = ((wide_lane == me + wide_sub) & (wide_sub < owned)).astype(F32)
    velocity_s[...] = dot_nt(mine, velocity)[0:owned, 0:mode_count]
    send(velocity_s, velocity_t)
    for t in range(blocks):
        total = modes_t[t, 0] * per_row[t][0:1, :]
        for k in range(1, mode_count):
            total = total + modes_t[t, k] * per_row[t][k : k + 1, :]
        flux_s[:, t * LANES : (t + 1) * LANES] = total.T
    send(flux_s, flux)
    for copy in outgoing:
        copy.wait()


def swap_near(value, axis):
    size = lax.axis_size(axis)
    return lax.ppermute(value, axis, [(i, i ^ 1) for i in range(size)])


def swap_far(value, axis):
    size = lax.axis_size(axis)
    pairs = [(i, i + 1) for i in range(1, size - 1, 2)]
    return lax.ppermute(value, axis, pairs + [(j, i) for i, j in pairs])


def sum_over(value, axis, together):
    size = lax.axis_size(axis)
    step = 1
    while step < size:
        count = min(together, size // step)
        total = value
        for n in range(1, count):
            pairs = [(i, i ^ (n * step)) for i in range(size)]
            total = total + lax.ppermute(value, axis, pairs)
        value = total
        step *= count
    return value


def per_device(
    forcing,
    start_potential,
    horiz_coef,
    vert_coef,
    vert_mix,
    mode_shapes,
    block_body,
    response,
    velocity_old,
):
    levels, rows, cols = forcing.shape
    mode_count = mode_shapes.shape[0]
    blocks = cols // LANES
    tiles = blocks + 1
    padded = rows + 4 * SUB
    owned = velocity_old.shape[1]
    body_total = owned * lax.axis_size(("gx", "gy"))
    width = 2 * body_total
    bodies_t = block_body.T
    response_t = jnp.swapaxes(response, 1, 2)
    old_t = velocity_old.T
    limit = pltpu.CompilerParams(vmem_limit_bytes=24 * 2**20)

    def call(kernel, name, outs, ins, args, scratch=()):
        return pl.pallas_call(
            kernel,
            out_shape=tuple(jax.ShapeDtypeStruct(shape, F32) for shape, _ in outs),
            in_specs=ins,
            out_specs=tuple(spec for _, spec in outs),
            scratch_shapes=list(scratch),
            compiler_params=limit,
            name=name,
        )(*args)

    strip = (levels + 1, SUB, cols)
    inner = (blocks, levels, rows, LANES)
    near, far = call(
        strip_kernel,
        "strip_kernel",
        [(strip, VMEM), (strip, VMEM)],
        [HBM] * 4,
        [
            pltpu.with_memory_space_constraint(value, pltpu.HBM)
            for value in (start_potential, forcing, horiz_coef, vert_coef)
        ],
        [
            pltpu.VMEM((2, blocks, levels, 3 * SUB, LANES), F32),
            pltpu.VMEM((2, blocks, levels, SUB, LANES), F32),
            pltpu.VMEM((2, SUB, cols), F32),
            pltpu.VMEM((2, SUB, cols), F32),
            pltpu.SemaphoreType.DMA((4 + 4 * blocks,)),
        ],
    )
    row_near, row_far = swap_near(near, "gx"), swap_far(far, "gx")
    packed_shape = (rows + 2 * SUB, LANES)
    res, packed, table = call(
        functools.partial(inner_kernel, body_total),
        "inner_kernel",
        [(inner, VMEM), (packed_shape, VMEM), ((3 * SUB, width), VMEM)],
        [VMEM] * 6,
        (start_potential, forcing, horiz_coef, vert_coef, response_t, old_t),
        [
            pltpu.VMEM((blocks, levels, rows + 2 * SUB, LANES), F32),
            pltpu.VMEM((LANES, LANES), F32),
        ],
    )
    strip = (rows // 2 + SUB, LANES)
    edge, edge_coef, own, near, far = call(
        edge_kernel,
        "edge_kernel",
        [
            ((4, blocks, levels, SUB, LANES), VMEM),
            ((2, 2, blocks, SUB, LANES), VMEM),
            (packed_shape, VMEM),
            (strip, VMEM),
            (strip, VMEM),
        ],
        [VMEM] * 7,
        (res, start_potential, horiz_coef, vert_coef, row_near, row_far, packed),
    )
    col_near, col_far = swap_near(near, "gy"), swap_far(far, "gy")
    field = (tiles, levels, padded, LANES)
    early_field = (blocks, levels, padded, LANES)
    plane = (blocks, padded, LANES)
    modes_t, hits, hits_t, early, res_own, horiz, vert, scale = call(
        functools.partial(ahead_kernel, body_total),
        "ahead_kernel",
        [((blocks, mode_count, LANES, rows), VMEM), ((blocks, width, rows), VMEM), ((blocks, rows, width), VMEM)]
        + [(early_field, VMEM)] * 2
        + [(plane, VMEM)] * 3,
        [VMEM] * 5 + [SMEM] + [VMEM] * 2,
        (res, edge, horiz_coef, vert_coef, edge_coef, vert_mix, mode_shapes, bodies_t),
    )

    side_plane = pltpu.VMEM((padded, LANES), F32)
    direction, part, message = call(
        functools.partial(main_kernel, body_total),
        "main_kernel",
        [(field, VMEM), (field, VMEM), ((4 * SUB, width), VMEM)],
        [VMEM] * 9 + [SMEM] + [VMEM] * 2,
        (
            early,
            res_own,
            horiz,
            vert,
            scale,
            own,
            col_near,
            col_far,
            table,
            vert_mix,
            modes_t,
            hits_t,
        ),
        [
            pltpu.VMEM((blocks, levels, padded, LANES), F32),
            pltpu.VMEM(field, F32),
            side_plane,
            side_plane,
            side_plane,
            pltpu.VMEM(packed_shape, F32),
        ],
    )
    message = sum_over(sum_over(message, "gx", 2), "gy", 4)

    potential, velocity_t, flux = call(
        functools.partial(last_kernel, body_total),
        "last_kernel",
        [((levels, rows, cols), HBM), ((owned, mode_count), HBM), ((rows, cols), HBM)],
        [VMEM] * 6,
        (message, start_potential, direction, part, modes_t, hits),
        [
            pltpu.VMEM((levels, rows, cols), F32),
            pltpu.VMEM((rows, cols), F32),
            pltpu.VMEM((owned, mode_count), F32),
            pltpu.SemaphoreType.DMA((levels + 2,)),
        ],
    )
    return (potential, velocity_t.T, flux)


def solution(mesh):
    return jax.shard_map(
        per_device,
        mesh=mesh,
        in_specs=(
            P(None, "gx", "gy"),
            P(None, "gx", "gy"),
            P("gx", "gy"),
            P("gx", "gy"),
            P(),
            P(None, "gx", "gy"),
            P("gx", "gy"),
            P(None, None, ("gx", "gy")),
            P(None, ("gx", "gy")),
        ),
        out_specs=(P(None, "gx", "gy"), P(None, ("gx", "gy")), P("gx", "gy")),
        check_vma=False,
    )
```
